32 devices in a mesh: dp: 4 (over z), sq: 8 (over y, x, core).
Axes of the slice: x: 2, y: 2, z: 4, core: 2. Of those that a mesh axis runs over, the one named last changes fastest.
Arguments:
- frames: bfloat16 [4, 1024, 1024], P('dp', 'sq'), may hold values from -6 to 6
- norm1_gain: float32 [1024], replicated, may hold values from 0.5 to 1.5
- w_qkv: bfloat16 [1024, 3072], replicated, may hold values from -0.1875 to 0.1875
- w_out: bfloat16 [1024, 1024], replicated, may hold values from -0.75 to 0.75
- norm2_gain: float32 [1024], replicated, may hold values from 0.5 to 1.5
- w_up: bfloat16 [1024, 4096], replicated, may hold values from -0.1875 to 0.1875
- w_down: bfloat16 [4096, 1024], replicated, may hold values from -0.09375 to 0.09375
- lengths: int32 [4, 8], P('dp'), may hold values from 1 to 896, as said below
- cotangent: bfloat16 [4, 1024, 1024], P('dp', 'sq'), may hold values from -6 to 6
Outputs:
- out: bfloat16 [4, 1024, 1024], P('dp', 'sq')
- d_in: float32 [4, 1024, 1024], P('dp', 'sq')
- g_norm1: float32 [1024], P('sq')
- g_qkv: float32 [1024, 3072], P('sq')
- g_out: float32 [1024, 1024], P('sq')
- g_norm2: float32 [1024], P('sq')
- g_up: float32 [1024, 4096], P('sq')
- g_down: float32 [4096, 1024], P('sq')
The draws below stay inside these ranges and needn't reach their ends.
Inputs may be any that keep to these rules, and one draw needn't show every extreme that they name: Each row's lengths sum to 1024. In each row exactly one item has 896 frames and is neither the first nor the last item of the row; the other items share the remaining 128 frames.
All inputs are finite; a program needn't handle non-finite values.
Results may differ from the reference program's by a relative error of at most 0.025.
Values may be sent and summed in bfloat16 or wider, within the bound.
A program may use at most 256 MiB of HBM per device.

```python
import jax
import jax.numpy as jnp
from jax import lax

D = 1024
HEADS = 16
HEAD_DIM = 64
FF = 4096
FR_DEV = 128
ITEMS = 8
ROW = 1024
ROWS = 4


def draw_lengths(key, part):
    key = jax.random.fold_in(key, 11)
    row_keys = jax.random.split(key, ROWS)

    def one_row(row_key):
        cut_key, place_key = jax.random.split(row_key)
        cuts = jnp.sort(jax.random.permutation(cut_key, FR_DEV - 1)[:ITEMS - 2] + 1).astype(jnp.int32)
        edges = jnp.concatenate([jnp.zeros((1,), jnp.int32), cuts, jnp.full((1,), FR_DEV, jnp.int32)])
        shorts = edges[1:] - edges[:-1]
        spot = jax.random.randint(place_key, (), 1, ITEMS - 1)
        index = jnp.arange(ITEMS, dtype=jnp.int32)
        before = shorts[jnp.clip(index, 0, ITEMS - 2)]
        after = shorts[jnp.clip(index - 1, 0, ITEMS - 2)]
        longest = jnp.full((ITEMS,), ROW - FR_DEV, jnp.int32)
        return jnp.where(index < spot, before, jnp.where(index == spot, longest, after)).astype(jnp.int32)
    return jax.vmap(one_row)(row_keys)


def shard_levels(key, dims, cuts, low, largest):
    factor_of, own = 1.0, jax.random.fold_in(key, 6)
    for axis_at, parts in cuts:
        steps = jnp.exp(jax.random.uniform(jax.random.fold_in(own, axis_at), (parts,), jnp.float32, low / len(cuts), largest / len(cuts)))
        factor_of = factor_of * jnp.repeat(steps, dims[axis_at] // parts).reshape([-1 if axis == axis_at else 1 for axis in range(len(dims))])
    return factor_of


def bell_draw(stream_key, extent, deviation, limit, cuts=(), kind=jnp.bfloat16):
    entries = jax.random.normal(stream_key, extent, jnp.float32) * deviation
    if len(cuts) > 0:
        entries = shard_levels(stream_key, extent, cuts, -0.22, 0.18) * entries
    return jnp.clip(entries, min=-limit, max=limit).astype(kind)


def setup_inputs(seed: int = 0) -> dict:
    key_list = jax.random.split(jax.random.key(seed), 10)
    return {
        "frames": bell_draw(key_list[0], (ROWS, ROW, D), 1.0, 6.0, ((0, 4), (1, 8))),
        "norm1_gain": jnp.clip(1.0 + 0.1 * jax.random.normal(key_list[1], (D,), jnp.float32), 0.5, 1.5),
        "w_qkv": bell_draw(key_list[2], (D, 3 * D), D ** -0.5, 0.1875),
        "w_out": bell_draw(key_list[3], (D, D), (max(1, D * 64 // ROW)) ** -0.5, 0.75),
        "norm2_gain": jnp.clip(1.0 + 0.1 * jax.random.normal(key_list[4], (D,), jnp.float32), 0.5, 1.5),
        "w_up": bell_draw(key_list[5], (D, FF), D ** -0.5, 0.1875),
        "w_down": bell_draw(key_list[6], (FF, D), FF ** -0.5, 0.09375),
        "lengths": draw_lengths(jax.random.fold_in(key_list[9], 71), 0),
        "cotangent": bell_draw(key_list[8], (ROWS, ROW, D), 1.0, 6.0, ((0, 4), (1, 8))),
    }


@jax.custom_vjp
def low(v):
    return lax.optimization_barrier(v.astype(jnp.bfloat16)).astype(jnp.float32)

@jax.custom_vjp
def low_back(v):
    return v

def low_keep(v):
    return (low(v), None)

def low_pass(kept, grad):
    return (grad,)

def back_keep(v):
    return (v, None)

def back_low(kept, grad):
    return (low(grad),)
low.defvjp(low_keep, low_pass)
low_back.defvjp(back_keep, back_low)

def norm_scaled(values, gain):
    return values * lax.rsqrt(lax.optimization_barrier(jnp.mean(values * values, axis=-1, keepdims=True)) + 1e-05) * gain

def attend(queries, keys, values, segment):
    positions = jnp.arange(ROW, dtype=jnp.int32)
    size = 512 if ROW % 512 == 0 else ROW
    number = ROW // size
    factor = HEAD_DIM ** (-0.5)
    highest = lax.Precision.HIGHEST

    def one_block(item):
        block_queries, block_pos, block_seg = item
        scores = jnp.einsum('qhd,khd->hqk', block_queries, keys, precision=highest) * factor
        scores = low_back(scores)
        mask = (positions[None, :] <= block_pos[:, None]) & (segment[None, :] == block_seg[:, None])
        scores = jnp.where(mask[None], scores, -1000000000.0)
        row_max = lax.optimization_barrier(jnp.max(scores, axis=-1, keepdims=True))
        weights = jnp.exp(scores - row_max)
        shares = low(weights / lax.optimization_barrier(jnp.sum(weights, axis=-1, keepdims=True)))
        return jnp.einsum('hqk,khd->qhd', shares, values, precision=highest)
    result = lax.map(jax.checkpoint(one_block), (queries.reshape(number, size, HEADS, HEAD_DIM), positions.reshape(number, size), segment.reshape(number, size)))
    return result.reshape(ROW, HEADS * HEAD_DIM)

def forward(frames_row, gain_one, w_qkv, w_out, gain_two, w_up, w_down, segment):
    highest = lax.Precision.HIGHEST
    width = HEADS * HEAD_DIM
    hidden = low(norm_scaled(frames_row, gain_one))
    mixed = low(low_back(jnp.dot(hidden, w_qkv, precision=highest, preferred_element_type=jnp.float32)))
    queries = mixed[:, :width].reshape(ROW, HEADS, HEAD_DIM)
    keys = mixed[:, width:2 * width].reshape(ROW, HEADS, HEAD_DIM)
    values = mixed[:, 2 * width:].reshape(ROW, HEADS, HEAD_DIM)
    attended = low(low_back(attend(queries, keys, values, segment)))
    branch = low_back(jnp.dot(attended, w_out, precision=highest, preferred_element_type=jnp.float32))
    middle = frames_row + branch
    second = low(norm_scaled(middle, gain_two))
    upward = low_back(jnp.dot(second, w_up, precision=highest, preferred_element_type=jnp.float32))
    active = low(jax.nn.gelu(upward))
    return middle + low_back(jnp.dot(active, w_down, precision=highest, preferred_element_type=jnp.float32))

def reference(frames, norm1_gain, w_qkv, w_out, norm2_gain, w_up, w_down, lengths, cotangent):
    params = (norm1_gain.astype(jnp.float32), w_qkv.astype(jnp.float32), w_out.astype(jnp.float32), norm2_gain.astype(jnp.float32), w_up.astype(jnp.float32), w_down.astype(jnp.float32))
    positions = jnp.arange(ROW, dtype=jnp.int32)

    def row_step(totals, item):
        frames_row, lengths_row, cot_row = item
        item_ends = jnp.cumsum(lengths_row).astype(jnp.int32)
        segment = lax.optimization_barrier(jnp.sum((positions[:, None] >= item_ends[None, :]).astype(jnp.int32), axis=1))

        def apply_layer(frames_in, *weights):
            return forward(frames_in, *weights, segment)
        output, pull = jax.vjp(apply_layer, frames_row.astype(jnp.float32), *params)
        grads = pull(cot_row.astype(jnp.float32))
        totals = tuple((total + grad for total, grad in zip(totals, grads[1:])))
        return (totals, (output.astype(jnp.bfloat16), grads[0]))
    start_totals = tuple((jnp.zeros(member.shape, jnp.float32) for member in params))
    totals, (outputs, input_grads) = lax.scan(row_step, start_totals, (frames, lengths, cotangent))
    return (outputs, input_grads, totals[0], totals[1], totals[2], totals[3], totals[4], totals[5])
```

```python
import jax
import jax.numpy as jnp
from jax import lax
from jax.sharding import PartitionSpec as P

HEADS = 16
HEAD_DIM = 64


EPSILON = 1e-05
NEG_FILL = -1000000000.0
START_MAX = -1e30


def norm_scaled(values, gain):
    return values * lax.rsqrt(jnp.mean(values * values, axis=-1, keepdims=True) + EPSILON) * gain


def segment_ids(positions, item_ends):
    return jnp.sum((positions[None, :, None] >= item_ends[:, None, :]).astype(jnp.int32), axis=2)


def running_ends(lengths):
    items = jnp.arange(lengths.shape[1], dtype=jnp.int32)
    before = items[None, None, :] <= items[None, :, None]
    return jnp.sum(jnp.where(before, lengths[:, None, :], 0), axis=2)


def visible(query_pos, query_seg, key_pos, key_seg):
    return (key_pos[None, None, :] <= query_pos[None, :, None]) & (
        key_seg[:, None, :] == query_seg[:, :, None]
    )


def block_size(count, limit):
    for candidate in range(min(count, limit), 0, -1):
        if count % candidate == 0:
            return candidate
    return count


def over_blocks(carry, arrays, start, step_fn, limit):
    count = arrays[0].shape[1]
    size = block_size(count, limit)
    number = count // size
    if number == 1:
        return step_fn(carry, arrays, start)
    stacked = tuple(
        (
            jnp.swapaxes(member.reshape((member.shape[0], number, size) + member.shape[2:]), 0, 1)
            for member in arrays
        )
    )

    def turn(state, item):
        offset, pieces = item
        return (step_fn(state, pieces, start + offset * size), None)

    offsets = jnp.arange(number, dtype=jnp.int32)
    return lax.scan(turn, carry, (offsets, stacked))[0]


def contract_rows(left, right):
    return lax.dot_general(
        left, right, (((0,), (0,)), ((), ())), preferred_element_type=jnp.float32
    )


def times_transpose(left, right):
    return lax.dot_general(
        left, right, (((1,), (1,)), ((), ())), preferred_element_type=jnp.float32
    )


def heads_flat(values, batch, rows, width):
    return values.transpose(0, 2, 1, 3).reshape(batch * rows, width)


def shards_by_rows(frames, norm1_gain, w_qkv, w_out, norm2_gain, w_up, w_down, lengths, cotangent):
    batch = frames.shape[0]
    rows = frames.shape[1]
    width = frames.shape[2]
    factor = HEAD_DIM ** (-0.5)
    first = lax.axis_index("sq") * rows
    query_pos = first + jnp.arange(rows, dtype=jnp.int32)
    item_ends = running_ends(lengths)
    query_seg = segment_ids(query_pos, item_ends)
    frames_own = frames.reshape(batch * rows, width).astype(jnp.float32)
    hidden1, norm1_pull = jax.vjp(norm_scaled, frames_own, norm1_gain)
    hidden1_low = hidden1.astype(jnp.bfloat16)
    mixed = jnp.dot(hidden1_low, w_qkv, preferred_element_type=jnp.float32).astype(jnp.bfloat16)
    query_rows = mixed[:, :width].reshape(batch, rows, width)
    key_rows = mixed[:, width : 2 * width].reshape(batch, rows, width)
    value_rows = mixed[:, 2 * width :].reshape(batch, rows, width)
    queries = query_rows.reshape(batch, rows, HEADS, HEAD_DIM)
    keys_own = key_rows.reshape(batch, rows, HEADS, HEAD_DIM)
    values_own = value_rows.reshape(batch, rows, HEADS, HEAD_DIM)

    def forward_step(carry, pieces, start):
        key_piece, value_piece = pieces
        count = key_piece.shape[1]
        key_pos = start + jnp.arange(count, dtype=jnp.int32)
        key_seg = segment_ids(key_pos, item_ends)

        def forward_work(state):
            running_max, running_sum, accum = state
            keys_block = key_piece.reshape(batch, count, HEADS, HEAD_DIM)
            values_block = value_piece.reshape(batch, count, HEADS, HEAD_DIM)
            scores = (
                jnp.einsum(
                    "rqhd,rkhd->rhqk", queries, keys_block, preferred_element_type=jnp.float32
                )
                * factor
            )
            mask = visible(query_pos, query_seg, key_pos, key_seg)[:, None]
            scores = jnp.where(mask, scores, NEG_FILL)
            new_max = jnp.maximum(running_max, jnp.max(scores, axis=-1))
            weights = jnp.where(mask, jnp.exp(scores - new_max[..., None]), 0.0)
            decay = jnp.exp(running_max - new_max)
            new_sum = decay * running_sum + jnp.sum(weights, axis=-1)
            update = jnp.einsum(
                "rhqk,rkhd->rhqd",
                weights.astype(jnp.bfloat16),
                values_block,
                preferred_element_type=jnp.float32,
            )
            return (new_max, new_sum, decay[..., None] * accum + update)

        return lax.cond(start <= query_pos[-1], forward_work, lambda state: state, carry)

    start_state = (
        jnp.full((batch, HEADS, rows), START_MAX, jnp.float32),
        jnp.zeros((batch, HEADS, rows), jnp.float32),
        jnp.zeros((batch, HEADS, rows, HEAD_DIM), jnp.float32),
    )
    final_max, final_sum, accum = over_blocks(
        start_state,
        (
            lax.all_gather(key_rows, "sq", axis=1, tiled=True),
            lax.all_gather(value_rows, "sq", axis=1, tiled=True),
        ),
        jnp.int32(0),
        forward_step,
        512,
    )
    attended = heads_flat(accum / final_sum[..., None], batch, rows, width)
    log_total = final_max + jnp.log(final_sum)
    attended_low = attended.astype(jnp.bfloat16)
    middle = frames_own + jnp.dot(attended_low, w_out, preferred_element_type=jnp.float32)
    hidden2, norm2_pull = jax.vjp(norm_scaled, middle, norm2_gain)
    hidden2_low = hidden2.astype(jnp.bfloat16)
    upward = jnp.dot(hidden2_low, w_up, preferred_element_type=jnp.float32)
    active, gelu_pull = jax.vjp(jax.nn.gelu, upward)
    active_low = active.astype(jnp.bfloat16)
    result = middle + jnp.dot(active_low, w_down, preferred_element_type=jnp.float32)
    grad_top = cotangent.reshape(batch * rows, width).astype(jnp.float32)
    grad_branch = grad_top.astype(jnp.bfloat16)
    grad_down = contract_rows(active_low, grad_branch)
    grad_active = times_transpose(grad_branch, w_down)
    grad_upward = gelu_pull(grad_active)[0].astype(jnp.bfloat16)
    grad_up = contract_rows(hidden2_low, grad_upward)
    grad_hidden2 = times_transpose(grad_upward, w_up)
    grad_middle_part, grad_gain2 = norm2_pull(grad_hidden2)
    grad_middle = grad_top + grad_middle_part
    grad_attn = grad_middle.astype(jnp.bfloat16)
    grad_outproj = contract_rows(attended_low, grad_attn)
    grad_attended = times_transpose(grad_attn, w_out).astype(jnp.bfloat16)
    grad_rows_own = grad_attended.reshape(batch, rows, width)
    grad_heads = grad_attended.reshape(batch, rows, HEADS, HEAD_DIM)
    delta_rows = jnp.sum(
        (grad_attended.astype(jnp.float32) * attended).reshape(batch, rows, HEADS, HEAD_DIM), axis=3
    )
    delta = delta_rows.transpose(0, 2, 1)

    def query_step(carry, pieces, start):
        key_piece, value_piece = pieces
        count = key_piece.shape[1]
        key_pos = start + jnp.arange(count, dtype=jnp.int32)
        key_seg = segment_ids(key_pos, item_ends)

        def query_work(grad_query):
            keys_block = key_piece.reshape(batch, count, HEADS, HEAD_DIM)
            values_block = value_piece.reshape(batch, count, HEADS, HEAD_DIM)
            scores = (
                jnp.einsum(
                    "rqhd,rkhd->rhqk", queries, keys_block, preferred_element_type=jnp.float32
                )
                * factor
            )
            mask = visible(query_pos, query_seg, key_pos, key_seg)[:, None]
            shares = jnp.where(mask, jnp.exp(scores - log_total[..., None]), 0.0)
            grad_shares = jnp.einsum(
                "rqhd,rkhd->rhqk", grad_heads, values_block, preferred_element_type=jnp.float32
            )
            grad_scores = (shares * (grad_shares - delta[..., None])).astype(jnp.bfloat16)
            return grad_query + jnp.einsum(
                "rhqk,rkhd->rhqd", grad_scores, keys_block, preferred_element_type=jnp.float32
            )

        return lax.cond(start <= query_pos[-1], query_work, lambda state: state, carry)

    zero_query = jnp.zeros((batch, HEADS, rows, HEAD_DIM), jnp.float32)
    grad_query = over_blocks(
        zero_query,
        (
            lax.all_gather(key_rows, "sq", axis=1, tiled=True),
            lax.all_gather(value_rows, "sq", axis=1, tiled=True),
        ),
        jnp.int32(0),
        query_step,
        512,
    )

    def key_step(carry, pieces, start):
        query_piece, grad_piece, total_piece, delta_piece = pieces
        count = query_piece.shape[1]
        remote_pos = start + jnp.arange(count, dtype=jnp.int32)
        remote_seg = segment_ids(remote_pos, item_ends)

        def key_work(state):
            grad_key, grad_value = state
            remote_queries = query_piece.reshape(batch, count, HEADS, HEAD_DIM)
            remote_grads = grad_piece.reshape(batch, count, HEADS, HEAD_DIM)
            scores = (
                jnp.einsum(
                    "rqhd,rkhd->rhqk", remote_queries, keys_own, preferred_element_type=jnp.float32
                )
                * factor
            )
            mask = visible(remote_pos, remote_seg, query_pos, query_seg)[:, None]
            shares = jnp.where(
                mask, jnp.exp(scores - total_piece.transpose(0, 2, 1)[..., None]), 0.0
            )
            grad_value = grad_value + jnp.einsum(
                "rhqk,rqhd->rhkd",
                shares.astype(jnp.bfloat16),
                remote_grads,
                preferred_element_type=jnp.float32,
            )
            grad_shares = jnp.einsum(
                "rqhd,rkhd->rhqk", remote_grads, values_own, preferred_element_type=jnp.float32
            )
            grad_scores = (
                shares * (grad_shares - delta_piece.transpose(0, 2, 1)[..., None])
            ).astype(jnp.bfloat16)
            grad_key = grad_key + jnp.einsum(
                "rhqk,rqhd->rhkd", grad_scores, remote_queries, preferred_element_type=jnp.float32
            )
            return (grad_key, grad_value)

        return lax.cond(start + count - 1 >= first, key_work, lambda state: state, carry)

    grad_key, grad_value = over_blocks(
        (zero_query, zero_query),
        (
            lax.all_gather(query_rows, "sq", axis=1, tiled=True),
            lax.all_gather(grad_rows_own, "sq", axis=1, tiled=True),
            lax.all_gather(
                log_total.transpose(0, 2, 1).astype(jnp.bfloat16), "sq", axis=1, tiled=True
            ).astype(jnp.float32),
            lax.all_gather(delta_rows.astype(jnp.bfloat16), "sq", axis=1, tiled=True).astype(
                jnp.float32
            ),
        ),
        jnp.int32(0),
        key_step,
        512,
    )
    grad_mixed = jnp.concatenate(
        [
            heads_flat(grad_query * factor, batch, rows, width),
            heads_flat(grad_key * factor, batch, rows, width),
            heads_flat(grad_value, batch, rows, width),
        ],
        axis=1,
    ).astype(jnp.bfloat16)
    grad_qkv = contract_rows(hidden1_low, grad_mixed)
    grad_hidden1 = times_transpose(grad_mixed, w_qkv)
    grad_frames_part, grad_gain1 = norm1_pull(grad_hidden1)
    grad_frames = (grad_middle + grad_frames_part).reshape(batch, rows, width)
    result_rows = result.astype(jnp.bfloat16).reshape(batch, rows, width)
    shares_sq = (
        lax.psum_scatter(grad_gain1, "sq", scatter_dimension=0, tiled=True),
        lax.psum_scatter(grad_qkv, "sq", scatter_dimension=0, tiled=True),
        lax.psum_scatter(grad_outproj, "sq", scatter_dimension=0, tiled=True),
        lax.psum_scatter(grad_gain2, "sq", scatter_dimension=0, tiled=True),
        lax.psum_scatter(grad_up, "sq", scatter_dimension=0, tiled=True),
        lax.psum_scatter(grad_down, "sq", scatter_dimension=0, tiled=True),
    )
    totals = (
        lax.psum(shares_sq[0].astype(jnp.bfloat16), "dp").astype(jnp.float32),
        lax.psum(shares_sq[1].astype(jnp.bfloat16), "dp").astype(jnp.float32),
        lax.psum(shares_sq[2].astype(jnp.bfloat16), "dp").astype(jnp.float32),
        lax.psum(shares_sq[3].astype(jnp.bfloat16), "dp").astype(jnp.float32),
        lax.psum(shares_sq[4].astype(jnp.bfloat16), "dp").astype(jnp.float32),
        lax.psum(shares_sq[5].astype(jnp.bfloat16), "dp").astype(jnp.float32),
    )
    return (
        result_rows,
        grad_frames,
        totals[0],
        totals[1],
        totals[2],
        totals[3],
        totals[4],
        totals[5],
    )


def low(values):
    return values.astype(jnp.bfloat16)


def times(left, right):
    return jnp.dot(left, right, preferred_element_type=jnp.float32)


def norm_scale(values):
    return lax.rsqrt(jnp.mean(values * values, axis=-1, keepdims=True) + EPSILON)


def norm_back(values, scale, gain, grad):
    scaled = gain * grad
    inner = jnp.mean(scaled * values, axis=-1, keepdims=True)
    part = scale * scaled - values * (scale * scale * scale) * inner
    return part, jnp.sum(grad * values * scale, axis=0)


def gelu_parts(values):
    root = 0.7978845608028654
    inner = jnp.tanh(root * (values + 0.044715 * values * values * values))
    slope = 0.5 * (1.0 + inner) + 0.5 * values * (1.0 - inner * inner) * root * (
        1.0 + 3 * 0.044715 * values * values
    )
    return 0.5 * values * (1.0 + inner), slope


def to_heads(rows_value):
    return lax.all_to_all(rows_value, "sq", split_axis=1, concat_axis=0, tiled=True)


def to_rows(heads_value):
    return lax.all_to_all(heads_value, "sq", split_axis=0, concat_axis=1, tiled=True)


def shards_by_heads(frames, norm1_gain, w_qkv, w_out, norm2_gain, w_up, w_down, lengths, cotangent):
    _, rows, width = frames.shape
    ff = w_up.shape[1]
    count = lax.axis_size("sq")
    me = lax.axis_index("sq")
    total = rows * count
    part = width // count
    local = part // HEAD_DIM
    factor = HEAD_DIM ** (-0.5)

    frames_own = frames[0].astype(jnp.float32)
    frames_all = lax.all_gather(frames[0], "sq", axis=0, tiled=True).astype(jnp.float32)
    grad_low = cotangent[0]
    grad_all = lax.all_gather(grad_low, "sq", axis=0, tiled=True)
    hidden1 = low(frames_all * norm_scale(frames_all) * norm1_gain)
    w_heads = jnp.concatenate(
        [lax.dynamic_slice_in_dim(w_qkv, k * width + me * part, part, 1) for k in range(3)], axis=1
    )
    mixed = low(times(hidden1, w_heads))
    queries, keys, values = (
        mixed[:, k * part : (k + 1) * part].reshape(total, local, HEAD_DIM) for k in range(3)
    )
    ends = running_ends(lengths)[0]
    place = jnp.arange(total, dtype=jnp.int32)
    begin = jnp.max(jnp.where(ends[None, :] <= place[:, None], ends[None, :], 0), axis=1)
    mask = (place[None, :] <= place[:, None]) & (place[None, :] >= begin[:, None])
    scores = jnp.einsum("qhd,khd->hqk", queries, keys, preferred_element_type=jnp.float32) * factor
    scores = jnp.where(mask[None], scores, NEG_FILL)
    top = jnp.max(scores, axis=-1, keepdims=True)
    weights = jnp.exp(scores - top)
    shares = weights / jnp.sum(weights, axis=-1, keepdims=True)
    shares_low = low(shares)
    attended = jnp.einsum("hqk,khd->qhd", shares_low, values, preferred_element_type=jnp.float32)
    attended_low = low(attended.reshape(total, part))
    attended_rows = to_rows(attended_low)
    middle = frames_own + times(attended_rows, w_out)
    scale2 = norm_scale(middle)
    hidden2 = low(middle * scale2 * norm2_gain)
    hidden2_all = lax.all_gather(hidden2, "sq", axis=0, tiled=True)

    active, slope = gelu_parts(times(hidden2, w_up))
    result = low(middle + times(low(active), w_down))[None]
    grad_up_own = low(times_transpose(grad_low, w_down) * slope)
    grad_hidden2 = times_transpose(grad_up_own, w_up)
    back2, gain2_part = norm_back(middle, scale2, norm2_gain, grad_hidden2)
    grad_middle = grad_low.astype(jnp.float32) + back2
    grad_attn = low(grad_middle)
    grad_attn_all = lax.all_gather(grad_attn, "sq", axis=0, tiled=True)
    grad_heads = to_heads(low(times_transpose(grad_attn, w_out)))

    grads = grad_heads.reshape(total, local, HEAD_DIM)
    grad_value = jnp.einsum("hqk,qhd->khd", shares_low, grads, preferred_element_type=jnp.float32)
    grad_shares = jnp.einsum("qhd,khd->hqk", grads, values, preferred_element_type=jnp.float32)
    delta = jnp.sum(grads.astype(jnp.float32) * attended, axis=2).T[:, :, None]
    grad_scores = low(shares * (grad_shares - delta))
    grad_query = jnp.einsum("hqk,khd->qhd", grad_scores, keys, preferred_element_type=jnp.float32)
    grad_key = jnp.einsum("hqk,qhd->khd", grad_scores, queries, preferred_element_type=jnp.float32)
    grad_mixed = [
        low(member.reshape(total, part))
        for member in (grad_query * factor, grad_key * factor, grad_value)
    ]
    grad_mixed_rows = jnp.concatenate([to_rows(member) for member in grad_mixed], axis=1)
    grad_hidden1 = times_transpose(grad_mixed_rows, w_qkv)
    back1, gain1_part = norm_back(frames_own, norm_scale(frames_own), norm1_gain, grad_hidden1)
    grad_frames = (grad_middle + back1)[None]

    slice_up = lax.dynamic_slice_in_dim(w_up, me * (ff // count), ff // count, 1)
    slice_down = lax.dynamic_slice_in_dim(w_down, me * (ff // count), ff // count, 0)
    active_part, slope_part = gelu_parts(times(hidden2_all, slice_up))
    grad_down = low(contract_rows(low(active_part), grad_all))
    grad_up_part = low(times_transpose(grad_all, slice_down) * slope_part)
    grad_up = to_rows(low(contract_rows(hidden2_all, grad_up_part)))
    grad_out = low(contract_rows(attended_low, grad_attn_all))
    grad_qkv = jnp.concatenate(
        [to_rows(low(contract_rows(hidden1, member))) for member in grad_mixed], axis=1
    )
    gains = lax.psum_scatter(jnp.stack([gain1_part, gain2_part]), "sq", scatter_dimension=1, tiled=True)
    gains = lax.psum(gains, "dp")
    sums = lax.psum((grad_qkv, grad_out, grad_up, grad_down), "dp")
    grad_qkv, grad_out, grad_up, grad_down = (member.astype(jnp.float32) for member in sums)
    return (result, grad_frames, gains[0], grad_qkv, grad_out, gains[1], grad_up, grad_down)


def solution(mesh):
    by_heads = HEADS % mesh.shape["sq"] == 0
    return jax.shard_map(
        shards_by_heads if by_heads else shards_by_rows,
        mesh=mesh,
        in_specs=(
            P("dp", "sq", None),
            P(),
            P(),
            P(),
            P(),
            P(),
            P(),
            P("dp", None),
            P("dp", "sq", None),
        ),
        out_specs=(
            P("dp", "sq", None),
            P("dp", "sq", None),
            P("sq"),
            P("sq", None),
            P("sq", None),
            P("sq"),
            P("sq", None),
            P("sq", None),
        ),
        check_vma=False,
    )
```

```python
import functools

import jax
import jax.numpy as jnp
from jax import lax
from jax.experimental import pallas as pl
from jax.experimental.pallas import tpu as pltpu
from jax.sharding import PartitionSpec as P

HEADS = 16
HEAD_DIM = 64


EPSILON = 1e-05
NEG_FILL = -1000000000.0
START_MAX = -1e30


def norm_scaled(values, gain):
    return values * lax.rsqrt(jnp.mean(values * values, axis=-1, keepdims=True) + EPSILON) * gain


def segment_ids(positions, item_ends):
    return jnp.sum((positions[None, :, None] >= item_ends[:, None, :]).astype(jnp.int32), axis=2)


def running_ends(lengths):
    items = jnp.arange(lengths.shape[1], dtype=jnp.int32)
    before = items[None, None, :] <= items[None, :, None]
    return jnp.sum(jnp.where(before, lengths[:, None, :], 0), axis=2)


def visible(query_pos, query_seg, key_pos, key_seg):
    return (key_pos[None, None, :] <= query_pos[None, :, None]) & (
        key_seg[:, None, :] == query_seg[:, :, None]
    )


def block_size(count, limit):
    for candidate in range(min(count, limit), 0, -1):
        if count % candidate == 0:
            return candidate
    return count


def over_blocks(carry, arrays, start, step_fn, limit):
    count = arrays[0].shape[1]
    size = block_size(count, limit)
    number = count // size
    if number == 1:
        return step_fn(carry, arrays, start)
    stacked = tuple(
        (
            jnp.swapaxes(member.reshape((member.shape[0], number, size) + member.shape[2:]), 0, 1)
            for member in arrays
        )
    )

    def turn(state, item):
        offset, pieces = item
        return (step_fn(state, pieces, start + offset * size), None)

    offsets = jnp.arange(number, dtype=jnp.int32)
    return lax.scan(turn, carry, (offsets, stacked))[0]


def contract_rows(left, right):
    return lax.dot_general(
        left, right, (((0,), (0,)), ((), ())), preferred_element_type=jnp.float32
    )


def times_transpose(left, right):
    return lax.dot_general(
        left, right, (((1,), (1,)), ((), ())), preferred_element_type=jnp.float32
    )


def heads_flat(values, batch, rows, width):
    return values.transpose(0, 2, 1, 3).reshape(batch * rows, width)


def shards_by_rows(frames, norm1_gain, w_qkv, w_out, norm2_gain, w_up, w_down, lengths, cotangent):
    batch = frames.shape[0]
    rows = frames.shape[1]
    width = frames.shape[2]
    factor = HEAD_DIM ** (-0.5)
    first = lax.axis_index("sq") * rows
    query_pos = first + jnp.arange(rows, dtype=jnp.int32)
    item_ends = running_ends(lengths)
    query_seg = segment_ids(query_pos, item_ends)
    frames_own = frames.reshape(batch * rows, width).astype(jnp.float32)
    hidden1, norm1_pull = jax.vjp(norm_scaled, frames_own, norm1_gain)
    hidden1_low = hidden1.astype(jnp.bfloat16)
    mixed = jnp.dot(hidden1_low, w_qkv, preferred_element_type=jnp.float32).astype(jnp.bfloat16)
    query_rows = mixed[:, :width].reshape(batch, rows, width)
    key_rows = mixed[:, width : 2 * width].reshape(batch, rows, width)
    value_rows = mixed[:, 2 * width :].reshape(batch, rows, width)
    queries = query_rows.reshape(batch, rows, HEADS, HEAD_DIM)
    keys_own = key_rows.reshape(batch, rows, HEADS, HEAD_DIM)
    values_own = value_rows.reshape(batch, rows, HEADS, HEAD_DIM)

    def forward_step(carry, pieces, start):
        key_piece, value_piece = pieces
        count = key_piece.shape[1]
        key_pos = start + jnp.arange(count, dtype=jnp.int32)
        key_seg = segment_ids(key_pos, item_ends)

        def forward_work(state):
            running_max, running_sum, accum = state
            keys_block = key_piece.reshape(batch, count, HEADS, HEAD_DIM)
            values_block = value_piece.reshape(batch, count, HEADS, HEAD_DIM)
            scores = (
                jnp.einsum(
                    "rqhd,rkhd->rhqk", queries, keys_block, preferred_element_type=jnp.float32
                )
                * factor
            )
            mask = visible(query_pos, query_seg, key_pos, key_seg)[:, None]
            scores = jnp.where(mask, scores, NEG_FILL)
            new_max = jnp.maximum(running_max, jnp.max(scores, axis=-1))
            weights = jnp.where(mask, jnp.exp(scores - new_max[..., None]), 0.0)
            decay = jnp.exp(running_max - new_max)
            new_sum = decay * running_sum + jnp.sum(weights, axis=-1)
            update = jnp.einsum(
                "rhqk,rkhd->rhqd",
                weights.astype(jnp.bfloat16),
                values_block,
                preferred_element_type=jnp.float32,
            )
            return (new_max, new_sum, decay[..., None] * accum + update)

        return lax.cond(start <= query_pos[-1], forward_work, lambda state: state, carry)

    start_state = (
        jnp.full((batch, HEADS, rows), START_MAX, jnp.float32),
        jnp.zeros((batch, HEADS, rows), jnp.float32),
        jnp.zeros((batch, HEADS, rows, HEAD_DIM), jnp.float32),
    )
    final_max, final_sum, accum = over_blocks(
        start_state,
        (
            lax.all_gather(key_rows, "sq", axis=1, tiled=True),
            lax.all_gather(value_rows, "sq", axis=1, tiled=True),
        ),
        jnp.int32(0),
        forward_step,
        512,
    )
    attended = heads_flat(accum / final_sum[..., None], batch, rows, width)
    log_total = final_max + jnp.log(final_sum)
    attended_low = attended.astype(jnp.bfloat16)
    middle = frames_own + jnp.dot(attended_low, w_out, preferred_element_type=jnp.float32)
    hidden2, norm2_pull = jax.vjp(norm_scaled, middle, norm2_gain)
    hidden2_low = hidden2.astype(jnp.bfloat16)
    upward = jnp.dot(hidden2_low, w_up, preferred_element_type=jnp.float32)
    active, gelu_pull = jax.vjp(jax.nn.gelu, upward)
    active_low = active.astype(jnp.bfloat16)
    result = middle + jnp.dot(active_low, w_down, preferred_element_type=jnp.float32)
    grad_top = cotangent.reshape(batch * rows, width).astype(jnp.float32)
    grad_branch = grad_top.astype(jnp.bfloat16)
    grad_down = contract_rows(active_low, grad_branch)
    grad_active = times_transpose(grad_branch, w_down)
    grad_upward = gelu_pull(grad_active)[0].astype(jnp.bfloat16)
    grad_up = contract_rows(hidden2_low, grad_upward)
    grad_hidden2 = times_transpose(grad_upward, w_up)
    grad_middle_part, grad_gain2 = norm2_pull(grad_hidden2)
    grad_middle = grad_top + grad_middle_part
    grad_attn = grad_middle.astype(jnp.bfloat16)
    grad_outproj = contract_rows(attended_low, grad_attn)
    grad_attended = times_transpose(grad_attn, w_out).astype(jnp.bfloat16)
    grad_rows_own = grad_attended.reshape(batch, rows, width)
    grad_heads = grad_attended.reshape(batch, rows, HEADS, HEAD_DIM)
    delta_rows = jnp.sum(
        (grad_attended.astype(jnp.float32) * attended).reshape(batch, rows, HEADS, HEAD_DIM), axis=3
    )
    delta = delta_rows.transpose(0, 2, 1)

    def query_step(carry, pieces, start):
        key_piece, value_piece = pieces
        count = key_piece.shape[1]
        key_pos = start + jnp.arange(count, dtype=jnp.int32)
        key_seg = segment_ids(key_pos, item_ends)

        def query_work(grad_query):
            keys_block = key_piece.reshape(batch, count, HEADS, HEAD_DIM)
            values_block = value_piece.reshape(batch, count, HEADS, HEAD_DIM)
            scores = (
                jnp.einsum(
                    "rqhd,rkhd->rhqk", queries, keys_block, preferred_element_type=jnp.float32
                )
                * factor
            )
            mask = visible(query_pos, query_seg, key_pos, key_seg)[:, None]
            shares = jnp.where(mask, jnp.exp(scores - log_total[..., None]), 0.0)
            grad_shares = jnp.einsum(
                "rqhd,rkhd->rhqk", grad_heads, values_block, preferred_element_type=jnp.float32
            )
            grad_scores = (shares * (grad_shares - delta[..., None])).astype(jnp.bfloat16)
            return grad_query + jnp.einsum(
                "rhqk,rkhd->rhqd", grad_scores, keys_block, preferred_element_type=jnp.float32
            )

        return lax.cond(start <= query_pos[-1], query_work, lambda state: state, carry)

    zero_query = jnp.zeros((batch, HEADS, rows, HEAD_DIM), jnp.float32)
    grad_query = over_blocks(
        zero_query,
        (
            lax.all_gather(key_rows, "sq", axis=1, tiled=True),
            lax.all_gather(value_rows, "sq", axis=1, tiled=True),
        ),
        jnp.int32(0),
        query_step,
        512,
    )

    def key_step(carry, pieces, start):
        query_piece, grad_piece, total_piece, delta_piece = pieces
        count = query_piece.shape[1]
        remote_pos = start + jnp.arange(count, dtype=jnp.int32)
        remote_seg = segment_ids(remote_pos, item_ends)

        def key_work(state):
            grad_key, grad_value = state
            remote_queries = query_piece.reshape(batch, count, HEADS, HEAD_DIM)
            remote_grads = grad_piece.reshape(batch, count, HEADS, HEAD_DIM)
            scores = (
                jnp.einsum(
                    "rqhd,rkhd->rhqk", remote_queries, keys_own, preferred_element_type=jnp.float32
                )
                * factor
            )
            mask = visible(remote_pos, remote_seg, query_pos, query_seg)[:, None]
            shares = jnp.where(
                mask, jnp.exp(scores - total_piece.transpose(0, 2, 1)[..., None]), 0.0
            )
            grad_value = grad_value + jnp.einsum(
                "rhqk,rqhd->rhkd",
                shares.astype(jnp.bfloat16),
                remote_grads,
                preferred_element_type=jnp.float32,
            )
            grad_shares = jnp.einsum(
                "rqhd,rkhd->rhqk", remote_grads, values_own, preferred_element_type=jnp.float32
            )
            grad_scores = (
                shares * (grad_shares - delta_piece.transpose(0, 2, 1)[..., None])
            ).astype(jnp.bfloat16)
            grad_key = grad_key + jnp.einsum(
                "rhqk,rqhd->rhkd", grad_scores, remote_queries, preferred_element_type=jnp.float32
            )
            return (grad_key, grad_value)

        return lax.cond(start + count - 1 >= first, key_work, lambda state: state, carry)

    grad_key, grad_value = over_blocks(
        (zero_query, zero_query),
        (
            lax.all_gather(query_rows, "sq", axis=1, tiled=True),
            lax.all_gather(grad_rows_own, "sq", axis=1, tiled=True),
            lax.all_gather(
                log_total.transpose(0, 2, 1).astype(jnp.bfloat16), "sq", axis=1, tiled=True
            ).astype(jnp.float32),
            lax.all_gather(delta_rows.astype(jnp.bfloat16), "sq", axis=1, tiled=True).astype(
                jnp.float32
            ),
        ),
        jnp.int32(0),
        key_step,
        512,
    )
    grad_mixed = jnp.concatenate(
        [
            heads_flat(grad_query * factor, batch, rows, width),
            heads_flat(grad_key * factor, batch, rows, width),
            heads_flat(grad_value, batch, rows, width),
        ],
        axis=1,
    ).astype(jnp.bfloat16)
    grad_qkv = contract_rows(hidden1_low, grad_mixed)
    grad_hidden1 = times_transpose(grad_mixed, w_qkv)
    grad_frames_part, grad_gain1 = norm1_pull(grad_hidden1)
    grad_frames = (grad_middle + grad_frames_part).reshape(batch, rows, width)
    result_rows = result.astype(jnp.bfloat16).reshape(batch, rows, width)
    shares_sq = (
        lax.psum_scatter(grad_gain1, "sq", scatter_dimension=0, tiled=True),
        lax.psum_scatter(grad_qkv, "sq", scatter_dimension=0, tiled=True),
        lax.psum_scatter(grad_outproj, "sq", scatter_dimension=0, tiled=True),
        lax.psum_scatter(grad_gain2, "sq", scatter_dimension=0, tiled=True),
        lax.psum_scatter(grad_up, "sq", scatter_dimension=0, tiled=True),
        lax.psum_scatter(grad_down, "sq", scatter_dimension=0, tiled=True),
    )
    totals = (
        lax.psum(shares_sq[0].astype(jnp.bfloat16), "dp").astype(jnp.float32),
        lax.psum(shares_sq[1].astype(jnp.bfloat16), "dp").astype(jnp.float32),
        lax.psum(shares_sq[2].astype(jnp.bfloat16), "dp").astype(jnp.float32),
        lax.psum(shares_sq[3].astype(jnp.bfloat16), "dp").astype(jnp.float32),
        lax.psum(shares_sq[4].astype(jnp.bfloat16), "dp").astype(jnp.float32),
        lax.psum(shares_sq[5].astype(jnp.bfloat16), "dp").astype(jnp.float32),
    )
    return (
        result_rows,
        grad_frames,
        totals[0],
        totals[1],
        totals[2],
        totals[3],
        totals[4],
        totals[5],
    )


def low(values):
    return values.astype(jnp.bfloat16)


def times(left, right):
    return jnp.dot(left, right, preferred_element_type=jnp.float32)


def norm_scale(values):
    return lax.rsqrt(jnp.mean(values * values, axis=-1, keepdims=True) + EPSILON)


def norm_back(values, scale, gain, grad):
    scaled = gain * grad
    inner = jnp.mean(scaled * values, axis=-1, keepdims=True)
    part = scale * scaled - values * (scale * scale * scale) * inner
    return part, jnp.sum(grad * values * scale, axis=0)


def gelu_parts(values):
    root = 0.7978845608028654
    inner = jnp.tanh(root * (values + 0.044715 * values * values * values))
    slope = 0.5 * (1.0 + inner) + 0.5 * values * (1.0 - inner * inner) * root * (
        1.0 + 3 * 0.044715 * values * values
    )
    return 0.5 * values * (1.0 + inner), slope


def to_heads(rows_value):
    return lax.all_to_all(rows_value, "sq", split_axis=1, concat_axis=0, tiled=True)


def to_rows(heads_value):
    return lax.all_to_all(heads_value, "sq", split_axis=0, concat_axis=1, tiled=True)


MESH = pl.DeviceIdType.MESH
bf16, f32 = jnp.bfloat16, jnp.float32

def chain_kernel(chunk, lag, g_ref, t_ref, dummy, x_ref, send, send2, rsem, xsem, tsem):
    dp = lax.axis_index("dp"); sq = lax.axis_index("sq")
    n = g_ref.shape[0] // chunk
    inner = (dp == 1) | (dp == 2)
    outer = (dp == 0) | (dp == 3)
    mate = 3 - dp
    edge = jnp.where(dp == 1, 0, 3)
    core = jnp.where(dp == 0, 1, 2)
    bar = pltpu.get_barrier_semaphore()
    def rows(c): return pl.ds(pl.multiple_of(c * chunk, chunk), chunk)
    def raw(c):
        return pltpu.make_async_remote_copy(g_ref.at[rows(c)], t_ref.at[rows(c)], send.at[c], rsem.at[c], device_id=(core, sq), device_id_type=MESH)
    def cross(c):
        return pltpu.make_async_remote_copy(g_ref.at[rows(c)], x_ref.at[rows(c)], send.at[c], xsem.at[c], device_id=(mate, sq), device_id_type=MESH)
    def back(c):
        return pltpu.make_async_remote_copy(t_ref.at[rows(c)], t_ref.at[rows(c)], send2.at[c], tsem.at[c], device_id=(edge, sq), device_id_type=MESH)
    @pl.when(outer)
    def _():
        pl.semaphore_signal(bar, inc=1, device_id=(core, sq), device_id_type=MESH)
        pl.semaphore_wait(bar, 1)
        @pl.loop(0, n)
        def _(c): raw(c).start()
        @pl.loop(0, n)
        def _(c):
            back(c).wait_recv()
            raw(c).wait_send()
    @pl.when(inner)
    def _():
        pl.semaphore_signal(bar, inc=1, device_id=(edge, sq), device_id_type=MESH)
        pl.semaphore_signal(bar, inc=1, device_id=(mate, sq), device_id_type=MESH)
        pl.semaphore_wait(bar, 2)
        def A(c):
            raw(c).wait_recv()
            g_ref[rows(c), :] = (g_ref[rows(c), :].astype(f32) + t_ref[rows(c), :].astype(f32)).astype(bf16)
            cross(c).start()
        def B(c):
            cross(c).wait_recv()
            t_ref[rows(c), :] = (g_ref[rows(c), :].astype(f32) + x_ref[rows(c), :].astype(f32)).astype(bf16)
            back(c).start()
        for c in range(lag): A(c)
        @pl.loop(lag, n)
        def _(c):
            A(c)
            B(c - lag)
        @pl.loop(n - lag, n)
        def _(c): B(c)
        @pl.loop(0, n)
        def _(c):
            cross(c).wait_send()
            back(c).wait_send()

def chain(g, chunk=64, lag=2):
    n = g.shape[0] // chunk
    V = pltpu.VMEM
    t, _ = pl.pallas_call(functools.partial(chain_kernel, chunk, lag),
        out_shape=(jax.ShapeDtypeStruct(g.shape, bf16),jax.ShapeDtypeStruct((8,128), f32)),
        in_specs=[pl.BlockSpec(memory_space=pltpu.VMEM)],
        out_specs=(pl.BlockSpec(memory_space=pltpu.VMEM),pl.BlockSpec(memory_space=pl.ANY)),
        scratch_shapes=[V(g.shape, bf16)] + [pltpu.SemaphoreType.DMA((n,))] * 5,
        compiler_params=pltpu.CompilerParams(has_side_effects=True, collective_id=1, vmem_limit_bytes=60*2**20))(g)
    return t


def low_blocks(grad):
    rows, columns = grad.shape
    return grad.reshape(rows, columns // 1024, 1024).swapaxes(0, 1).reshape(-1, 1024)


def from_blocks(blocks, number):
    rows = blocks.shape[0] // number
    return blocks.reshape(number, rows, 1024).swapaxes(0, 1).reshape(rows, -1)


def shards_by_heads(frames, norm1_gain, w_qkv, w_out, norm2_gain, w_up, w_down, lengths, cotangent):
    _, rows, width = frames.shape
    ff = w_up.shape[1]
    count = lax.axis_size("sq")
    me = lax.axis_index("sq")
    total = rows * count
    part = width // count
    local = part // HEAD_DIM
    factor = HEAD_DIM ** (-0.5)

    frames_own = frames[0].astype(jnp.float32)
    frames_all = lax.all_gather(frames[0], "sq", axis=0, tiled=True).astype(jnp.float32)
    grad_low = cotangent[0]
    grad_all = lax.all_gather(grad_low, "sq", axis=0, tiled=True)
    hidden1 = low(frames_all * norm_scale(frames_all) * norm1_gain)
    w_heads = jnp.concatenate(
        [lax.dynamic_slice_in_dim(w_qkv, k * width + me * part, part, 1) for k in range(3)], axis=1
    )
    mixed = low(times(hidden1, w_heads))
    queries, keys, values = (
        mixed[:, k * part : (k + 1) * part].reshape(total, local, HEAD_DIM) for k in range(3)
    )
    ends = running_ends(lengths)[0]
    place = jnp.arange(total, dtype=jnp.int32)
    begin = jnp.max(jnp.where(ends[None, :] <= place[:, None], ends[None, :], 0), axis=1)
    mask = (place[None, :] <= place[:, None]) & (place[None, :] >= begin[:, None])
    scores = jnp.einsum("qhd,khd->hqk", queries, keys, preferred_element_type=jnp.float32) * factor
    scores = jnp.where(mask[None], scores, NEG_FILL)
    top = jnp.max(scores, axis=-1, keepdims=True)
    weights = jnp.exp(scores - top)
    shares = weights / jnp.sum(weights, axis=-1, keepdims=True)
    shares_low = low(shares)
    attended = jnp.einsum("hqk,khd->qhd", shares_low, values, preferred_element_type=jnp.float32)
    attended_low = low(attended.reshape(total, part))
    attended_rows = to_rows(attended_low)
    middle = frames_own + times(attended_rows, w_out)
    scale2 = norm_scale(middle)
    hidden2 = low(middle * scale2 * norm2_gain)
    hidden2_all = lax.all_gather(hidden2, "sq", axis=0, tiled=True)

    active, slope = gelu_parts(times(hidden2, w_up))
    result = low(middle + times(low(active), w_down))[None]
    grad_up_own = low(times_transpose(grad_low, w_down) * slope)
    grad_hidden2 = times_transpose(grad_up_own, w_up)
    back2, gain2_part = norm_back(middle, scale2, norm2_gain, grad_hidden2)
    grad_middle = grad_low.astype(jnp.float32) + back2
    grad_attn = low(grad_middle)
    grad_attn_all = lax.all_gather(grad_attn, "sq", axis=0, tiled=True)
    grad_heads = to_heads(low(times_transpose(grad_attn, w_out)))

    grads = grad_heads.reshape(total, local, HEAD_DIM)
    grad_value = jnp.einsum("hqk,qhd->khd", shares_low, grads, preferred_element_type=jnp.float32)
    grad_shares = jnp.einsum("qhd,khd->hqk", grads, values, preferred_element_type=jnp.float32)
    delta = jnp.sum(grads.astype(jnp.float32) * attended, axis=2).T[:, :, None]
    grad_scores = low(shares * (grad_shares - delta))
    grad_query = jnp.einsum("hqk,khd->qhd", grad_scores, keys, preferred_element_type=jnp.float32)
    grad_key = jnp.einsum("hqk,qhd->khd", grad_scores, queries, preferred_element_type=jnp.float32)
    grad_mixed = [
        low(member.reshape(total, part))
        for member in (grad_query * factor, grad_key * factor, grad_value)
    ]
    grad_mixed_rows = jnp.concatenate([to_rows(member) for member in grad_mixed], axis=1)
    grad_hidden1 = times_transpose(grad_mixed_rows, w_qkv)
    back1, gain1_part = norm_back(frames_own, norm_scale(frames_own), norm1_gain, grad_hidden1)
    grad_frames = (grad_middle + back1)[None]

    slice_up = lax.dynamic_slice_in_dim(w_up, me * (ff // count), ff // count, 1)
    slice_down = lax.dynamic_slice_in_dim(w_down, me * (ff // count), ff // count, 0)
    active_part, slope_part = gelu_parts(times(hidden2_all, slice_up))
    grad_down = low(contract_rows(low(active_part), grad_all))
    grad_up_part = low(times_transpose(grad_all, slice_down) * slope_part)
    grad_up = to_rows(low(contract_rows(hidden2_all, grad_up_part)))
    grad_out = low(contract_rows(attended_low, grad_attn_all))
    grad_qkv = jnp.concatenate(
        [to_rows(low(contract_rows(hidden1, member))) for member in grad_mixed], axis=1
    )
    gains = lax.psum_scatter(jnp.stack([gain1_part, gain2_part]), "sq", scatter_dimension=1, tiled=True)
    gains = lax.psum(gains, "dp")
    pieces = (grad_down, low_blocks(grad_up), grad_out, low_blocks(grad_qkv))
    sums = chain(jnp.concatenate(pieces, axis=0), 32, 2)
    starts = [0]
    for piece in pieces:
        starts.append(starts[-1] + piece.shape[0])
    grad_down, grad_up, grad_out, grad_qkv = (
        from_blocks(sums[starts[k] : starts[k + 1]], where).astype(jnp.float32)
        for k, where in enumerate((1, ff // width, 1, 3))
    )
    return (result, grad_frames, gains[0], grad_qkv, grad_out, gains[1], grad_up, grad_down)


def solution(mesh):
    by_heads = HEADS % mesh.shape["sq"] == 0
    return jax.shard_map(
        shards_by_heads if by_heads else shards_by_rows,
        mesh=mesh,
        in_specs=(
            P("dp", "sq", None),
            P(),
            P(),
            P(),
            P(),
            P(),
            P(),
            P("dp", None),
            P("dp", "sq", None),
        ),
        out_specs=(
            P("dp", "sq", None),
            P("dp", "sq", None),
            P("sq"),
            P("sq", None),
            P("sq", None),
            P("sq"),
            P("sq", None),
            P("sq", None),
        ),
        check_vma=False,
    )
```

```python
import functools

import jax
import jax.numpy as jnp
from jax import lax
from jax.experimental import pallas as pl
from jax.experimental.pallas import tpu as pltpu
from jax.sharding import PartitionSpec as P

HEADS = 16
HEAD_DIM = 64


EPSILON = 1e-05
NEG_FILL = -1000000000.0
START_MAX = -1e30


def norm_scaled(values, gain):
    return values * lax.rsqrt(jnp.mean(values * values, axis=-1, keepdims=True) + EPSILON) * gain


def segment_ids(positions, item_ends):
    return jnp.sum((positions[None, :, None] >= item_ends[:, None, :]).astype(jnp.int32), axis=2)


def running_ends(lengths):
    items = jnp.arange(lengths.shape[1], dtype=jnp.int32)
    before = items[None, None, :] <= items[None, :, None]
    return jnp.sum(jnp.where(before, lengths[:, None, :], 0), axis=2)


def visible(query_pos, query_seg, key_pos, key_seg):
    return (key_pos[None, None, :] <= query_pos[None, :, None]) & (
        key_seg[:, None, :] == query_seg[:, :, None]
    )


def block_size(count, limit):
    for candidate in range(min(count, limit), 0, -1):
        if count % candidate == 0:
            return candidate
    return count


def over_blocks(carry, arrays, start, step_fn, limit):
    count = arrays[0].shape[1]
    size = block_size(count, limit)
    number = count // size
    if number == 1:
        return step_fn(carry, arrays, start)
    stacked = tuple(
        (
            jnp.swapaxes(member.reshape((member.shape[0], number, size) + member.shape[2:]), 0, 1)
            for member in arrays
        )
    )

    def turn(state, item):
        offset, pieces = item
        return (step_fn(state, pieces, start + offset * size), None)

    offsets = jnp.arange(number, dtype=jnp.int32)
    return lax.scan(turn, carry, (offsets, stacked))[0]


def contract_rows(left, right):
    return lax.dot_general(
        left, right, (((0,), (0,)), ((), ())), preferred_element_type=jnp.float32
    )


def times_transpose(left, right):
    return lax.dot_general(
        left, right, (((1,), (1,)), ((), ())), preferred_element_type=jnp.float32
    )


def heads_flat(values, batch, rows, width):
    return values.transpose(0, 2, 1, 3).reshape(batch * rows, width)


def shards_by_rows(frames, norm1_gain, w_qkv, w_out, norm2_gain, w_up, w_down, lengths, cotangent):
    batch = frames.shape[0]
    rows = frames.shape[1]
    width = frames.shape[2]
    factor = HEAD_DIM ** (-0.5)
    first = lax.axis_index("sq") * rows
    query_pos = first + jnp.arange(rows, dtype=jnp.int32)
    item_ends = running_ends(lengths)
    query_seg = segment_ids(query_pos, item_ends)
    frames_own = frames.reshape(batch * rows, width).astype(jnp.float32)
    hidden1, norm1_pull = jax.vjp(norm_scaled, frames_own, norm1_gain)
    hidden1_low = hidden1.astype(jnp.bfloat16)
    mixed = jnp.dot(hidden1_low, w_qkv, preferred_element_type=jnp.float32).astype(jnp.bfloat16)
    query_rows = mixed[:, :width].reshape(batch, rows, width)
    key_rows = mixed[:, width : 2 * width].reshape(batch, rows, width)
    value_rows = mixed[:, 2 * width :].reshape(batch, rows, width)
    queries = query_rows.reshape(batch, rows, HEADS, HEAD_DIM)
    keys_own = key_rows.reshape(batch, rows, HEADS, HEAD_DIM)
    values_own = value_rows.reshape(batch, rows, HEADS, HEAD_DIM)

    def forward_step(carry, pieces, start):
        key_piece, value_piece = pieces
        count = key_piece.shape[1]
        key_pos = start + jnp.arange(count, dtype=jnp.int32)
        key_seg = segment_ids(key_pos, item_ends)

        def forward_work(state):
            running_max, running_sum, accum = state
            keys_block = key_piece.reshape(batch, count, HEADS, HEAD_DIM)
            values_block = value_piece.reshape(batch, count, HEADS, HEAD_DIM)
            scores = (
                jnp.einsum(
                    "rqhd,rkhd->rhqk", queries, keys_block, preferred_element_type=jnp.float32
                )
                * factor
            )
            mask = visible(query_pos, query_seg, key_pos, key_seg)[:, None]
            scores = jnp.where(mask, scores, NEG_FILL)
            new_max = jnp.maximum(running_max, jnp.max(scores, axis=-1))
            weights = jnp.where(mask, jnp.exp(scores - new_max[..., None]), 0.0)
            decay = jnp.exp(running_max - new_max)
            new_sum = decay * running_sum + jnp.sum(weights, axis=-1)
            update = jnp.einsum(
                "rhqk,rkhd->rhqd",
                weights.astype(jnp.bfloat16),
                values_block,
                preferred_element_type=jnp.float32,
            )
            return (new_max, new_sum, decay[..., None] * accum + update)

        return lax.cond(start <= query_pos[-1], forward_work, lambda state: state, carry)

    start_state = (
        jnp.full((batch, HEADS, rows), START_MAX, jnp.float32),
        jnp.zeros((batch, HEADS, rows), jnp.float32),
        jnp.zeros((batch, HEADS, rows, HEAD_DIM), jnp.float32),
    )
    final_max, final_sum, accum = over_blocks(
        start_state,
        (
            lax.all_gather(key_rows, "sq", axis=1, tiled=True),
            lax.all_gather(value_rows, "sq", axis=1, tiled=True),
        ),
        jnp.int32(0),
        forward_step,
        512,
    )
    attended = heads_flat(accum / final_sum[..., None], batch, rows, width)
    log_total = final_max + jnp.log(final_sum)
    attended_low = attended.astype(jnp.bfloat16)
    middle = frames_own + jnp.dot(attended_low, w_out, preferred_element_type=jnp.float32)
    hidden2, norm2_pull = jax.vjp(norm_scaled, middle, norm2_gain)
    hidden2_low = hidden2.astype(jnp.bfloat16)
    upward = jnp.dot(hidden2_low, w_up, preferred_element_type=jnp.float32)
    active, gelu_pull = jax.vjp(jax.nn.gelu, upward)
    active_low = active.astype(jnp.bfloat16)
    result = middle + jnp.dot(active_low, w_down, preferred_element_type=jnp.float32)
    grad_top = cotangent.reshape(batch * rows, width).astype(jnp.float32)
    grad_branch = grad_top.astype(jnp.bfloat16)
    grad_down = contract_rows(active_low, grad_branch)
    grad_active = times_transpose(grad_branch, w_down)
    grad_upward = gelu_pull(grad_active)[0].astype(jnp.bfloat16)
    grad_up = contract_rows(hidden2_low, grad_upward)
    grad_hidden2 = times_transpose(grad_upward, w_up)
    grad_middle_part, grad_gain2 = norm2_pull(grad_hidden2)
    grad_middle = grad_top + grad_middle_part
    grad_attn = grad_middle.astype(jnp.bfloat16)
    grad_outproj = contract_rows(attended_low, grad_attn)
    grad_attended = times_transpose(grad_attn, w_out).astype(jnp.bfloat16)
    grad_rows_own = grad_attended.reshape(batch, rows, width)
    grad_heads = grad_attended.reshape(batch, rows, HEADS, HEAD_DIM)
    delta_rows = jnp.sum(
        (grad_attended.astype(jnp.float32) * attended).reshape(batch, rows, HEADS, HEAD_DIM), axis=3
    )
    delta = delta_rows.transpose(0, 2, 1)

    def query_step(carry, pieces, start):
        key_piece, value_piece = pieces
        count = key_piece.shape[1]
        key_pos = start + jnp.arange(count, dtype=jnp.int32)
        key_seg = segment_ids(key_pos, item_ends)

        def query_work(grad_query):
            keys_block = key_piece.reshape(batch, count, HEADS, HEAD_DIM)
            values_block = value_piece.reshape(batch, count, HEADS, HEAD_DIM)
            scores = (
                jnp.einsum(
                    "rqhd,rkhd->rhqk", queries, keys_block, preferred_element_type=jnp.float32
                )
                * factor
            )
            mask = visible(query_pos, query_seg, key_pos, key_seg)[:, None]
            shares = jnp.where(mask, jnp.exp(scores - log_total[..., None]), 0.0)
            grad_shares = jnp.einsum(
                "rqhd,rkhd->rhqk", grad_heads, values_block, preferred_element_type=jnp.float32
            )
            grad_scores = (shares * (grad_shares - delta[..., None])).astype(jnp.bfloat16)
            return grad_query + jnp.einsum(
                "rhqk,rkhd->rhqd", grad_scores, keys_block, preferred_element_type=jnp.float32
            )

        return lax.cond(start <= query_pos[-1], query_work, lambda state: state, carry)

    zero_query = jnp.zeros((batch, HEADS, rows, HEAD_DIM), jnp.float32)
    grad_query = over_blocks(
        zero_query,
        (
            lax.all_gather(key_rows, "sq", axis=1, tiled=True),
            lax.all_gather(value_rows, "sq", axis=1, tiled=True),
        ),
        jnp.int32(0),
        query_step,
        512,
    )

    def key_step(carry, pieces, start):
        query_piece, grad_piece, total_piece, delta_piece = pieces
        count = query_piece.shape[1]
        remote_pos = start + jnp.arange(count, dtype=jnp.int32)
        remote_seg = segment_ids(remote_pos, item_ends)

        def key_work(state):
            grad_key, grad_value = state
            remote_queries = query_piece.reshape(batch, count, HEADS, HEAD_DIM)
            remote_grads = grad_piece.reshape(batch, count, HEADS, HEAD_DIM)
            scores = (
                jnp.einsum(
                    "rqhd,rkhd->rhqk", remote_queries, keys_own, preferred_element_type=jnp.float32
                )
                * factor
            )
            mask = visible(remote_pos, remote_seg, query_pos, query_seg)[:, None]
            shares = jnp.where(
                mask, jnp.exp(scores - total_piece.transpose(0, 2, 1)[..., None]), 0.0
            )
            grad_value = grad_value + jnp.einsum(
                "rhqk,rqhd->rhkd",
                shares.astype(jnp.bfloat16),
                remote_grads,
                preferred_element_type=jnp.float32,
            )
            grad_shares = jnp.einsum(
                "rqhd,rkhd->rhqk", remote_grads, values_own, preferred_element_type=jnp.float32
            )
            grad_scores = (
                shares * (grad_shares - delta_piece.transpose(0, 2, 1)[..., None])
            ).astype(jnp.bfloat16)
            grad_key = grad_key + jnp.einsum(
                "rhqk,rqhd->rhkd", grad_scores, remote_queries, preferred_element_type=jnp.float32
            )
            return (grad_key, grad_value)

        return lax.cond(start + count - 1 >= first, key_work, lambda state: state, carry)

    grad_key, grad_value = over_blocks(
        (zero_query, zero_query),
        (
            lax.all_gather(query_rows, "sq", axis=1, tiled=True),
            lax.all_gather(grad_rows_own, "sq", axis=1, tiled=True),
            lax.all_gather(
                log_total.transpose(0, 2, 1).astype(jnp.bfloat16), "sq", axis=1, tiled=True
            ).astype(jnp.float32),
            lax.all_gather(delta_rows.astype(jnp.bfloat16), "sq", axis=1, tiled=True).astype(
                jnp.float32
            ),
        ),
        jnp.int32(0),
        key_step,
        512,
    )
    grad_mixed = jnp.concatenate(
        [
            heads_flat(grad_query * factor, batch, rows, width),
            heads_flat(grad_key * factor, batch, rows, width),
            heads_flat(grad_value, batch, rows, width),
        ],
        axis=1,
    ).astype(jnp.bfloat16)
    grad_qkv = contract_rows(hidden1_low, grad_mixed)
    grad_hidden1 = times_transpose(grad_mixed, w_qkv)
    grad_frames_part, grad_gain1 = norm1_pull(grad_hidden1)
    grad_frames = (grad_middle + grad_frames_part).reshape(batch, rows, width)
    result_rows = result.astype(jnp.bfloat16).reshape(batch, rows, width)
    shares_sq = (
        lax.psum_scatter(grad_gain1, "sq", scatter_dimension=0, tiled=True),
        lax.psum_scatter(grad_qkv, "sq", scatter_dimension=0, tiled=True),
        lax.psum_scatter(grad_outproj, "sq", scatter_dimension=0, tiled=True),
        lax.psum_scatter(grad_gain2, "sq", scatter_dimension=0, tiled=True),
        lax.psum_scatter(grad_up, "sq", scatter_dimension=0, tiled=True),
        lax.psum_scatter(grad_down, "sq", scatter_dimension=0, tiled=True),
    )
    totals = (
        lax.psum(shares_sq[0].astype(jnp.bfloat16), "dp").astype(jnp.float32),
        lax.psum(shares_sq[1].astype(jnp.bfloat16), "dp").astype(jnp.float32),
        lax.psum(shares_sq[2].astype(jnp.bfloat16), "dp").astype(jnp.float32),
        lax.psum(shares_sq[3].astype(jnp.bfloat16), "dp").astype(jnp.float32),
        lax.psum(shares_sq[4].astype(jnp.bfloat16), "dp").astype(jnp.float32),
        lax.psum(shares_sq[5].astype(jnp.bfloat16), "dp").astype(jnp.float32),
    )
    return (
        result_rows,
        grad_frames,
        totals[0],
        totals[1],
        totals[2],
        totals[3],
        totals[4],
        totals[5],
    )


MESH = pl.DeviceIdType.MESH
ZROWS = 32
ZLAG = 2
QBLOCK = 256


def dot(left, right):
    return jnp.dot(left, right, preferred_element_type=jnp.float32)


def dot_nt(left, right):
    return lax.dot_general(
        left, right, (((1,), (1,)), ((), ())), preferred_element_type=jnp.float32
    )


def dot_tn(left, right):
    return lax.dot_general(
        left, right, (((0,), (0,)), ((), ())), preferred_element_type=jnp.float32
    )


def low(values):
    return values.astype(jnp.bfloat16)


def wide(values):
    return values.astype(jnp.float32)


def span(start, size):
    return pl.ds(pl.multiple_of(start, size), size)


def norm_scale(values):
    return lax.rsqrt(jnp.mean(values * values, axis=-1, keepdims=True) + EPSILON)


def norm_back(values, scale, gain, grad):
    scaled = gain * grad
    inner = jnp.mean(scaled * values, axis=-1, keepdims=True)
    part = scale * scaled - values * (scale * scale * scale) * inner
    return part, jnp.sum(grad * values * scale, axis=0, keepdims=True)


def gelu_parts(values):
    root = 0.7978845608028654
    square = values * values
    inner = jnp.tanh(root * values * (1.0 + 0.044715 * square))
    half = 0.5 * (1.0 + inner)
    slope = half + 0.5 * root * values * (1.0 - inner * inner) * (1.0 + 0.134145 * square)
    return values * half, slope


def layer_kernel(
    count, planes,
    frames_in, gain1_ref, w_qkv_in, w_out_in, gain2_ref, w_up_in, w_down_in, lengths_ref, cot_in,
    result_ref, d_in_ref, gains_ref, sum_ref,
    frames_all, hidden1_all, cot_all, hidden2_all, attn_all,
    w_heads, w_out, w_up, w_down,
    mixed, q_pad, k_pad, v_pad, g_pad, shares, scores, o_turned, o_heads, o_rows,
    middle, acc_a, acc_b, grad_mid, g_rows, g_heads,
    active_s, slope_s, up_stage, mixed_grad, mixed_stage, mixed_rows, k_acc, v_acc,
    own, cross_in, gain_out, gain_in, gain_z,
    load_sem, ag_send, ag_recv, o_send, o_recv, g_send, g_recv, m_send, m_recv,
    u_send, u_recv, s_send, s_recv, n_send, n_recv, nz_send, nz_recv,
    z_send, zb_send, z_raw_recv, z_cross_recv, z_back_recv,
):
    bf16, f32 = jnp.bfloat16, jnp.float32
    rows, width = result_ref.shape
    total = rows * count
    part = width // count
    local = part // HEAD_DIM
    ff = w_up.shape[1]
    slab = ff // count
    half = rows // 2
    factor = HEAD_DIM ** (-0.5)
    me, plane = lax.axis_index("sq"), lax.axis_index("dp")

    def flip(index, bit):
        return index + bit - 2 * bit * lax.rem(lax.div(index, bit), 2)

    mate, over_x, over_y = flip(me, 1), flip(me, 2), flip(me, 4)
    corner = flip(over_x, 4)
    inner = (plane == 1) | (plane == 2)
    outer = (plane == 0) | (plane == 3)
    z_mate = planes - 1 - plane
    z_edge = jnp.where(plane == 1, 0, planes - 1)
    z_core = jnp.where(plane == 0, 1, planes - 2)

    def remote(source, target, send, recv, to, to_plane=None):
        return pltpu.make_async_remote_copy(
            src_ref=source, dst_ref=target, send_sem=send, recv_sem=recv,
            device_id=(plane if to_plane is None else to_plane, to), device_id_type=MESH,
        )

    def others(body):
        @pl.loop(1, count)
        def _(step):
            body(lax.rem(me + step, count))

    mine = span(me * rows, rows)
    loads = [
        pltpu.make_async_copy(frames_in.at[0], frames_all.at[mine], load_sem.at[0]),
        pltpu.make_async_copy(cot_in.at[0], cot_all.at[mine], load_sem.at[1]),
    ] + [
        pltpu.make_async_copy(
            w_qkv_in.at[:, span(k * width + me * part, part)],
            w_heads.at[:, pl.ds(k * part, part)],
            load_sem.at[2 + k],
        )
        for k in range(3)
    ] + [
        pltpu.make_async_copy(w_out_in, w_out, load_sem.at[5]),
        pltpu.make_async_copy(w_up_in, w_up, load_sem.at[6]),
        pltpu.make_async_copy(w_down_in, w_down, load_sem.at[7]),
    ]
    load_qkv = pltpu.make_async_copy(w_qkv_in, w_up.at[:, pl.ds(0, 3 * width)], load_sem.at[8])
    for load in loads[:5]:
        load.start()

    barrier = pltpu.get_barrier_semaphore()
    others(lambda s: pl.semaphore_signal(
        barrier, inc=1, device_id=(plane, s), device_id_type=MESH))

    @pl.loop(1, planes)
    def _(step):
        pl.semaphore_signal(
            barrier, inc=1, device_id=(lax.rem(plane + step, planes), me), device_id_type=MESH)

    pl.semaphore_wait(barrier, count - 1 + planes - 1)

    def slots(index):
        return [
            (me, None, mate, mate),
            (me, 0, over_x, over_x), (me, 1, over_x, over_x),
            (me, 1, over_y, over_y), (me, 0, over_y, over_y),
            (over_x, 0, over_y, corner), (over_y, 1, over_x, corner),
            (over_x, 0, mate, flip(mate, 2)), (over_x, 1, mate, flip(mate, 2)),
            (over_y, 1, mate, flip(mate, 4)), (over_y, 0, mate, flip(mate, 4)),
            (corner, 0, mate, flip(corner, 1)), (corner, 1, mate, flip(corner, 1)),
        ][index]

    def gather(number, array, source=None):
        def piece(block, which):
            if which is None:
                return span(block * rows, rows)
            return span(block * rows + which * half, half)

        def copy(slot, sent=True):
            block, which, target, arrives = slots(slot)
            there = piece(block if sent else arrives, which)
            here = array.at[there]
            if sent and source is not None and slot < 5:
                here = source if which is None else source.at[pl.ds(which * half, half)]
            return remote(
                here, array.at[there], ag_send.at[number, slot], ag_recv.at[number, slot], target)

        def start(*numbers):
            for slot in numbers:
                copy(slot).start()

        def wait(*numbers):
            for slot in numbers:
                copy(slot, sent=False).wait_recv()

        def finish():
            for slot in range(13):
                copy(slot).wait_send()

        return start, wait, finish

    f_start, f_wait, f_finish = gather(0, frames_all, frames_in.at[0])
    c_start, c_wait, c_finish = gather(1, cot_all, cot_in.at[0])
    h_start, h_wait, h_finish = gather(2, hidden2_all)
    a_start, a_wait, a_finish = gather(3, attn_all)

    def z_raw(c):
        at = span(c * ZROWS, ZROWS)
        return remote(own.at[at], sum_ref.at[at], z_send.at[c], z_raw_recv.at[c], me, z_core)

    def z_cross(c):
        at = span(c * ZROWS, ZROWS)
        return remote(own.at[at], cross_in.at[at], z_send.at[c], z_cross_recv.at[c], me, z_mate)

    def z_back(c):
        at = span(c * ZROWS, ZROWS)
        return remote(sum_ref.at[at], sum_ref.at[at], zb_send.at[c], z_back_recv.at[c], me, z_edge)

    def z_join(c):
        at = span(c * ZROWS, ZROWS)
        z_raw(c).wait_recv()
        own[at, :] = low(wide(own[at, :]) + wide(sum_ref[at, :]))
        z_cross(c).start()

    def z_close(c):
        at = span(c * ZROWS, ZROWS)
        z_cross(c).wait_recv()
        sum_ref[at, :] = low(wide(own[at, :]) + wide(cross_in[at, :]))
        z_back(c).start()

    chunks = own.shape[0] // ZROWS
    z_done = [0]

    def z_inner(number):
        first, last = z_done[0], z_done[0] + number
        z_done[0] = last

        @pl.when(inner)
        def _():
            split = min(max(first, ZLAG), last)
            for c in range(first, split):
                z_join(c)
            if last > split:
                @pl.loop(split, last)
                def _(c):
                    z_join(c)
                    z_close(c - ZLAG)

    def z_outer(first, last):
        @pl.when(outer)
        def _():
            @pl.loop(first, last)
            def _(c):
                z_raw(c).start()

    f_start(0, 1, 3, 2, 4)
    for load in loads[5:]:
        load.start()
    lane_head = lax.broadcasted_iota(jnp.int32, (rows, part), 1) // HEAD_DIM
    gain1 = gain1_ref[...]
    gain2 = gain2_ref[...]

    def qkv_block(block):
        at = span(block * rows, rows)
        values = wide(frames_all[at, :])
        hidden = low(values * norm_scale(values) * gain1)
        hidden1_all[at, :] = hidden
        projected = low(dot(hidden, w_heads[...]))
        mixed[at, :] = projected
        for head in range(local):
            on = lane_head == head
            q_pad[head, at, :] = low(jnp.where(on, wide(projected[:, :part]) * factor, 0.0))
            k_pad[head, at, :] = low(jnp.where(on, wide(projected[:, part : 2 * part]), 0.0))
            v_pad[head, at, :] = low(jnp.where(on, wide(projected[:, 2 * part :]), 0.0))

    loads[0].wait()
    for k in range(3):
        loads[2 + k].wait()
    qkv_block(me)
    f_wait(0)
    qkv_block(mate)
    f_wait(1)
    f_start(5, 7)
    f_wait(3)
    f_start(6, 9)
    c_start(0, 1, 3, 2, 4)
    f_wait(2)
    f_start(8)
    qkv_block(over_x)
    f_wait(4)
    f_start(10)
    qkv_block(over_y)
    f_wait(7, 8)
    qkv_block(flip(mate, 2))
    f_wait(9, 10)
    qkv_block(flip(mate, 4))
    f_wait(5)
    f_start(11)
    f_wait(6)
    f_start(12)
    qkv_block(corner)
    f_wait(11, 12)
    qkv_block(flip(corner, 1))

    ends, running = [], None
    for item in range(lengths_ref.shape[1]):
        length = lengths_ref[0, item]
        running = length if running is None else running + length
        ends.append(running)

    keys_at = pl.ds(part, part)
    values_at = pl.ds(2 * part, part)
    query_blocks = total // QBLOCK
    per_block = QBLOCK // rows

    def o_copy(target, source):
        return remote(
            o_heads.at[span(target * rows, rows)], o_rows.at[:, span(source * part, part)],
            o_send.at[target], o_recv.at[source], target)

    @pl.loop(0, query_blocks)
    def _(i):
        at = span(i * QBLOCK, QBLOCK)
        query_pos = i * QBLOCK + lax.broadcasted_iota(jnp.int32, (1, QBLOCK), 1)
        begin = jnp.zeros((1, QBLOCK), jnp.int32)
        for end in ends:
            begin = jnp.maximum(begin, jnp.where(query_pos >= end, end, 0))
        turned = jnp.zeros((part, QBLOCK), f32)
        for head in range(local):
            queries = q_pad[head, at, :]

            def score(j, top):
                keys = span(j * QBLOCK, QBLOCK)
                key_pos = j * QBLOCK + lax.broadcasted_iota(jnp.int32, (QBLOCK, 1), 0)
                value = dot_nt(mixed[keys, keys_at], queries)
                value = jnp.where((key_pos <= query_pos) & (key_pos >= begin), value, NEG_FILL)
                scores[keys, :] = value
                return jnp.maximum(top, jnp.max(value, axis=0, keepdims=True))

            top = lax.fori_loop(0, i + 1, score, jnp.full((1, QBLOCK), START_MAX, f32))

            def weigh(j, weight_sum):
                keys = span(j * QBLOCK, QBLOCK)
                weight = jnp.exp(scores[keys, :] - top)
                scores[keys, :] = weight
                return weight_sum + jnp.sum(weight, axis=0, keepdims=True)

            weight_sum = lax.fori_loop(0, i + 1, weigh, jnp.zeros((1, QBLOCK), f32))
            over = 1.0 / weight_sum

            def attend(j, accum):
                keys = span(j * QBLOCK, QBLOCK)
                share = low(scores[keys, :] * over)
                shares[head, keys, at] = share
                return accum + dot_tn(v_pad[head, keys, :], share)

            turned = lax.fori_loop(0, i + 1, attend, turned)
        o_turned[:, at] = turned
        o_heads[at, :] = low(turned.T)
        for k in range(per_block):
            target = i * per_block + k

            @pl.when(target != me)
            def _():
                o_copy(target, me).start()

            @pl.when(target == me)
            def _():
                o_rows[:, span(me * part, part)] = o_heads[mine, :]

    c_wait(1)
    c_start(5, 7)
    c_wait(3)
    c_start(6, 9)
    loads[5].wait()
    others(lambda s: o_copy(me, s).wait_recv())
    middle_own = wide(frames_all[mine, :]) + dot(o_rows[...], w_out[...])
    middle[...] = middle_own
    hidden2_own = low(middle_own * norm_scale(middle_own) * gain2)
    hidden2_all[mine, :] = hidden2_own
    h_start(0, 1, 3, 2, 4)

    loads[1].wait()
    loads[6].wait()
    loads[7].wait()
    acc_a[...] = middle_own
    acc_b[...] = jnp.zeros_like(acc_b)

    def ff_tile(t):
        at = span(t * slab, slab)
        active, slope = gelu_parts(dot(hidden2_all[mine, :], w_up[:, at]))
        acc_a[...] += dot(low(active), w_down[at, :])
        grad = low(dot_nt(cot_all[mine, :], w_down[at, :]) * slope)
        acc_b[...] += dot_nt(grad, w_up[:, at])

    pl.loop(0, count // 2)(ff_tile)
    h_wait(1)
    h_start(5, 7)
    h_wait(3)
    h_start(6, 9)
    pl.loop(count // 2, count)(ff_tile)
    result_ref[...] = low(acc_a[...])

    middle_own = middle[...]
    back2, gain2_part = norm_back(middle_own, norm_scale(middle_own), gain2, acc_b[...])
    gain_out[...] = jnp.zeros_like(gain_out)
    for s in range(count):
        gain_out[s, 1:2, :] = gain2_part[:, s * part : (s + 1) * part]
    grad_mid_own = wide(cot_all[mine, :]) + back2
    grad_mid[...] = grad_mid_own
    attn_own = low(grad_mid_own)
    attn_all[mine, :] = attn_own
    g_rows[...] = low(dot_nt(attn_own, w_out[...]))

    def g_copy(target, source):
        return remote(
            g_rows.at[:, span(target * part, part)], g_heads.at[span(source * rows, rows)],
            g_send.at[target], g_recv.at[source], target)

    others(lambda s: g_copy(s, me).start())
    g_heads[mine, :] = g_rows[:, span(me * part, part)]
    a_start(0, 1, 3, 2, 4)

    slab_at = span(me * slab, slab)

    def slab_block(block):
        at = span(block * rows, rows)
        active, slope = gelu_parts(dot(hidden2_all[at, :], w_up[:, slab_at]))
        active_s[at, :] = low(active)
        slope_s[at, :] = low(dot_nt(cot_all[at, :], w_down[slab_at, :]) * slope)

    slab_block(me)
    c_wait(0)
    h_wait(0)
    slab_block(mate)
    c_wait(2, 4)
    c_start(8, 10)
    h_wait(2, 4)
    h_start(8, 10)
    slab_block(over_x)
    slab_block(over_y)
    c_wait(7, 8)
    h_wait(7, 8)
    slab_block(flip(mate, 2))
    c_wait(9, 10)
    h_wait(9, 10)
    slab_block(flip(mate, 4))
    c_wait(5, 6)
    c_start(11, 12)
    h_wait(5, 6)
    h_start(11, 12)
    slab_block(corner)
    c_wait(11, 12)
    h_wait(11, 12)
    slab_block(flip(corner, 1))
    load_qkv.start()

    down_rows, up_rows = slab, rows * (ff // width)
    down_at, up_at = 0, down_rows
    out_at = up_at + up_rows
    mixed_at = out_at + part
    slabs = width // slab

    @pl.loop(0, slab // part)
    def _(t):
        own[span(down_at + t * part, part), :] = low(
            dot_tn(active_s[:, span(t * part, part)], cot_all[...]))

    z_outer(0, up_at // ZROWS)

    def u_copy(target, source):
        return remote(
            up_stage.at[span(target * rows, rows)],
            own.at[span(up_at + lax.div(source, slabs) * rows, rows),
                   span(lax.rem(source, slabs) * slab, slab)],
            u_send.at[target], u_recv.at[source], target)

    @pl.loop(0, count)
    def _(s):
        at = span(s * rows, rows)
        up_stage[at, :] = low(dot_tn(hidden2_all[:, at], slope_s[...]))

        @pl.when(s != me)
        def _():
            u_copy(s, me).start()

    own[span(up_at + lax.div(me, slabs) * rows, rows), span(lax.rem(me, slabs) * slab, slab)] = (
        up_stage[mine, :])
    a_wait(1)
    a_start(5, 7)
    a_wait(3)
    a_start(6, 9)

    others(lambda s: g_copy(me, s).wait_recv())
    for head in range(local):
        @pl.loop(0, count)
        def _(s):
            at = span(s * rows, rows)
            g_pad[head, at, :] = low(jnp.where(lane_head == head, wide(g_heads[at, :]), 0.0))
    k_acc[...] = jnp.zeros_like(k_acc)
    v_acc[...] = jnp.zeros_like(v_acc)

    def back_block(i):
        at = span(i * QBLOCK, QBLOCK)
        product = wide(g_heads[at, :]).T * o_turned[:, at]
        deltas = [
            jnp.sum(product[h * HEAD_DIM : (h + 1) * HEAD_DIM], axis=0, keepdims=True)
            for h in range(local)
        ]

        def step(j, turned):
            keys = span(j * QBLOCK, QBLOCK)
            for head in range(local):
                share = shares[head, keys, at]
                grad_share = dot_nt(mixed[keys, values_at], g_pad[head, at, :])
                grad_score = low(wide(share) * (grad_share - deltas[head]))
                v_acc[keys, :] += dot(share, g_pad[head, at, :])
                k_acc[keys, :] += dot(grad_score, q_pad[head, at, :])
                turned = turned + dot_tn(k_pad[head, keys, :], grad_score)
            return turned

        turned = lax.fori_loop(0, i + 1, step, jnp.zeros((part, QBLOCK), f32))
        mixed_grad[at, pl.ds(0, part)] = low((turned * factor).T)

    pl.loop(0, query_blocks - 1)(back_block)
    z_inner(1)
    pl.loop(query_blocks - 1, query_blocks)(back_block)
    mixed_grad[:, keys_at] = low(k_acc[...])
    mixed_grad[:, values_at] = low(v_acc[...])
    z_inner(2)

    def s_copy(k, target, source):
        return remote(
            mixed_stage.at[span(target * rows, rows), pl.ds(k * part, part)],
            own.at[span(mixed_at + k * rows, rows), span(source * part, part)],
            s_send.at[k, target], s_recv.at[k, source], target)

    def m_copy(k, target, source):
        return remote(
            mixed_grad.at[span(target * rows, rows), pl.ds(k * part, part)],
            mixed_rows.at[:, span(k * width + source * part, part)],
            m_send.at[k, target], m_recv.at[k, source], target)

    @pl.loop(0, count)
    def _(s):
        at = span(s * rows, rows)
        mixed_stage[at, :] = low(dot_tn(hidden1_all[:, at], mixed_grad[...]))

        @pl.when(s != me)
        def _():
            for k in range(3):
                s_copy(k, s, me).start()

    for k in range(3):
        own[span(mixed_at + k * rows, rows), span(me * part, part)] = (
            mixed_stage[mine, pl.ds(k * part, part)])
        mixed_rows[:, span(k * width + me * part, part)] = mixed_grad[mine, pl.ds(k * part, part)]

    @pl.loop(1, count)
    def _(step):
        s = lax.rem(me + step, count)
        for k in range(3):
            m_copy(k, s, me).start()

    z_inner(3)

    a_wait(0, 2, 4)
    a_start(8, 10)
    a_wait(5, 6)
    a_start(11, 12)
    z_inner(2)
    a_wait(7, 8, 9, 10, 11, 12)
    own[pl.ds(out_at, part), :] = low(dot(low(o_turned[...]), attn_all[...]))
    z_inner(up_at // ZROWS - z_done[0])

    others(lambda s: u_copy(me, s).wait_recv())
    z_outer(up_at // ZROWS, mixed_at // ZROWS)
    z_inner((mixed_at - up_at) // ZROWS // 2)

    for k in range(3):
        others(lambda s: s_copy(k, me, s).wait_recv())
    z_outer(mixed_at // ZROWS, chunks)
    z_inner(mixed_at // ZROWS - z_done[0])

    load_qkv.wait()
    for k in range(3):
        others(lambda s: m_copy(k, me, s).wait_recv())
    acc_a[...] = jnp.zeros_like(acc_a)

    @pl.loop(0, 3)
    def _(k):
        at = span(k * width, width)
        acc_a[...] += dot_nt(mixed_rows[:, at], w_up[:, at])

    frames_own = wide(frames_all[mine, :])
    back1, gain1_part = norm_back(frames_own, norm_scale(frames_own), gain1, acc_a[...])
    d_in_ref[...] = grad_mid[...] + back1

    for s in range(count):
        gain_out[s, 0:1, :] = gain1_part[:, s * part : (s + 1) * part]

    def n_copy(target, source):
        return remote(
            gain_out.at[target], gain_in.at[source], n_send.at[target], n_recv.at[source], target)

    def nz_copy(target, source):
        return remote(
            gain_z.at[source], gain_z.at[source], nz_send.at[target], nz_recv.at[source], me, target)

    others(lambda s: n_copy(s, me).start())
    gain_in[me] = gain_out[me]
    z_inner(4)
    others(lambda s: n_copy(me, s).wait_recv())
    gain_sum = gain_in[0]
    for s in range(1, count):
        gain_sum = gain_sum + gain_in[s]
    gain_z[plane] = gain_sum

    @pl.loop(1, planes)
    def _(step):
        nz_copy(lax.rem(plane + step, planes), plane).start()

    z_inner(chunks - z_done[0])

    @pl.loop(1, planes)
    def _(step):
        nz_copy(plane, lax.rem(plane + step, planes)).wait_recv()

    gain_sum = gain_z[0]
    for p in range(1, planes):
        gain_sum = gain_sum + gain_z[p]
    gains_ref[...] = gain_sum

    @pl.when(inner)
    def _():
        @pl.loop(chunks - ZLAG, chunks)
        def _(c):
            z_close(c)

    for finish in (f_finish, c_finish, h_finish, a_finish):
        finish()

    @pl.loop(1, count)
    def _(step):
        s = lax.rem(me + step, count)
        o_copy(s, me).wait_send()
        g_copy(s, me).wait_send()
        u_copy(s, me).wait_send()
        n_copy(s, me).wait_send()
        for k in range(3):
            s_copy(k, s, me).wait_send()
            m_copy(k, s, me).wait_send()

    @pl.loop(1, planes)
    def _(step):
        nz_copy(lax.rem(plane + step, planes), plane).wait_send()

    @pl.when(outer)
    def _():
        @pl.loop(0, chunks)
        def _(c):
            z_raw(c).wait_send()
            z_back(c).wait_recv()

    @pl.when(inner)
    def _():
        @pl.loop(0, chunks)
        def _(c):
            z_cross(c).wait_send()
            z_back(c).wait_send()


def shards_by_heads(frames, norm1_gain, w_qkv, w_out, norm2_gain, w_up, w_down, lengths, cotangent):
    _, rows, width = frames.shape
    ff = w_up.shape[1]
    count, planes = lax.axis_size("sq"), lax.axis_size("dp")
    total, part, slab = rows * count, width // count, ff // count
    local = part // HEAD_DIM
    bf16, f32 = jnp.bfloat16, jnp.float32
    blocks = ff // width
    own_rows = slab + rows * blocks + part + rows * 3
    chunks = own_rows // ZROWS
    vmem, anywhere = pl.BlockSpec(memory_space=pltpu.VMEM), pl.BlockSpec(memory_space=pl.ANY)
    smem = pl.BlockSpec(memory_space=pltpu.SMEM)

    def low_array(*shape):
        return pltpu.VMEM(shape, bf16)

    def wide_array(*shape):
        return pltpu.VMEM(shape, f32)

    def copies(*shape):
        return pltpu.SemaphoreType.DMA(shape)

    scratch = (
        [low_array(total, width)] * 5
        + [low_array(width, 3 * part), low_array(width, width), low_array(width, ff), low_array(ff, width)]
        + [low_array(total, 3 * part)]
        + [low_array(local, total, part)] * 4
        + [low_array(local, total, total), wide_array(total, QBLOCK), wide_array(part, total)]
        + [low_array(total, part), low_array(rows, width)]
        + [wide_array(rows, width)] * 4
        + [low_array(rows, width), low_array(total, part)]
        + [low_array(total, slab)] * 3
        + [low_array(total, 3 * part)] * 2
        + [low_array(rows, 3 * width)]
        + [wide_array(total, part)] * 2
        + [low_array(own_rows, width)] * 2
        + [wide_array(count, 8, part)] * 2
        + [wide_array(planes, 8, part)]
        + [copies(9), copies(4, 13), copies(4, 13)]
        + [copies(count)] * 4
        + [copies(3, count)] * 2
        + [copies(count)] * 2
        + [copies(3, count)] * 2
        + [copies(count)] * 2
        + [copies(planes)] * 2
        + [copies(chunks)] * 5
    )
    result, d_in, gains, sums = pl.pallas_call(
        functools.partial(layer_kernel, count, planes),
        out_shape=(
            jax.ShapeDtypeStruct((rows, width), bf16),
            jax.ShapeDtypeStruct((rows, width), f32),
            jax.ShapeDtypeStruct((8, part), f32),
            jax.ShapeDtypeStruct((own_rows, width), bf16),
        ),
        in_specs=[anywhere, vmem, anywhere, anywhere, vmem, anywhere, anywhere, smem, anywhere],
        out_specs=(vmem, vmem, vmem, vmem),
        scratch_shapes=scratch,
        compiler_params=pltpu.CompilerParams(
            collective_id=0, has_side_effects=True, vmem_limit_bytes=60 * 2**20),
    )(frames, norm1_gain[None], w_qkv, w_out, norm2_gain[None], w_up, w_down, lengths, cotangent)

    def from_blocks(first, number):
        pieces = sums[first : first + number * rows].reshape(number, rows, width)
        return pieces.swapaxes(0, 1).reshape(rows, number * width).astype(f32)

    grad_down = sums[:slab].astype(f32)
    grad_up = from_blocks(slab, blocks)
    grad_out = sums[slab + rows * blocks :][:part].astype(f32)
    grad_qkv = from_blocks(slab + rows * blocks + part, 3)
    return (result[None], d_in[None], gains[0], grad_qkv, grad_out, gains[1], grad_up, grad_down)


def solution(mesh):
    by_heads = HEADS % mesh.shape["sq"] == 0 and dict(mesh.shape) == {"dp": 4, "sq": 8}
    return jax.shard_map(
        shards_by_heads if by_heads else shards_by_rows,
        mesh=mesh,
        in_specs=(
            P("dp", "sq", None),
            P(),
            P(),
            P(),
            P(),
            P(),
            P(),
            P("dp", None),
            P("dp", "sq", None),
        ),
        out_specs=(
            P("dp", "sq", None),
            P("dp", "sq", None),
            P("sq"),
            P("sq", None),
            P("sq", None),
            P("sq"),
            P("sq", None),
            P("sq", None),
        ),
        check_vma=False,
    )
```

```python
import functools

import jax
import jax.numpy as jnp
from jax import lax
from jax.experimental import pallas as pl
from jax.experimental.pallas import tpu as pltpu
from jax.sharding import PartitionSpec as P

HEADS = 16
HEAD_DIM = 64


EPSILON = 1e-05
NEG_FILL = -1000000000.0
START_MAX = -1e30


def norm_scaled(values, gain):
    return values * lax.rsqrt(jnp.mean(values * values, axis=-1, keepdims=True) + EPSILON) * gain


def segment_ids(positions, item_ends):
    return jnp.sum((positions[None, :, None] >= item_ends[:, None, :]).astype(jnp.int32), axis=2)


def running_ends(lengths):
    items = jnp.arange(lengths.shape[1], dtype=jnp.int32)
    before = items[None, None, :] <= items[None, :, None]
    return jnp.sum(jnp.where(before, lengths[:, None, :], 0), axis=2)


def visible(query_pos, query_seg, key_pos, key_seg):
    return (key_pos[None, None, :] <= query_pos[None, :, None]) & (
        key_seg[:, None, :] == query_seg[:, :, None]
    )


def block_size(count, limit):
    for candidate in range(min(count, limit), 0, -1):
        if count % candidate == 0:
            return candidate
    return count


def over_blocks(carry, arrays, start, step_fn, limit):
    count = arrays[0].shape[1]
    size = block_size(count, limit)
    number = count // size
    if number == 1:
        return step_fn(carry, arrays, start)
    stacked = tuple(
        (
            jnp.swapaxes(member.reshape((member.shape[0], number, size) + member.shape[2:]), 0, 1)
            for member in arrays
        )
    )

    def turn(state, item):
        offset, pieces = item
        return (step_fn(state, pieces, start + offset * size), None)

    offsets = jnp.arange(number, dtype=jnp.int32)
    return lax.scan(turn, carry, (offsets, stacked))[0]


def contract_rows(left, right):
    return lax.dot_general(
        left, right, (((0,), (0,)), ((), ())), preferred_element_type=jnp.float32
    )


def times_transpose(left, right):
    return lax.dot_general(
        left, right, (((1,), (1,)), ((), ())), preferred_element_type=jnp.float32
    )


def heads_flat(values, batch, rows, width):
    return values.transpose(0, 2, 1, 3).reshape(batch * rows, width)


def shards_by_rows(frames, norm1_gain, w_qkv, w_out, norm2_gain, w_up, w_down, lengths, cotangent):
    batch = frames.shape[0]
    rows = frames.shape[1]
    width = frames.shape[2]
    factor = HEAD_DIM ** (-0.5)
    first = lax.axis_index("sq") * rows
    query_pos = first + jnp.arange(rows, dtype=jnp.int32)
    item_ends = running_ends(lengths)
    query_seg = segment_ids(query_pos, item_ends)
    frames_own = frames.reshape(batch * rows, width).astype(jnp.float32)
    hidden1, norm1_pull = jax.vjp(norm_scaled, frames_own, norm1_gain)
    hidden1_low = hidden1.astype(jnp.bfloat16)
    mixed = jnp.dot(hidden1_low, w_qkv, preferred_element_type=jnp.float32).astype(jnp.bfloat16)
    query_rows = mixed[:, :width].reshape(batch, rows, width)
    key_rows = mixed[:, width : 2 * width].reshape(batch, rows, width)
    value_rows = mixed[:, 2 * width :].reshape(batch, rows, width)
    queries = query_rows.reshape(batch, rows, HEADS, HEAD_DIM)
    keys_own = key_rows.reshape(batch, rows, HEADS, HEAD_DIM)
    values_own = value_rows.reshape(batch, rows, HEADS, HEAD_DIM)

    def forward_step(carry, pieces, start):
        key_piece, value_piece = pieces
        count = key_piece.shape[1]
        key_pos = start + jnp.arange(count, dtype=jnp.int32)
        key_seg = segment_ids(key_pos, item_ends)

        def forward_work(state):
            running_max, running_sum, accum = state
            keys_block = key_piece.reshape(batch, count, HEADS, HEAD_DIM)
            values_block = value_piece.reshape(batch, count, HEADS, HEAD_DIM)
            scores = (
                jnp.einsum(
                    "rqhd,rkhd->rhqk", queries, keys_block, preferred_element_type=jnp.float32
                )
                * factor
            )
            mask = visible(query_pos, query_seg, key_pos, key_seg)[:, None]
            scores = jnp.where(mask, scores, NEG_FILL)
            new_max = jnp.maximum(running_max, jnp.max(scores, axis=-1))
            weights = jnp.where(mask, jnp.exp(scores - new_max[..., None]), 0.0)
            decay = jnp.exp(running_max - new_max)
            new_sum = decay * running_sum + jnp.sum(weights, axis=-1)
            update = jnp.einsum(
                "rhqk,rkhd->rhqd",
                weights.astype(jnp.bfloat16),
                values_block,
                preferred_element_type=jnp.float32,
            )
            return (new_max, new_sum, decay[..., None] * accum + update)

        return lax.cond(start <= query_pos[-1], forward_work, lambda state: state, carry)

    start_state = (
        jnp.full((batch, HEADS, rows), START_MAX, jnp.float32),
        jnp.zeros((batch, HEADS, rows), jnp.float32),
        jnp.zeros((batch, HEADS, rows, HEAD_DIM), jnp.float32),
    )
    final_max, final_sum, accum = over_blocks(
        start_state,
        (
            lax.all_gather(key_rows, "sq", axis=1, tiled=True),
            lax.all_gather(value_rows, "sq", axis=1, tiled=True),
        ),
        jnp.int32(0),
        forward_step,
        512,
    )
    attended = heads_flat(accum / final_sum[..., None], batch, rows, width)
    log_total = final_max + jnp.log(final_sum)
    attended_low = attended.astype(jnp.bfloat16)
    middle = frames_own + jnp.dot(attended_low, w_out, preferred_element_type=jnp.float32)
    hidden2, norm2_pull = jax.vjp(norm_scaled, middle, norm2_gain)
    hidden2_low = hidden2.astype(jnp.bfloat16)
    upward = jnp.dot(hidden2_low, w_up, preferred_element_type=jnp.float32)
    active, gelu_pull = jax.vjp(jax.nn.gelu, upward)
    active_low = active.astype(jnp.bfloat16)
    result = middle + jnp.dot(active_low, w_down, preferred_element_type=jnp.float32)
    grad_top = cotangent.reshape(batch * rows, width).astype(jnp.float32)
    grad_branch = grad_top.astype(jnp.bfloat16)
    grad_down = contract_rows(active_low, grad_branch)
    grad_active = times_transpose(grad_branch, w_down)
    grad_upward = gelu_pull(grad_active)[0].astype(jnp.bfloat16)
    grad_up = contract_rows(hidden2_low, grad_upward)
    grad_hidden2 = times_transpose(grad_upward, w_up)
    grad_middle_part, grad_gain2 = norm2_pull(grad_hidden2)
    grad_middle = grad_top + grad_middle_part
    grad_attn = grad_middle.astype(jnp.bfloat16)
    grad_outproj = contract_rows(attended_low, grad_attn)
    grad_attended = times_transpose(grad_attn, w_out).astype(jnp.bfloat16)
    grad_rows_own = grad_attended.reshape(batch, rows, width)
    grad_heads = grad_attended.reshape(batch, rows, HEADS, HEAD_DIM)
    delta_rows = jnp.sum(
        (grad_attended.astype(jnp.float32) * attended).reshape(batch, rows, HEADS, HEAD_DIM), axis=3
    )
    delta = delta_rows.transpose(0, 2, 1)

    def query_step(carry, pieces, start):
        key_piece, value_piece = pieces
        count = key_piece.shape[1]
        key_pos = start + jnp.arange(count, dtype=jnp.int32)
        key_seg = segment_ids(key_pos, item_ends)

        def query_work(grad_query):
            keys_block = key_piece.reshape(batch, count, HEADS, HEAD_DIM)
            values_block = value_piece.reshape(batch, count, HEADS, HEAD_DIM)
            scores = (
                jnp.einsum(
                    "rqhd,rkhd->rhqk", queries, keys_block, preferred_element_type=jnp.float32
                )
                * factor
            )
            mask = visible(query_pos, query_seg, key_pos, key_seg)[:, None]
            shares = jnp.where(mask, jnp.exp(scores - log_total[..., None]), 0.0)
            grad_shares = jnp.einsum(
                "rqhd,rkhd->rhqk", grad_heads, values_block, preferred_element_type=jnp.float32
            )
            grad_scores = (shares * (grad_shares - delta[..., None])).astype(jnp.bfloat16)
            return grad_query + jnp.einsum(
                "rhqk,rkhd->rhqd", grad_scores, keys_block, preferred_element_type=jnp.float32
            )

        return lax.cond(start <= query_pos[-1], query_work, lambda state: state, carry)

    zero_query = jnp.zeros((batch, HEADS, rows, HEAD_DIM), jnp.float32)
    grad_query = over_blocks(
        zero_query,
        (
            lax.all_gather(key_rows, "sq", axis=1, tiled=True),
            lax.all_gather(value_rows, "sq", axis=1, tiled=True),
        ),
        jnp.int32(0),
        query_step,
        512,
    )

    def key_step(carry, pieces, start):
        query_piece, grad_piece, total_piece, delta_piece = pieces
        count = query_piece.shape[1]
        remote_pos = start + jnp.arange(count, dtype=jnp.int32)
        remote_seg = segment_ids(remote_pos, item_ends)

        def key_work(state):
            grad_key, grad_value = state
            remote_queries = query_piece.reshape(batch, count, HEADS, HEAD_DIM)
            remote_grads = grad_piece.reshape(batch, count, HEADS, HEAD_DIM)
            scores = (
                jnp.einsum(
                    "rqhd,rkhd->rhqk", remote_queries, keys_own, preferred_element_type=jnp.float32
                )
                * factor
            )
            mask = visible(remote_pos, remote_seg, query_pos, query_seg)[:, None]
            shares = jnp.where(
                mask, jnp.exp(scores - total_piece.transpose(0, 2, 1)[..., None]), 0.0
            )
            grad_value = grad_value + jnp.einsum(
                "rhqk,rqhd->rhkd",
                shares.astype(jnp.bfloat16),
                remote_grads,
                preferred_element_type=jnp.float32,
            )
            grad_shares = jnp.einsum(
                "rqhd,rkhd->rhqk", remote_grads, values_own, preferred_element_type=jnp.float32
            )
            grad_scores = (
                shares * (grad_shares - delta_piece.transpose(0, 2, 1)[..., None])
            ).astype(jnp.bfloat16)
            grad_key = grad_key + jnp.einsum(
                "rhqk,rqhd->rhkd", grad_scores, remote_queries, preferred_element_type=jnp.float32
            )
            return (grad_key, grad_value)

        return lax.cond(start + count - 1 >= first, key_work, lambda state: state, carry)

    grad_key, grad_value = over_blocks(
        (zero_query, zero_query),
        (
            lax.all_gather(query_rows, "sq", axis=1, tiled=True),
            lax.all_gather(grad_rows_own, "sq", axis=1, tiled=True),
            lax.all_gather(
                log_total.transpose(0, 2, 1).astype(jnp.bfloat16), "sq", axis=1, tiled=True
            ).astype(jnp.float32),
            lax.all_gather(delta_rows.astype(jnp.bfloat16), "sq", axis=1, tiled=True).astype(
                jnp.float32
            ),
        ),
        jnp.int32(0),
        key_step,
        512,
    )
    grad_mixed = jnp.concatenate(
        [
            heads_flat(grad_query * factor, batch, rows, width),
            heads_flat(grad_key * factor, batch, rows, width),
            heads_flat(grad_value, batch, rows, width),
        ],
        axis=1,
    ).astype(jnp.bfloat16)
    grad_qkv = contract_rows(hidden1_low, grad_mixed)
    grad_hidden1 = times_transpose(grad_mixed, w_qkv)
    grad_frames_part, grad_gain1 = norm1_pull(grad_hidden1)
    grad_frames = (grad_middle + grad_frames_part).reshape(batch, rows, width)
    result_rows = result.astype(jnp.bfloat16).reshape(batch, rows, width)
    shares_sq = (
        lax.psum_scatter(grad_gain1, "sq", scatter_dimension=0, tiled=True),
        lax.psum_scatter(grad_qkv, "sq", scatter_dimension=0, tiled=True),
        lax.psum_scatter(grad_outproj, "sq", scatter_dimension=0, tiled=True),
        lax.psum_scatter(grad_gain2, "sq", scatter_dimension=0, tiled=True),
        lax.psum_scatter(grad_up, "sq", scatter_dimension=0, tiled=True),
        lax.psum_scatter(grad_down, "sq", scatter_dimension=0, tiled=True),
    )
    totals = (
        lax.psum(shares_sq[0].astype(jnp.bfloat16), "dp").astype(jnp.float32),
        lax.psum(shares_sq[1].astype(jnp.bfloat16), "dp").astype(jnp.float32),
        lax.psum(shares_sq[2].astype(jnp.bfloat16), "dp").astype(jnp.float32),
        lax.psum(shares_sq[3].astype(jnp.bfloat16), "dp").astype(jnp.float32),
        lax.psum(shares_sq[4].astype(jnp.bfloat16), "dp").astype(jnp.float32),
        lax.psum(shares_sq[5].astype(jnp.bfloat16), "dp").astype(jnp.float32),
    )
    return (
        result_rows,
        grad_frames,
        totals[0],
        totals[1],
        totals[2],
        totals[3],
        totals[4],
        totals[5],
    )


MESH = pl.DeviceIdType.MESH
ZROWS = 32
ZLAG = 2
QBLOCK = 256
KEEP = pltpu.VMEM


def dot(left, right):
    return jnp.dot(left, right, preferred_element_type=jnp.float32)


def dot_nt(left, right):
    return lax.dot_general(
        left, right, (((1,), (1,)), ((), ())), preferred_element_type=jnp.float32
    )


def dot_tn(left, right):
    return lax.dot_general(
        left, right, (((0,), (0,)), ((), ())), preferred_element_type=jnp.float32
    )


def low(values):
    return values.astype(jnp.bfloat16)


def wide(values):
    return values.astype(jnp.float32)


def span(start, size):
    return pl.ds(pl.multiple_of(start, size), size)


def norm_scale(values):
    return lax.rsqrt(jnp.mean(values * values, axis=-1, keepdims=True) + EPSILON)


def norm_back(values, scale, gain, grad):
    scaled = gain * grad
    inner = jnp.mean(scaled * values, axis=-1, keepdims=True)
    part = scale * scaled - values * (scale * scale * scale) * inner
    return part, jnp.sum(grad * values * scale, axis=0, keepdims=True)


def gelu_parts(values):
    root = 0.7978845608028654
    square = values * values
    inner = jnp.tanh(root * values * (1.0 + 0.044715 * square))
    half = 0.5 * (1.0 + inner)
    slope = half + 0.5 * root * values * (1.0 - inner * inner) * (1.0 + 0.134145 * square)
    return values * half, slope


def layer_kernel(
    count, planes,
    frames_in, gain1_ref, w_qkv_in, w_out_in, gain2_ref, w_up_in, w_down_in, lengths_ref, cot_in,
    result_ref, d_in_ref, gains_ref, sum_ref,
    frames_all, hidden1_all, cot_all, hidden2_all, attn_all,
    w_heads, w_out, w_up, w_down,
    mixed, q_pad, k_pad, v_pad, g_pad, shares, o_turned, o_heads, o_rows,
    middle, acc_a, acc_b, grad_mid, g_rows, g_heads,
    active_s, slope_s, up_stage, mixed_grad, mixed_stage, mixed_rows,
    own, cross_in, gain_out, gain_in, gain_z,
    load_sem, ag_send, ag_recv, swap_send, swap_recv, z_send, z_outer_recv, z_cross_recv,
):
    bf16, f32 = jnp.bfloat16, jnp.float32
    rows, width = result_ref.shape
    total = rows * count
    part = width // count
    local = part // HEAD_DIM
    ff = w_up.shape[1]
    slab = ff // count
    half = rows // 2
    factor = HEAD_DIM ** (-0.5)
    me, plane = lax.axis_index("sq"), lax.axis_index("dp")

    def flip(index, bit):
        return index + bit - 2 * bit * lax.rem(lax.div(index, bit), 2)

    mate, over_x, over_y = flip(me, 1), flip(me, 2), flip(me, 4)
    corner = flip(over_x, 4)
    inner = (plane == 1) | (plane == 2)
    outer = (plane == 0) | (plane == 3)
    z_mate = planes - 1 - plane
    z_edge = jnp.where(plane == 1, 0, planes - 1)
    z_core = jnp.where(plane == 0, 1, planes - 2)

    def remote(source, target, send, recv, to, to_plane=None):
        return pltpu.make_async_remote_copy(
            src_ref=source, dst_ref=target, send_sem=send, recv_sem=recv,
            device_id=(plane if to_plane is None else to_plane, to), device_id_type=MESH,
        )

    def others(body):
        @pl.loop(1, count)
        def _(step):
            body(lax.rem(me + step, count))

    mine = span(me * rows, rows)
    loads = [
        pltpu.make_async_copy(frames_in.at[0], frames_all.at[mine], load_sem.at[0]),
        pltpu.make_async_copy(cot_in.at[0], cot_all.at[mine], load_sem.at[1]),
    ] + [
        pltpu.make_async_copy(
            w_qkv_in.at[:, span(k * width + me * part, part)],
            w_heads.at[:, pl.ds(k * part, part)],
            load_sem.at[2 + k],
        )
        for k in range(3)
    ] + [
        pltpu.make_async_copy(w_out_in, w_out, load_sem.at[5]),
        pltpu.make_async_copy(w_up_in, w_up, load_sem.at[6]),
        pltpu.make_async_copy(w_down_in, w_down, load_sem.at[7]),
    ]
    load_qkv = pltpu.make_async_copy(w_qkv_in, w_up.at[:, pl.ds(0, 3 * width)], load_sem.at[8])
    for load in loads[:5]:
        load.start()

    barrier = pltpu.get_barrier_semaphore()
    others(lambda s: pl.semaphore_signal(
        barrier, inc=1, device_id=(plane, s), device_id_type=MESH))

    @pl.loop(1, planes)
    def _(step):
        pl.semaphore_signal(
            barrier, inc=1, device_id=(lax.rem(plane + step, planes), me), device_id_type=MESH)

    pl.semaphore_wait(barrier, count - 1 + planes - 1)

    def slots(index):
        return [
            (me, None, mate, mate, 0),
            (me, 0, over_x, over_x, 1), (me, 1, over_x, over_x, 2),
            (me, 1, over_y, over_y, 3), (me, 0, over_y, over_y, 4),
            (over_x, 0, over_y, corner, 5), (over_y, 1, over_x, corner, 6),
            (over_x, 0, mate, flip(mate, 2), 7), (over_x, 1, mate, flip(mate, 2), 7),
            (over_y, 1, mate, flip(mate, 4), 8), (over_y, 0, mate, flip(mate, 4), 8),
            (corner, 0, mate, flip(corner, 1), 9), (corner, 1, mate, flip(corner, 1), 9),
        ][index]

    def gather(number, array, source=None):
        def piece(block, which):
            if which is None:
                return span(block * rows, rows)
            return span(block * rows + which * half, half)

        def copy(slot, sent=True, whole=False):
            block, which, target, arrives, sem = slots(slot)
            there = piece(block if sent else arrives, None if whole else which)
            here = array.at[there]
            if sent and source is not None and slot < 5:
                here = source if which is None else source.at[pl.ds(which * half, half)]
            return remote(here, array.at[there], ag_send.at[number], ag_recv.at[number, sem], target)

        def start(*numbers):
            for slot in numbers:
                copy(slot).start()

        def wait(*numbers):
            for slot in numbers:
                copy(slot, sent=False, whole=slot >= 7).wait_recv()

        def finish():
            sent = array.at[pl.ds(0, (count - 1) * rows)]
            remote(sent, sent, ag_send.at[number], ag_recv.at[number, 0], mate).wait_send()

        return start, wait, finish

    def swap(number, pairs, whole):
        def start(target):
            for source, dest in pairs(target, me):
                remote(source, dest, swap_send.at[number], swap_recv.at[number], target).start()

        def wait():
            remote(whole, whole, swap_send.at[number], swap_recv.at[number], mate).wait_recv()

        def finish():
            remote(whole, whole, swap_send.at[number], swap_recv.at[number], mate).wait_send()

        return start, wait, finish

    f_start, f_wait, f_finish = gather(0, frames_all, frames_in.at[0])
    c_start, c_wait, c_finish = gather(1, cot_all, cot_in.at[0])
    h_start, h_wait, h_finish = gather(2, hidden2_all)
    a_start, a_wait, a_finish = gather(3, attn_all)

    def z_raw(c):
        at = span(c * ZROWS, ZROWS)
        return remote(own.at[at], sum_ref.at[at], z_send.at[0], z_outer_recv.at[c], me, z_core)

    def z_cross(c):
        at = span(c * ZROWS, ZROWS)
        return remote(own.at[at], cross_in.at[at], z_send.at[0], z_cross_recv.at[c], me, z_mate)

    def z_back(c):
        at = span(c * ZROWS, ZROWS)
        return remote(sum_ref.at[at], sum_ref.at[at], z_send.at[1], z_outer_recv.at[c], me, z_edge)

    def z_join(c):
        at = span(c * ZROWS, ZROWS)
        z_raw(c).wait_recv()
        own[at, :] = low(wide(own[at, :]) + wide(sum_ref[at, :]))
        z_cross(c).start()

    def z_close(c):
        at = span(c * ZROWS, ZROWS)
        z_cross(c).wait_recv()
        sum_ref[at, :] = low(wide(own[at, :]) + wide(cross_in[at, :]))
        z_back(c).start()

    chunks = own.shape[0] // ZROWS
    z_done = [0]

    def z_inner(number):
        first, last = z_done[0], z_done[0] + number
        z_done[0] = last

        @pl.when(inner)
        def _():
            split = min(max(first, ZLAG), last)
            for c in range(first, split):
                z_join(c)
            if last > split:
                @pl.loop(split, last)
                def _(c):
                    z_join(c)
                    z_close(c - ZLAG)

    def z_outer(first, last):
        @pl.when(outer)
        def _():
            @pl.loop(first, last)
            def _(c):
                z_raw(c).start()

    f_start(0, 1, 3, 2, 4)
    for load in loads[5:]:
        load.start()
    pair = 2 * rows
    lane_head = lax.broadcasted_iota(jnp.int32, (pair, part), 1) // HEAD_DIM
    gain1 = gain1_ref[...]
    gain2 = gain2_ref[...]

    def chip(index):
        return span(lax.div(index, 2) * pair, pair)

    def padded(ref, at, values):
        for head in range(local):
            ref[head, at, :] = low(jnp.where(lane_head == head, values, 0.0))

    def qkv_chip(index):
        at = chip(index)
        values = wide(frames_all[at, :])
        hidden = low(values * norm_scale(values) * gain1)
        hidden1_all[at, :] = hidden
        projected = low(dot(hidden, w_heads[...]))
        mixed[at, :] = projected
        padded(q_pad, at, wide(projected[:, :part]) * factor)
        padded(k_pad, at, wide(projected[:, part : 2 * part]))
        padded(v_pad, at, wide(projected[:, 2 * part :]))

    loads[0].wait()
    for k in range(3):
        loads[2 + k].wait()
    f_wait(0)
    qkv_chip(me)
    f_wait(1)
    f_start(5, 7)
    f_wait(3)
    f_start(6, 9)
    c_start(0, 1, 3, 2, 4)
    f_wait(2)
    f_start(8)
    f_wait(4)
    f_start(10)
    f_wait(7)
    qkv_chip(over_x)
    f_wait(9)
    qkv_chip(over_y)
    f_wait(5)
    f_start(11)
    f_wait(6)
    f_start(12)
    f_wait(11)
    qkv_chip(corner)

    ends, running = [], None
    for item in range(lengths_ref.shape[1]):
        length = lengths_ref[0, item]
        running = length if running is None else running + length
        ends.append(running)

    keys_at = pl.ds(part, part)
    values_at = pl.ds(2 * part, part)
    query_blocks = total // QBLOCK
    per_block = QBLOCK // rows

    def o_pairs(target, source):
        yield o_heads.at[span(target * rows, rows)], o_rows.at[:, span(source * part, part)]

    o_start, o_wait, o_finish = swap(0, o_pairs, o_heads.at[pl.ds(0, total - rows)])

    for i in range(query_blocks):
        at, keys = pl.ds(i * QBLOCK, QBLOCK), pl.ds(0, (i + 1) * QBLOCK)
        query_pos = i * QBLOCK + lax.broadcasted_iota(jnp.int32, (1, QBLOCK), 1)
        begin = jnp.zeros((1, QBLOCK), jnp.int32)
        for end in ends:
            begin = jnp.maximum(begin, jnp.where(query_pos >= end, end, 0))
        key_pos = lax.broadcasted_iota(jnp.int32, ((i + 1) * QBLOCK, 1), 0)
        mask = (key_pos <= query_pos) & (key_pos >= begin)
        turned = None
        for head in range(local):
            score = jnp.where(mask, dot_nt(mixed[keys, keys_at], q_pad[head, at, :]), NEG_FILL)
            weight = jnp.exp(score - jnp.max(score, axis=0, keepdims=True))
            share = low(weight * (1.0 / jnp.sum(weight, axis=0, keepdims=True)))
            shares[head, keys, at] = share
            value = dot_tn(v_pad[head, keys, :], share)
            turned = value if turned is None else turned + value
        o_turned[:, at] = turned
        o_heads[at, :] = low(turned.T)
        for k in range(per_block):
            target = i * per_block + k

            @pl.when(target != me)
            def _():
                o_start(target)

            @pl.when(target == me)
            def _():
                o_rows[:, span(me * part, part)] = o_heads[mine, :]

    c_wait(1)
    c_start(5, 7)
    c_wait(3)
    c_start(6, 9)
    loads[5].wait()
    o_wait()
    middle_own = wide(frames_all[mine, :]) + dot(o_rows[...], w_out[...])
    middle[...] = middle_own
    hidden2_all[mine, :] = low(middle_own * norm_scale(middle_own) * gain2)
    h_start(0, 1, 3, 2, 4)

    c_wait(2)
    c_start(8)
    c_wait(4)
    c_start(10)
    loads[1].wait()
    loads[6].wait()
    loads[7].wait()
    acc_a[...] = middle_own
    acc_b[...] = jnp.zeros_like(acc_b)

    def ff_tile(t):
        at = span(t * width, width)
        active, slope = gelu_parts(dot(hidden2_all[mine, :], w_up[:, at]))
        acc_a[...] += dot(low(active), w_down[at, :])
        grad = low(dot_nt(cot_all[mine, :], w_down[at, :]) * slope)
        acc_b[...] += dot_nt(grad, w_up[:, at])

    tiles = ff // width
    pl.loop(0, tiles // 2)(ff_tile)
    h_wait(1)
    h_start(5, 7)
    h_wait(3)
    h_start(6, 9)
    c_wait(5)
    c_start(11)
    c_wait(6)
    c_start(12)
    pl.loop(tiles // 2, tiles - 1)(ff_tile)
    h_wait(2)
    h_start(8)
    h_wait(4)
    h_start(10)
    pl.loop(tiles - 1, tiles)(ff_tile)
    h_wait(5)
    h_start(11)
    h_wait(6)
    h_start(12)

    slab_at = span(me * slab, slab)

    def slab_chip(index):
        at = chip(index)
        active, slope = gelu_parts(dot(hidden2_all[at, :], w_up[:, slab_at]))
        active_s[at, :] = low(active)
        slope_s[at, :] = low(slope)

    h_wait(0)
    slab_chip(me)
    h_wait(7)
    slab_chip(over_x)
    h_wait(9)
    slab_chip(over_y)
    h_wait(11)
    slab_chip(corner)
    load_qkv.start()
    c_wait(0, 7, 9, 11)

    down_rows, up_rows = slab, rows * (ff // width)
    down_at, up_at = 0, down_rows
    out_at = up_at + up_rows
    mixed_at = out_at + part
    slabs = width // slab

    @pl.loop(0, slab // part)
    def _(t):
        at = span(down_at + t * part, part)
        own[at, :] = low(dot_tn(active_s[:, span(t * part, part)], cot_all[...]))

        @pl.when(outer)
        def _():
            for c in range(part // ZROWS):
                z_raw(t * (part // ZROWS) + c).start()

    result_ref[...] = low(acc_a[...])
    middle_own = middle[...]
    back2, gain2_part = norm_back(middle_own, norm_scale(middle_own), gain2, acc_b[...])
    gain_out[...] = jnp.zeros_like(gain_out)
    for s in range(count):
        gain_out[s, 1:2, :] = gain2_part[:, s * part : (s + 1) * part]
    grad_mid_own = wide(cot_all[mine, :]) + back2
    grad_mid[...] = grad_mid_own
    attn_own = low(grad_mid_own)
    attn_all[mine, :] = attn_own
    g_rows[...] = low(dot_nt(attn_own, w_out[...]))

    def g_pairs(target, source):
        yield g_rows.at[:, span(target * part, part)], g_heads.at[span(source * rows, rows)]

    g_start, g_wait, g_finish = swap(1, g_pairs, g_heads.at[pl.ds(0, total - rows)])
    others(g_start)
    g_heads[mine, :] = g_rows[:, span(me * part, part)]

    for c in range(0, count, 2):
        at = span(c * rows, pair)
        slope_s[at, :] = low(dot_nt(cot_all[at, :], w_down[slab_at, :]) * wide(slope_s[at, :]))

    def u_pairs(target, source):
        yield (
            up_stage.at[span(target * rows, rows)],
            own.at[span(up_at + lax.div(source, slabs) * rows, rows),
                   span(lax.rem(source, slabs) * slab, slab)],
        )

    u_start, u_wait, u_finish = swap(2, u_pairs, up_stage.at[pl.ds(0, total - rows)])
    z_inner(1)

    @pl.loop(0, count // 2)
    def _(c):
        at = span(c * pair, pair)
        up_stage[at, :] = low(dot_tn(hidden2_all[:, at], slope_s[...]))
        for s in (2 * c, 2 * c + 1):
            @pl.when(s != me)
            def _():
                u_start(s)

    own[span(up_at + lax.div(me, slabs) * rows, rows), span(lax.rem(me, slabs) * slab, slab)] = (
        up_stage[mine, :])
    a_start(0, 1, 3, 2, 4)
    z_inner(2)

    g_wait()
    for c in range(count // 2):
        at = span(c * pair, pair)
        padded(g_pad, at, wide(g_heads[at, :]))

    def late(j):
        return pl.ds(j * QBLOCK, total - j * QBLOCK)

    for j in range(query_blocks):
        keys = pl.ds(j * QBLOCK, QBLOCK)
        grad = None
        for head in range(local):
            value = dot(shares[head, keys, late(j)], g_pad[head, late(j), :])
            grad = value if grad is None else grad + value
        mixed_grad[keys, values_at] = low(grad)
    z_inner(2)
    for i in range(query_blocks):
        at, keys = pl.ds(i * QBLOCK, QBLOCK), pl.ds(0, (i + 1) * QBLOCK)
        product = wide(g_heads[at, :]).T * o_turned[:, at]
        turned = None
        for head in range(local):
            delta = jnp.sum(
                product[head * HEAD_DIM : (head + 1) * HEAD_DIM], axis=0, keepdims=True)
            grad_share = dot_nt(mixed[keys, values_at], g_pad[head, at, :])
            grad_score = low(wide(shares[head, keys, at]) * (grad_share - delta))
            shares[head, keys, at] = grad_score
            value = dot_tn(k_pad[head, keys, :], grad_score)
            turned = value if turned is None else turned + value
        mixed_grad[at, pl.ds(0, part)] = low((turned * factor).T)
        z_inner(1)
    for j in range(query_blocks):
        keys = pl.ds(j * QBLOCK, QBLOCK)
        grad = None
        for head in range(local):
            value = dot(shares[head, keys, late(j)], q_pad[head, late(j), :])
            grad = value if grad is None else grad + value
        mixed_grad[keys, keys_at] = low(grad)
    z_inner(2)

    def s_pairs(target, source):
        for k in range(3):
            yield (
                mixed_stage.at[span(target * rows, rows), pl.ds(k * part, part)],
                own.at[span(mixed_at + k * rows, rows), span(source * part, part)],
            )

    def m_pairs(target, source):
        for k in range(3):
            yield (
                mixed_grad.at[span(target * rows, rows), pl.ds(k * part, part)],
                mixed_rows.at[:, span(k * width + source * part, part)],
            )

    s_start, s_wait, s_finish = swap(3, s_pairs, mixed_stage.at[pl.ds(0, total - rows)])
    m_start, m_wait, m_finish = swap(4, m_pairs, mixed_grad.at[pl.ds(0, total - rows)])

    @pl.loop(0, count // 2)
    def _(c):
        at = span(c * pair, pair)
        mixed_stage[at, :] = low(dot_tn(hidden1_all[:, at], mixed_grad[...]))
        for s in (2 * c, 2 * c + 1):
            @pl.when(s != me)
            def _():
                s_start(s)

    for k in range(3):
        own[span(mixed_at + k * rows, rows), span(me * part, part)] = (
            mixed_stage[mine, pl.ds(k * part, part)])
        mixed_rows[:, span(k * width + me * part, part)] = mixed_grad[mine, pl.ds(k * part, part)]
    a_wait(1)
    a_start(5, 7)
    a_wait(3)
    a_start(6, 9)
    a_wait(2)
    a_start(8)
    a_wait(4)
    a_start(10)
    others(m_start)
    z_inner(2)
    u_wait()
    z_outer(up_at // ZROWS, out_at // ZROWS)
    z_inner(2)

    a_wait(5)
    a_start(11)
    a_wait(6)
    a_start(12)
    z_inner(2)
    a_wait(0, 7, 9, 11)
    own[pl.ds(out_at, part), :] = low(dot(low(o_turned[...]), attn_all[...]))
    z_outer(out_at // ZROWS, mixed_at // ZROWS)
    z_inner(4)
    s_wait()
    z_outer(mixed_at // ZROWS, chunks)
    z_inner(6)

    load_qkv.wait()
    m_wait()
    acc_a[...] = jnp.zeros_like(acc_a)

    @pl.loop(0, 3)
    def _(k):
        at = span(k * width, width)
        acc_a[...] += dot_nt(mixed_rows[:, at], w_up[:, at])

    frames_own = wide(frames_all[mine, :])
    back1, gain1_part = norm_back(frames_own, norm_scale(frames_own), gain1, acc_a[...])
    d_in_ref[...] = grad_mid[...] + back1
    z_inner(2)

    for s in range(count):
        gain_out[s, 0:1, :] = gain1_part[:, s * part : (s + 1) * part]

    def n_pairs(target, source):
        yield gain_out.at[target], gain_in.at[source]

    n_start, n_wait, n_finish = swap(5, n_pairs, gain_out.at[pl.ds(0, count - 1)])

    def nz_copy(target, source):
        return remote(
            gain_z.at[source], gain_z.at[source], swap_send.at[6], swap_recv.at[6], me, target)

    others(n_start)
    gain_in[me] = gain_out[me]
    z_inner(4)
    n_wait()
    gain_sum = gain_in[0]
    for s in range(1, count):
        gain_sum = gain_sum + gain_in[s]
    gain_z[plane] = gain_sum

    @pl.loop(1, planes)
    def _(step):
        nz_copy(lax.rem(plane + step, planes), plane).start()

    z_inner(chunks - z_done[0])
    gains_all = gain_z.at[pl.ds(0, planes - 1)]
    all_gains = remote(gains_all, gains_all, swap_send.at[6], swap_recv.at[6], mate)
    all_gains.wait_recv()
    gain_sum = gain_z[0]
    for p in range(1, planes):
        gain_sum = gain_sum + gain_z[p]
    gains_ref[...] = gain_sum

    @pl.when(inner)
    def _():
        @pl.loop(chunks - ZLAG, chunks)
        def _(c):
            z_close(c)

    for finish in (
        f_finish, c_finish, h_finish, a_finish,
        o_finish, g_finish, u_finish, s_finish, m_finish, n_finish,
    ):
        finish()
    all_gains.wait_send()

    @pl.when(outer)
    def _():
        remote(own, own, z_send.at[0], z_outer_recv.at[0], me, z_core).wait_send()

        @pl.loop(0, chunks)
        def _(c):
            z_back(c).wait_recv()

    @pl.when(inner)
    def _():
        remote(own, own, z_send.at[0], z_outer_recv.at[0], me, z_mate).wait_send()
        remote(own, own, z_send.at[1], z_outer_recv.at[0], me, z_edge).wait_send()


def finish_kernel(
    result_in, d_in_in, gains_in, sum_in,
    result_ref, d_in_ref, gain1_ref, qkv_ref, out_ref, gain2_ref, up_ref, down_ref,
    staged, gains, sems,
):
    rows, width = result_in.shape
    slab, part = down_ref.shape[0], out_ref.shape[0]
    targets = [down_ref]
    starts = [0]
    sizes = [slab]
    for ref, tall in ((up_ref, rows), (out_ref, part), (qkv_ref, rows)):
        for k in range(ref.shape[1] // width):
            starts.append(starts[-1] + sizes[-1])
            sizes.append(tall)
            targets.append(ref.at[:, pl.ds(k * width, width)])
    copies = [
        pltpu.make_async_copy(result_in, result_ref.at[0], sems.at[0]),
        pltpu.make_async_copy(d_in_in, d_in_ref.at[0], sems.at[1]),
    ]
    for copy in copies:
        copy.start()
    for k, (first, size, target) in enumerate(zip(starts, sizes, targets)):
        at = pl.ds(first, size)
        staged[at, :] = sum_in[at, :].astype(jnp.float32)
        copy = pltpu.make_async_copy(staged.at[at], target, sems.at[2 + k])
        copy.start()
        copies.append(copy)
    gain1_ref[...] = gains_in[0]
    gain2_ref[...] = gains_in[1]
    for copy in copies:
        copy.wait()


def shards_by_heads(frames, norm1_gain, w_qkv, w_out, norm2_gain, w_up, w_down, lengths, cotangent):
    _, rows, width = frames.shape
    ff = w_up.shape[1]
    count, planes = lax.axis_size("sq"), lax.axis_size("dp")
    total, part, slab = rows * count, width // count, ff // count
    local = part // HEAD_DIM
    bf16, f32 = jnp.bfloat16, jnp.float32
    blocks = ff // width
    own_rows = slab + rows * blocks + part + rows * 3
    chunks = own_rows // ZROWS
    vmem, anywhere = pl.BlockSpec(memory_space=pltpu.VMEM), pl.BlockSpec(memory_space=pl.ANY)
    smem = pl.BlockSpec(memory_space=pltpu.SMEM)

    def low_array(*shape):
        return pltpu.VMEM(shape, bf16)

    def wide_array(*shape):
        return pltpu.VMEM(shape, f32)

    def copies(*shape):
        return pltpu.SemaphoreType.DMA(shape)

    scratch = (
        [low_array(total, width)] * 5
        + [low_array(width, 3 * part), low_array(width, width), low_array(width, ff), low_array(ff, width)]
        + [low_array(total, 3 * part)]
        + [low_array(local, total, part)] * 4
        + [low_array(local, total, total), wide_array(part, total)]
        + [low_array(total, part), low_array(rows, width)]
        + [wide_array(rows, width)] * 4
        + [low_array(rows, width), low_array(total, part)]
        + [low_array(total, slab)] * 3
        + [low_array(total, 3 * part)] * 2
        + [low_array(rows, 3 * width)]
        + [low_array(own_rows, width)] * 2
        + [wide_array(count, 8, part)] * 2
        + [wide_array(planes, 8, part)]
        + [copies(9), copies(4), copies(4, 10), copies(7), copies(7), copies(2)]
        + [copies(chunks)] * 2
    )
    kept = pl.pallas_call(
        functools.partial(layer_kernel, count, planes),
        out_shape=(
            KEEP((rows, width), bf16),
            KEEP((rows, width), f32),
            KEEP((8, part), f32),
            KEEP((own_rows, width), bf16),
        ),
        in_specs=[anywhere, vmem, anywhere, anywhere, vmem, anywhere, anywhere, smem, anywhere],
        out_specs=(vmem, vmem, vmem, vmem),
        scratch_shapes=scratch,
        compiler_params=pltpu.CompilerParams(
            collective_id=0, has_side_effects=True, vmem_limit_bytes=60 * 2**20),
    )(frames, norm1_gain[None], w_qkv, w_out, norm2_gain[None], w_up, w_down, lengths, cotangent)
    return pl.pallas_call(
        finish_kernel,
        out_shape=tuple(
            jax.ShapeDtypeStruct(shape, kind)
            for shape, kind in (
                ((1, rows, width), bf16), ((1, rows, width), f32), ((part,), f32),
                ((part, 3 * width), f32), ((part, width), f32), ((part,), f32),
                ((part, ff), f32), ((slab, width), f32),
            )
        ),
        in_specs=[vmem] * 4,
        out_specs=(anywhere, anywhere, vmem, anywhere, anywhere, vmem, anywhere, anywhere),
        scratch_shapes=[wide_array(own_rows, width), wide_array(8, part), copies(11)],
        compiler_params=pltpu.CompilerParams(vmem_limit_bytes=24 * 2**20),
    )(*kept)


def solution(mesh):
    by_heads = HEADS % mesh.shape["sq"] == 0 and dict(mesh.shape) == {"dp": 4, "sq": 8}
    return jax.shard_map(
        shards_by_heads if by_heads else shards_by_rows,
        mesh=mesh,
        in_specs=(
            P("dp", "sq", None),
            P(),
            P(),
            P(),
            P(),
            P(),
            P(),
            P("dp", None),
            P("dp", "sq", None),
        ),
        out_specs=(
            P("dp", "sq", None),
            P("dp", "sq", None),
            P("sq"),
            P("sq", None),
            P("sq", None),
            P("sq"),
            P("sq", None),
            P("sq", None),
        ),
        check_vma=False,
    )
```

```python
import functools

import jax
import jax.numpy as jnp
from jax import lax
from jax.experimental import pallas as pl
from jax.experimental.pallas import tpu as pltpu
from jax.sharding import PartitionSpec as P

HEADS = 16
HEAD_DIM = 64


EPSILON = 1e-05
NEG_FILL = -1000000000.0
START_MAX = -1e30


def norm_scaled(values, gain):
    return values * lax.rsqrt(jnp.mean(values * values, axis=-1, keepdims=True) + EPSILON) * gain


def segment_ids(positions, item_ends):
    return jnp.sum((positions[None, :, None] >= item_ends[:, None, :]).astype(jnp.int32), axis=2)


def running_ends(lengths):
    items = jnp.arange(lengths.shape[1], dtype=jnp.int32)
    before = items[None, None, :] <= items[None, :, None]
    return jnp.sum(jnp.where(before, lengths[:, None, :], 0), axis=2)


def visible(query_pos, query_seg, key_pos, key_seg):
    return (key_pos[None, None, :] <= query_pos[None, :, None]) & (
        key_seg[:, None, :] == query_seg[:, :, None]
    )


def block_size(count, limit):
    for candidate in range(min(count, limit), 0, -1):
        if count % candidate == 0:
            return candidate
    return count


def over_blocks(carry, arrays, start, step_fn, limit):
    count = arrays[0].shape[1]
    size = block_size(count, limit)
    number = count // size
    if number == 1:
        return step_fn(carry, arrays, start)
    stacked = tuple(
        (
            jnp.swapaxes(member.reshape((member.shape[0], number, size) + member.shape[2:]), 0, 1)
            for member in arrays
        )
    )

    def turn(state, item):
        offset, pieces = item
        return (step_fn(state, pieces, start + offset * size), None)

    offsets = jnp.arange(number, dtype=jnp.int32)
    return lax.scan(turn, carry, (offsets, stacked))[0]


def contract_rows(left, right):
    return lax.dot_general(
        left, right, (((0,), (0,)), ((), ())), preferred_element_type=jnp.float32
    )


def times_transpose(left, right):
    return lax.dot_general(
        left, right, (((1,), (1,)), ((), ())), preferred_element_type=jnp.float32
    )


def heads_flat(values, batch, rows, width):
    return values.transpose(0, 2, 1, 3).reshape(batch * rows, width)


def shards_by_rows(frames, norm1_gain, w_qkv, w_out, norm2_gain, w_up, w_down, lengths, cotangent):
    batch = frames.shape[0]
    rows = frames.shape[1]
    width = frames.shape[2]
    factor = HEAD_DIM ** (-0.5)
    first = lax.axis_index("sq") * rows
    query_pos = first + jnp.arange(rows, dtype=jnp.int32)
    item_ends = running_ends(lengths)
    query_seg = segment_ids(query_pos, item_ends)
    frames_own = frames.reshape(batch * rows, width).astype(jnp.float32)
    hidden1, norm1_pull = jax.vjp(norm_scaled, frames_own, norm1_gain)
    hidden1_low = hidden1.astype(jnp.bfloat16)
    mixed = jnp.dot(hidden1_low, w_qkv, preferred_element_type=jnp.float32).astype(jnp.bfloat16)
    query_rows = mixed[:, :width].reshape(batch, rows, width)
    key_rows = mixed[:, width : 2 * width].reshape(batch, rows, width)
    value_rows = mixed[:, 2 * width :].reshape(batch, rows, width)
    queries = query_rows.reshape(batch, rows, HEADS, HEAD_DIM)
    keys_own = key_rows.reshape(batch, rows, HEADS, HEAD_DIM)
    values_own = value_rows.reshape(batch, rows, HEADS, HEAD_DIM)

    def forward_step(carry, pieces, start):
        key_piece, value_piece = pieces
        count = key_piece.shape[1]
        key_pos = start + jnp.arange(count, dtype=jnp.int32)
        key_seg = segment_ids(key_pos, item_ends)

        def forward_work(state):
            running_max, running_sum, accum = state
            keys_block = key_piece.reshape(batch, count, HEADS, HEAD_DIM)
            values_block = value_piece.reshape(batch, count, HEADS, HEAD_DIM)
            scores = (
                jnp.einsum(
                    "rqhd,rkhd->rhqk", queries, keys_block, preferred_element_type=jnp.float32
                )
                * factor
            )
            mask = visible(query_pos, query_seg, key_pos, key_seg)[:, None]
            scores = jnp.where(mask, scores, NEG_FILL)
            new_max = jnp.maximum(running_max, jnp.max(scores, axis=-1))
            weights = jnp.where(mask, jnp.exp(scores - new_max[..., None]), 0.0)
            decay = jnp.exp(running_max - new_max)
            new_sum = decay * running_sum + jnp.sum(weights, axis=-1)
            update = jnp.einsum(
                "rhqk,rkhd->rhqd",
                weights.astype(jnp.bfloat16),
                values_block,
                preferred_element_type=jnp.float32,
            )
            return (new_max, new_sum, decay[..., None] * accum + update)

        return lax.cond(start <= query_pos[-1], forward_work, lambda state: state, carry)

    start_state = (
        jnp.full((batch, HEADS, rows), START_MAX, jnp.float32),
        jnp.zeros((batch, HEADS, rows), jnp.float32),
        jnp.zeros((batch, HEADS, rows, HEAD_DIM), jnp.float32),
    )
    final_max, final_sum, accum = over_blocks(
        start_state,
        (
            lax.all_gather(key_rows, "sq", axis=1, tiled=True),
            lax.all_gather(value_rows, "sq", axis=1, tiled=True),
        ),
        jnp.int32(0),
        forward_step,
        512,
    )
    attended = heads_flat(accum / final_sum[..., None], batch, rows, width)
    log_total = final_max + jnp.log(final_sum)
    attended_low = attended.astype(jnp.bfloat16)
    middle = frames_own + jnp.dot(attended_low, w_out, preferred_element_type=jnp.float32)
    hidden2, norm2_pull = jax.vjp(norm_scaled, middle, norm2_gain)
    hidden2_low = hidden2.astype(jnp.bfloat16)
    upward = jnp.dot(hidden2_low, w_up, preferred_element_type=jnp.float32)
    active, gelu_pull = jax.vjp(jax.nn.gelu, upward)
    active_low = active.astype(jnp.bfloat16)
    result = middle + jnp.dot(active_low, w_down, preferred_element_type=jnp.float32)
    grad_top = cotangent.reshape(batch * rows, width).astype(jnp.float32)
    grad_branch = grad_top.astype(jnp.bfloat16)
    grad_down = contract_rows(active_low, grad_branch)
    grad_active = times_transpose(grad_branch, w_down)
    grad_upward = gelu_pull(grad_active)[0].astype(jnp.bfloat16)
    grad_up = contract_rows(hidden2_low, grad_upward)
    grad_hidden2 = times_transpose(grad_upward, w_up)
    grad_middle_part, grad_gain2 = norm2_pull(grad_hidden2)
    grad_middle = grad_top + grad_middle_part
    grad_attn = grad_middle.astype(jnp.bfloat16)
    grad_outproj = contract_rows(attended_low, grad_attn)
    grad_attended = times_transpose(grad_attn, w_out).astype(jnp.bfloat16)
    grad_rows_own = grad_attended.reshape(batch, rows, width)
    grad_heads = grad_attended.reshape(batch, rows, HEADS, HEAD_DIM)
    delta_rows = jnp.sum(
        (grad_attended.astype(jnp.float32) * attended).reshape(batch, rows, HEADS, HEAD_DIM), axis=3
    )
    delta = delta_rows.transpose(0, 2, 1)

    def query_step(carry, pieces, start):
        key_piece, value_piece = pieces
        count = key_piece.shape[1]
        key_pos = start + jnp.arange(count, dtype=jnp.int32)
        key_seg = segment_ids(key_pos, item_ends)

        def query_work(grad_query):
            keys_block = key_piece.reshape(batch, count, HEADS, HEAD_DIM)
            values_block = value_piece.reshape(batch, count, HEADS, HEAD_DIM)
            scores = (
                jnp.einsum(
                    "rqhd,rkhd->rhqk", queries, keys_block, preferred_element_type=jnp.float32
                )
                * factor
            )
            mask = visible(query_pos, query_seg, key_pos, key_seg)[:, None]
            shares = jnp.where(mask, jnp.exp(scores - log_total[..., None]), 0.0)
            grad_shares = jnp.einsum(
                "rqhd,rkhd->rhqk", grad_heads, values_block, preferred_element_type=jnp.float32
            )
            grad_scores = (shares * (grad_shares - delta[..., None])).astype(jnp.bfloat16)
            return grad_query + jnp.einsum(
                "rhqk,rkhd->rhqd", grad_scores, keys_block, preferred_element_type=jnp.float32
            )

        return lax.cond(start <= query_pos[-1], query_work, lambda state: state, carry)

    zero_query = jnp.zeros((batch, HEADS, rows, HEAD_DIM), jnp.float32)
    grad_query = over_blocks(
        zero_query,
        (
            lax.all_gather(key_rows, "sq", axis=1, tiled=True),
            lax.all_gather(value_rows, "sq", axis=1, tiled=True),
        ),
        jnp.int32(0),
        query_step,
        512,
    )

    def key_step(carry, pieces, start):
        query_piece, grad_piece, total_piece, delta_piece = pieces
        count = query_piece.shape[1]
        remote_pos = start + jnp.arange(count, dtype=jnp.int32)
        remote_seg = segment_ids(remote_pos, item_ends)

        def key_work(state):
            grad_key, grad_value = state
            remote_queries = query_piece.reshape(batch, count, HEADS, HEAD_DIM)
            remote_grads = grad_piece.reshape(batch, count, HEADS, HEAD_DIM)
            scores = (
                jnp.einsum(
                    "rqhd,rkhd->rhqk", remote_queries, keys_own, preferred_element_type=jnp.float32
                )
                * factor
            )
            mask = visible(remote_pos, remote_seg, query_pos, query_seg)[:, None]
            shares = jnp.where(
                mask, jnp.exp(scores - total_piece.transpose(0, 2, 1)[..., None]), 0.0
            )
            grad_value = grad_value + jnp.einsum(
                "rhqk,rqhd->rhkd",
                shares.astype(jnp.bfloat16),
                remote_grads,
                preferred_element_type=jnp.float32,
            )
            grad_shares = jnp.einsum(
                "rqhd,rkhd->rhqk", remote_grads, values_own, preferred_element_type=jnp.float32
            )
            grad_scores = (
                shares * (grad_shares - delta_piece.transpose(0, 2, 1)[..., None])
            ).astype(jnp.bfloat16)
            grad_key = grad_key + jnp.einsum(
                "rhqk,rqhd->rhkd", grad_scores, remote_queries, preferred_element_type=jnp.float32
            )
            return (grad_key, grad_value)

        return lax.cond(start + count - 1 >= first, key_work, lambda state: state, carry)

    grad_key, grad_value = over_blocks(
        (zero_query, zero_query),
        (
            lax.all_gather(query_rows, "sq", axis=1, tiled=True),
            lax.all_gather(grad_rows_own, "sq", axis=1, tiled=True),
            lax.all_gather(
                log_total.transpose(0, 2, 1).astype(jnp.bfloat16), "sq", axis=1, tiled=True
            ).astype(jnp.float32),
            lax.all_gather(delta_rows.astype(jnp.bfloat16), "sq", axis=1, tiled=True).astype(
                jnp.float32
            ),
        ),
        jnp.int32(0),
        key_step,
        512,
    )
    grad_mixed = jnp.concatenate(
        [
            heads_flat(grad_query * factor, batch, rows, width),
            heads_flat(grad_key * factor, batch, rows, width),
            heads_flat(grad_value, batch, rows, width),
        ],
        axis=1,
    ).astype(jnp.bfloat16)
    grad_qkv = contract_rows(hidden1_low, grad_mixed)
    grad_hidden1 = times_transpose(grad_mixed, w_qkv)
    grad_frames_part, grad_gain1 = norm1_pull(grad_hidden1)
    grad_frames = (grad_middle + grad_frames_part).reshape(batch, rows, width)
    result_rows = result.astype(jnp.bfloat16).reshape(batch, rows, width)
    shares_sq = (
        lax.psum_scatter(grad_gain1, "sq", scatter_dimension=0, tiled=True),
        lax.psum_scatter(grad_qkv, "sq", scatter_dimension=0, tiled=True),
        lax.psum_scatter(grad_outproj, "sq", scatter_dimension=0, tiled=True),
        lax.psum_scatter(grad_gain2, "sq", scatter_dimension=0, tiled=True),
        lax.psum_scatter(grad_up, "sq", scatter_dimension=0, tiled=True),
        lax.psum_scatter(grad_down, "sq", scatter_dimension=0, tiled=True),
    )
    totals = (
        lax.psum(shares_sq[0].astype(jnp.bfloat16), "dp").astype(jnp.float32),
        lax.psum(shares_sq[1].astype(jnp.bfloat16), "dp").astype(jnp.float32),
        lax.psum(shares_sq[2].astype(jnp.bfloat16), "dp").astype(jnp.float32),
        lax.psum(shares_sq[3].astype(jnp.bfloat16), "dp").astype(jnp.float32),
        lax.psum(shares_sq[4].astype(jnp.bfloat16), "dp").astype(jnp.float32),
        lax.psum(shares_sq[5].astype(jnp.bfloat16), "dp").astype(jnp.float32),
    )
    return (
        result_rows,
        grad_frames,
        totals[0],
        totals[1],
        totals[2],
        totals[3],
        totals[4],
        totals[5],
    )


MESH = pl.DeviceIdType.MESH
ZROWS = 32
ZLAG = 3
QBLOCK = 256
KEEP = pltpu.VMEM


def dot(left, right):
    return jnp.dot(left, right, preferred_element_type=jnp.float32)


def dot_nt(left, right):
    return lax.dot_general(
        left, right, (((1,), (1,)), ((), ())), preferred_element_type=jnp.float32
    )


def dot_tn(left, right):
    return lax.dot_general(
        left, right, (((0,), (0,)), ((), ())), preferred_element_type=jnp.float32
    )


def low(values):
    return values.astype(jnp.bfloat16)


def wide(values):
    return values.astype(jnp.float32)


def span(start, size):
    return pl.ds(pl.multiple_of(start, size), size)


def norm_scale(values):
    return lax.rsqrt(jnp.mean(values * values, axis=-1, keepdims=True) + EPSILON)


def norm_back(values, scale, gain, grad):
    scaled = gain * grad
    inner = jnp.mean(scaled * values, axis=-1, keepdims=True)
    part = scale * scaled - values * (scale * scale * scale) * inner
    return part, jnp.sum(grad * values * scale, axis=0, keepdims=True)


def gelu_parts(values):
    root = 0.7978845608028654
    square = values * values
    inner = jnp.tanh(root * values * (1.0 + 0.044715 * square))
    half = 0.5 * (1.0 + inner)
    slope = half + 0.5 * root * values * (1.0 - inner * inner) * (1.0 + 0.134145 * square)
    return values * half, slope


def layer_kernel(
    count, planes,
    frames_in, gain1_ref, w_qkv_in, w_out_in, gain2_ref, w_up_in, w_down_in, lengths_ref, cot_in,
    result_ref, d_in_ref, gains_ref, sum_ref,
    frames_all, hidden1_all, cot_all, hidden2_all, attn_all,
    w_heads, w_out, w_up, w_down, w_up_s, w_down_s, active_rows, slope_rows,
    mixed, q_pad, k_pad, v_pad, g_pad, shares, o_turned, o_heads, o_rows,
    middle, acc_a, acc_b, grad_mid, g_rows, g_heads,
    active_s, slope_s, up_stage, mixed_grad, mixed_stage, mixed_rows,
    own, cross_in, gain_out, gain_in, gain_z,
    load_sem, ag_send, ag_recv, swap_send, swap_recv, z_send, z_outer_recv, z_cross_recv,
):
    bf16, f32 = jnp.bfloat16, jnp.float32
    rows, width = result_ref.shape
    total = rows * count
    part = width // count
    local = part // HEAD_DIM
    ff = w_up.shape[1]
    slab = ff // count
    half = rows // 2
    factor = HEAD_DIM ** (-0.5)
    me, plane = lax.axis_index("sq"), lax.axis_index("dp")

    def flip(index, bit):
        return index + bit - 2 * bit * lax.rem(lax.div(index, bit), 2)

    mate, over_x, over_y = flip(me, 1), flip(me, 2), flip(me, 4)
    corner = flip(over_x, 4)
    inner = (plane == 1) | (plane == 2)
    outer = (plane == 0) | (plane == 3)
    z_mate = planes - 1 - plane
    z_edge = jnp.where(plane == 1, 0, planes - 1)
    z_core = jnp.where(plane == 0, 1, planes - 2)

    def remote(source, target, send, recv, to, to_plane=None):
        return pltpu.make_async_remote_copy(
            src_ref=source, dst_ref=target, send_sem=send, recv_sem=recv,
            device_id=(plane if to_plane is None else to_plane, to), device_id_type=MESH,
        )

    def others(body):
        @pl.loop(1, count)
        def _(step):
            body(lax.rem(me + step, count))

    mine = span(me * rows, rows)
    loads = [
        pltpu.make_async_copy(frames_in.at[0], frames_all.at[mine], load_sem.at[0]),
        pltpu.make_async_copy(cot_in.at[0], cot_all.at[mine], load_sem.at[1]),
    ] + [
        pltpu.make_async_copy(
            w_qkv_in.at[:, span(k * width + me * part, part)],
            w_heads.at[:, pl.ds(k * part, part)],
            load_sem.at[2 + k],
        )
        for k in range(3)
    ] + [
        pltpu.make_async_copy(w_out_in, w_out, load_sem.at[5]),
        pltpu.make_async_copy(w_up_in.at[:, span(me * slab, slab)], w_up_s, load_sem.at[6]),
        pltpu.make_async_copy(w_down_in.at[span(me * slab, slab)], w_down_s, load_sem.at[7]),
    ]

    def load_up(wait=False):
        if wait:
            pltpu.make_async_copy(w_up_in, w_up, load_sem.at[9]).wait()
            return

        @pl.loop(0, ff // part)
        def _(n):
            k, s = lax.div(n, count), lax.rem(n, count)
            pltpu.make_async_copy(
                w_up_in.at[:, span(s * slab + k * part, part)],
                w_up.at[:, span(k * width + s * part, part)], load_sem.at[9]).start()

    def load_down(wait=False):
        if wait:
            pltpu.make_async_copy(w_down_in, w_down, load_sem.at[10]).wait()
            return

        @pl.loop(0, ff // part)
        def _(n):
            k, s = lax.div(n, count), lax.rem(n, count)
            pltpu.make_async_copy(
                w_down_in.at[span(s * slab + k * part, part)],
                w_down.at[span(k * width + s * part, part)], load_sem.at[10]).start()

    load_qkv = pltpu.make_async_copy(w_qkv_in, w_up.at[:, pl.ds(0, 3 * width)], load_sem.at[8])
    for load in loads[:5]:
        load.start()

    barrier = pltpu.get_barrier_semaphore()
    others(lambda s: pl.semaphore_signal(
        barrier, inc=1, device_id=(plane, s), device_id_type=MESH))

    @pl.loop(1, planes)
    def _(step):
        pl.semaphore_signal(
            barrier, inc=1, device_id=(lax.rem(plane + step, planes), me), device_id_type=MESH)

    pl.semaphore_wait(barrier, count - 1 + planes - 1)

    def slots(index):
        return [
            (me, None, mate, mate, 0),
            (me, 0, over_x, over_x, 1), (me, 1, over_x, over_x, 2),
            (me, 1, over_y, over_y, 3), (me, 0, over_y, over_y, 4),
            (over_x, 0, over_y, corner, 5), (over_y, 1, over_x, corner, 6),
            (over_x, 0, mate, flip(mate, 2), 7), (over_x, 1, mate, flip(mate, 2), 7),
            (over_y, 1, mate, flip(mate, 4), 8), (over_y, 0, mate, flip(mate, 4), 8),
            (corner, 0, mate, flip(corner, 1), 9), (corner, 1, mate, flip(corner, 1), 9),
        ][index]

    def gather(number, array, source=None):
        def piece(block, which):
            if which is None:
                return span(block * rows, rows)
            return span(block * rows + which * half, half)

        def copy(slot, sent=True, whole=False):
            block, which, target, arrives, sem = slots(slot)
            there = piece(block if sent else arrives, None if whole else which)
            here = array.at[there]
            if sent and source is not None and slot < 5:
                here = source if which is None else source.at[pl.ds(which * half, half)]
            return remote(here, array.at[there], ag_send.at[number], ag_recv.at[number, sem], target)

        def start(*numbers):
            for slot in numbers:
                copy(slot).start()

        def wait(*numbers):
            for slot in numbers:
                copy(slot, sent=False, whole=slot >= 7).wait_recv()

        def finish():
            sent = array.at[pl.ds(0, (count - 1) * rows)]
            remote(sent, sent, ag_send.at[number], ag_recv.at[number, 0], mate).wait_send()

        return start, wait, finish

    def swap(number, pairs, whole):
        def start(target):
            for source, dest in pairs(target, me):
                remote(source, dest, swap_send.at[number], swap_recv.at[number], target).start()

        def wait():
            remote(whole, whole, swap_send.at[number], swap_recv.at[number], mate).wait_recv()

        def finish():
            remote(whole, whole, swap_send.at[number], swap_recv.at[number], mate).wait_send()

        return start, wait, finish

    f_start, f_wait, f_finish = gather(0, frames_all, frames_in.at[0])
    c_start, c_wait, c_finish = gather(1, cot_all, cot_in.at[0])
    h_start, h_wait, h_finish = gather(2, hidden2_all)
    a_start, a_wait, a_finish = gather(3, attn_all)

    def z_raw(c):
        at = span(c * ZROWS, ZROWS)
        return remote(own.at[at], sum_ref.at[at], z_send.at[0], z_outer_recv.at[c], me, z_core)

    def z_cross(c):
        at = span(c * ZROWS, ZROWS)
        return remote(own.at[at], cross_in.at[at], z_send.at[0], z_cross_recv.at[c], me, z_mate)

    def z_back(c):
        at = span(c * ZROWS, ZROWS)
        return remote(sum_ref.at[at], sum_ref.at[at], z_send.at[1], z_outer_recv.at[c], me, z_edge)

    def z_join(c):
        at = span(c * ZROWS, ZROWS)
        z_raw(c).wait_recv()
        own[at, :] = low(wide(own[at, :]) + wide(sum_ref[at, :]))
        z_cross(c).start()

    def z_close(c):
        at = span(c * ZROWS, ZROWS)
        z_cross(c).wait_recv()
        sum_ref[at, :] = low(wide(own[at, :]) + wide(cross_in[at, :]))
        z_back(c).start()

    chunks = own.shape[0] // ZROWS
    z_done = [0]

    def z_inner(number):
        first, last = z_done[0], z_done[0] + number
        z_done[0] = last

        @pl.when(inner)
        def _():
            split = min(max(first, ZLAG), last)
            for c in range(first, split):
                z_join(c)
            if last > split:
                @pl.loop(split, last)
                def _(c):
                    z_join(c)
                    z_close(c - ZLAG)

    def z_upto(number):
        if number > z_done[0]:
            z_inner(number - z_done[0])

    def z_outer(first, last):
        @pl.when(outer)
        def _():
            @pl.loop(first, last)
            def _(c):
                z_raw(c).start()

    f_start(0, 1, 3, 2, 4)
    loads[5].start()
    load_up()
    load_down()
    loads[6].start()
    loads[7].start()
    pair = 2 * rows
    lane_head = lax.broadcasted_iota(jnp.int32, (pair, part), 1) // HEAD_DIM
    gain1 = gain1_ref[...]
    gain2 = gain2_ref[...]

    def chip(index):
        return span(lax.div(index, 2) * pair, pair)

    def padded(ref, at, values):
        for head in range(local):
            ref[head, at, :] = low(jnp.where(lane_head == head, values, 0.0))

    def qkv_chip(index):
        at = chip(index)
        values = wide(frames_all[at, :])
        hidden = low(values * norm_scale(values) * gain1)
        hidden1_all[at, :] = hidden
        projected = low(dot(hidden, w_heads[...]))
        mixed[at, :] = projected
        padded(q_pad, at, wide(projected[:, :part]) * factor)
        padded(k_pad, at, wide(projected[:, part : 2 * part]))
        padded(v_pad, at, wide(projected[:, 2 * part :]))

    loads[0].wait()
    for k in range(3):
        loads[2 + k].wait()
    f_wait(0)
    qkv_chip(me)
    f_wait(1)
    f_start(5, 7)
    f_wait(3)
    f_start(6, 9)
    c_start(0, 1, 3, 2, 4)
    f_wait(2)
    f_start(8)
    f_wait(4)
    f_start(10)
    f_wait(7)
    qkv_chip(over_x)
    f_wait(9)
    qkv_chip(over_y)
    f_wait(5)
    f_start(11)
    f_wait(6)
    f_start(12)
    f_wait(11)
    qkv_chip(corner)

    ends, running = [], None
    for item in range(lengths_ref.shape[1]):
        length = lengths_ref[0, item]
        running = length if running is None else running + length
        ends.append(running)

    keys_at = pl.ds(part, part)
    values_at = pl.ds(2 * part, part)
    query_blocks = total // QBLOCK
    per_block = QBLOCK // rows

    def o_pairs(target, source):
        yield o_heads.at[span(target * rows, rows)], o_rows.at[:, span(source * part, part)]

    o_start, o_wait, o_finish = swap(0, o_pairs, o_heads.at[pl.ds(0, total - rows)])

    for i in range(query_blocks):
        at, keys = pl.ds(i * QBLOCK, QBLOCK), pl.ds(0, (i + 1) * QBLOCK)
        query_pos = i * QBLOCK + lax.broadcasted_iota(jnp.int32, (1, QBLOCK), 1)
        begin = jnp.zeros((1, QBLOCK), jnp.int32)
        for end in ends:
            begin = jnp.maximum(begin, jnp.where(query_pos >= end, end, 0))
        key_pos = lax.broadcasted_iota(jnp.int32, ((i + 1) * QBLOCK, 1), 0)
        mask = (key_pos <= query_pos) & (key_pos >= begin)
        turned = None
        for head in range(local):
            score = jnp.where(mask, dot_nt(mixed[keys, keys_at], q_pad[head, at, :]), NEG_FILL)
            weight = jnp.exp(score - jnp.max(score, axis=0, keepdims=True))
            share = low(weight * (1.0 / jnp.sum(weight, axis=0, keepdims=True)))
            shares[head, keys, at] = share
            value = dot_tn(v_pad[head, keys, :], share)
            turned = value if turned is None else turned + value
        if i == 1:
            c_wait(1)
            c_start(5, 7)
            c_wait(3)
            c_start(6, 9)
        o_turned[:, at] = turned
        o_heads[at, :] = low(turned.T)
        for k in range(per_block):
            target = i * per_block + k

            @pl.when(target != me)
            def _():
                o_start(target)

            @pl.when(target == me)
            def _():
                o_rows[:, span(me * part, part)] = o_heads[mine, :]

    c_wait(2)
    c_start(8)
    c_wait(4)
    c_start(10)
    loads[5].wait()
    o_wait()
    middle_own = wide(frames_all[mine, :]) + dot(o_rows[...], w_out[...])
    middle[...] = middle_own
    hidden2_own = low(middle_own * norm_scale(middle_own) * gain2)
    hidden2_all[mine, :] = hidden2_own

    load_up(wait=True)
    tiles = ff // width
    pieces = []
    for k in range(tiles):
        tile = pl.ds(k * width, width)
        active, slope = gelu_parts(dot(hidden2_own, w_up[:, tile]))
        active_rows[:, tile] = low(active)
        slope_rows[:, tile] = low(slope)
        if k < tiles - 1:
            def a_pairs(target, source, k=k):
                yield (
                    active_rows.at[:, span(k * width + target * part, part)],
                    active_s.at[span(source * rows, rows), pl.ds(k * part, part)],
                )

            pieces.append(swap(7 + k, a_pairs, o_heads.at[pl.ds(0, total - rows)]))
            others(pieces[k][0])
            active_s[mine, pl.ds(k * part, part)] = active_rows[:, span(k * width + me * part, part)]
        if k == tiles - 2:
            h_start(0, 1, 3, 2, 4)
    loads[1].wait()
    load_down(wait=True)
    acc_b[...] = jnp.zeros_like(acc_b)

    def back_tile(k):
        tile = span(k * width, width)
        grad = low(dot_nt(cot_all[mine, :], w_down[tile, :]) * wide(slope_rows[:, tile]))
        acc_b[...] += dot_nt(grad, w_up[:, tile])

    def down_piece(k):
        at = pl.ds(k * part, part)
        own[at, :] = low(dot_tn(active_s[:, at], cot_all[...]))
        z_outer(k * (part // ZROWS), (k + 1) * (part // ZROWS))

    back_tile(0)
    c_wait(5)
    c_start(11)
    c_wait(6)
    c_start(12)
    back_tile(1)
    c_wait(0, 7, 9, 11)
    pieces[0][1]()
    down_piece(0)
    back_tile(2)
    pieces[1][1]()
    down_piece(1)
    back_tile(3)
    load_qkv.start()
    pieces[2][1]()
    down_piece(2)
    z_upto(1)

    middle_own = middle[...]
    back2, gain2_part = norm_back(middle_own, norm_scale(middle_own), gain2, acc_b[...])
    gain_out[...] = jnp.zeros_like(gain_out)
    for s in range(count):
        gain_out[s, 1:2, :] = gain2_part[:, s * part : (s + 1) * part]
    grad_mid_own = wide(cot_all[mine, :]) + back2
    grad_mid[...] = grad_mid_own
    attn_own = low(grad_mid_own)
    attn_all[mine, :] = attn_own
    g_rows[...] = low(dot_nt(attn_own, w_out[...]))
    acc_a[...] = middle[...]
    for k in range(tiles):
        tile = pl.ds(k * width, width)
        acc_a[...] += dot(active_rows[:, tile], w_down[tile, :])
    result_ref[...] = low(acc_a[...])
    z_upto(3)

    h_wait(1)
    h_start(5, 7)
    h_wait(3)
    h_start(6, 9)

    def g_pairs(target, source):
        yield g_rows.at[:, span(target * part, part)], g_heads.at[span(source * rows, rows)]

    g_start, g_wait, g_finish = swap(1, g_pairs, g_heads.at[pl.ds(0, total - rows)])
    others(g_start)
    g_heads[mine, :] = g_rows[:, span(me * part, part)]
    loads[6].wait()
    loads[7].wait()
    for c in range(0, count, 2):
        at = span(c * rows, pair)
        slope_s[at, :] = low(dot_nt(cot_all[at, :], w_down_s[...]))
    z_upto(4)
    last_piece = pl.ds((tiles - 1) * part, part)

    def slab_chip(index):
        at = chip(index)
        active, slope = gelu_parts(dot(hidden2_all[at, :], w_up_s[...]))
        active_s[at, last_piece] = low(active[:, (tiles - 1) * part :])
        slope_s[at, :] = low(wide(slope_s[at, :]) * slope)

    h_wait(0)
    slab_chip(me)
    h_wait(2)
    h_start(8)
    h_wait(4)
    h_start(10)
    h_wait(7)
    slab_chip(over_x)
    h_wait(9)
    slab_chip(over_y)
    z_upto(6)
    h_wait(5)
    h_start(11)
    h_wait(6)
    h_start(12)
    h_wait(11)
    slab_chip(corner)
    down_piece(tiles - 1)

    up_at = slab
    mixed_at = up_at + rows * tiles
    out_at = mixed_at + rows * 3
    slabs = width // slab
    near, middle_up, far, mixed_z, out_z = (
        up_at // ZROWS, (up_at + rows) // ZROWS, (up_at + 3 * rows) // ZROWS,
        mixed_at // ZROWS, out_at // ZROWS,
    )

    def distance(one, other):
        one, other = lax.div(one, 2), lax.div(other, 2)
        return lax.rem(one + other, 2) + 2 * lax.rem(lax.div(one, 2) + lax.div(other, 2), 2)

    def u_place(target, source):
        return (span(up_at + distance(target, source) * rows, rows),
                span(lax.rem(source, slabs) * slab, slab))

    u_sems = (10, 11, 11, 12)

    def u_send(target, near_by):
        here = up_stage.at[span(target * rows, rows)]
        remote(here, own.at[u_place(target, me)], swap_send.at[2], swap_recv.at[u_sems[near_by]],
               target).start()

    def u_wait(number, blocks):
        some = up_stage.at[pl.ds(0, blocks * rows)]
        remote(some, some, swap_send.at[2], swap_recv.at[number], mate).wait_recv()

    def u_finish():
        some = up_stage.at[pl.ds(0, total - rows)]
        remote(some, some, swap_send.at[2], swap_recv.at[2], mate).wait_send()

    for near_by, index in ((1, over_x), (2, over_y), (3, corner), (0, me)):
        at = chip(index)
        up_stage[at, :] = low(dot_tn(hidden2_all[:, at], slope_s[...]))
        if near_by:
            u_send(index, near_by)
            u_send(flip(index, 1), near_by)
        else:
            u_send(mate, near_by)
            own[u_place(me, me)] = up_stage[mine, :]
    z_upto(9)
    u_wait(u_sems[0], 1)
    z_outer(near, middle_up)

    g_wait()
    for c in range(count // 2):
        at = span(c * pair, pair)
        padded(g_pad, at, wide(g_heads[at, :]))

    def late(j):
        return pl.ds(j * QBLOCK, total - j * QBLOCK)

    for j in range(query_blocks):
        keys = pl.ds(j * QBLOCK, QBLOCK)
        grad = None
        for head in range(local):
            value = dot(shares[head, keys, late(j)], g_pad[head, late(j), :])
            grad = value if grad is None else grad + value
        mixed_grad[keys, values_at] = low(grad)
    z_upto(10)
    for i in range(query_blocks):
        at, keys = pl.ds(i * QBLOCK, QBLOCK), pl.ds(0, (i + 1) * QBLOCK)
        product = wide(g_heads[at, :]).T * o_turned[:, at]
        turned = None
        for head in range(local):
            delta = jnp.sum(
                product[head * HEAD_DIM : (head + 1) * HEAD_DIM], axis=0, keepdims=True)
            grad_share = dot_nt(mixed[keys, values_at], g_pad[head, at, :])
            grad_score = low(wide(shares[head, keys, at]) * (grad_share - delta))
            shares[head, keys, at] = grad_score
            value = dot_tn(k_pad[head, keys, :], grad_score)
            turned = value if turned is None else turned + value
        mixed_grad[at, pl.ds(0, part)] = low((turned * factor).T)
        z_upto((10, 11, 12, 13)[min(i, 3)])
    for j in range(query_blocks):
        keys = pl.ds(j * QBLOCK, QBLOCK)
        grad = None
        for head in range(local):
            value = dot(shares[head, keys, late(j)], q_pad[head, late(j), :])
            grad = value if grad is None else grad + value
        mixed_grad[keys, keys_at] = low(grad)
    z_upto(15)

    def s_pairs(target, source):
        for k in range(3):
            yield (
                mixed_stage.at[span(target * rows, rows), pl.ds(k * part, part)],
                own.at[span(mixed_at + k * rows, rows), span(source * part, part)],
            )

    def m_pairs(target, source):
        for k in range(3):
            yield (
                mixed_grad.at[span(target * rows, rows), pl.ds(k * part, part)],
                mixed_rows.at[:, span(k * width + source * part, part)],
            )

    s_start, s_wait, s_finish = swap(3, s_pairs, mixed_stage.at[pl.ds(0, total - rows)])
    m_start, m_wait, m_finish = swap(4, m_pairs, mixed_grad.at[pl.ds(0, total - rows)])

    for index in (over_x, over_y, corner, me):
        at = chip(index)
        mixed_stage[at, :] = low(dot_tn(hidden1_all[:, at], mixed_grad[...]))
        if index is not me:
            s_start(index)
            s_start(flip(index, 1))
        else:
            s_start(mate)
    for k in range(3):
        own[span(mixed_at + k * rows, rows), span(me * part, part)] = (
            mixed_stage[mine, pl.ds(k * part, part)])
        mixed_rows[:, span(k * width + me * part, part)] = mixed_grad[mine, pl.ds(k * part, part)]
    a_start(0, 1, 3, 2, 4)
    z_upto(17)
    u_wait(u_sems[1], 4)
    z_outer(middle_up, far)
    z_upto(21)
    u_wait(u_sems[3], 2)
    z_outer(far, mixed_z)
    z_upto(27)
    s_wait()
    z_outer(mixed_z, out_z)

    a_wait(1)
    a_start(5, 7)
    a_wait(3)
    a_start(6, 9)
    others(m_start)
    z_upto(30)
    a_wait(2)
    a_start(8)
    a_wait(4)
    a_start(10)
    z_upto(34)
    a_wait(5)
    a_start(11)
    a_wait(6)
    a_start(12)
    z_upto(36)
    a_wait(0, 7, 9, 11)
    own[pl.ds(out_at, part), :] = low(dot(low(o_turned[...]), attn_all[...]))
    z_outer(out_z, chunks)
    z_upto(40)

    load_qkv.wait()
    m_wait()
    acc_a[...] = jnp.zeros_like(acc_a)

    @pl.loop(0, 3)
    def _(k):
        at = span(k * width, width)
        acc_a[...] += dot_nt(mixed_rows[:, at], w_up[:, at])

    frames_own = wide(frames_all[mine, :])
    back1, gain1_part = norm_back(frames_own, norm_scale(frames_own), gain1, acc_a[...])
    d_in_ref[...] = grad_mid[...] + back1

    for s in range(count):
        gain_out[s, 0:1, :] = gain1_part[:, s * part : (s + 1) * part]

    def n_pairs(target, source):
        yield gain_out.at[target], gain_in.at[source]

    n_start, n_wait, n_finish = swap(5, n_pairs, gain_out.at[pl.ds(0, count - 1)])

    def nz_copy(target, source):
        return remote(
            gain_z.at[source], gain_z.at[source], swap_send.at[6], swap_recv.at[6], me, target)

    others(n_start)
    gain_in[me] = gain_out[me]
    z_upto(44)
    n_wait()
    gain_sum = gain_in[0]
    for s in range(1, count):
        gain_sum = gain_sum + gain_in[s]
    gain_z[plane] = gain_sum

    @pl.loop(1, planes)
    def _(step):
        nz_copy(lax.rem(plane + step, planes), plane).start()

    z_upto(chunks)
    gains_all = gain_z.at[pl.ds(0, planes - 1)]
    all_gains = remote(gains_all, gains_all, swap_send.at[6], swap_recv.at[6], mate)
    all_gains.wait_recv()
    gain_sum = gain_z[0]
    for p in range(1, planes):
        gain_sum = gain_sum + gain_z[p]
    gains_ref[...] = gain_sum

    @pl.when(inner)
    def _():
        @pl.loop(chunks - ZLAG, chunks)
        def _(c):
            z_close(c)

    for finish in (
        f_finish, c_finish, h_finish, a_finish,
        o_finish, g_finish, u_finish, s_finish, m_finish, n_finish,
    ):
        finish()
    for piece in pieces:
        piece[2]()
    all_gains.wait_send()

    @pl.when(outer)
    def _():
        remote(own, own, z_send.at[0], z_outer_recv.at[0], me, z_core).wait_send()

        @pl.loop(0, chunks)
        def _(c):
            z_back(c).wait_recv()

    @pl.when(inner)
    def _():
        remote(own, own, z_send.at[0], z_outer_recv.at[0], me, z_mate).wait_send()
        remote(own, own, z_send.at[1], z_outer_recv.at[0], me, z_edge).wait_send()


def finish_kernel(
    result_in, d_in_in, gains_in, sum_in,
    result_ref, d_in_ref, gain1_ref, qkv_ref, out_ref, gain2_ref, up_ref, down_ref,
    staged, gains, sems,
):
    rows, width = result_in.shape
    slab, part = down_ref.shape[0], out_ref.shape[0]
    here = lax.div(lax.axis_index("sq"), 2)
    targets = [down_ref]
    starts = [0]
    sizes = [slab]
    for ref, tall in ((up_ref, rows), (qkv_ref, rows), (out_ref, part)):
        for k in range(ref.shape[1] // width):
            starts.append(starts[-1] + sizes[-1])
            sizes.append(tall)
            block = k
            if ref is up_ref:
                low_bit, high_bit = lax.rem(here, 2), lax.div(here, 2)
                block = lax.rem(low_bit + k, 2) + 2 * lax.rem(high_bit + k // 2, 2)
            targets.append(ref.at[:, span(block * width, width)])
    copies = [
        pltpu.make_async_copy(result_in, result_ref.at[0], sems.at[0]),
        pltpu.make_async_copy(d_in_in, d_in_ref.at[0], sems.at[1]),
    ]
    for copy in copies:
        copy.start()
    for k, (first, size, target) in enumerate(zip(starts, sizes, targets)):
        at = pl.ds(first, size)
        staged[at, :] = sum_in[at, :].astype(jnp.float32)
        copy = pltpu.make_async_copy(staged.at[at], target, sems.at[2 + k])
        copy.start()
        copies.append(copy)
    gain1_ref[...] = gains_in[0]
    gain2_ref[...] = gains_in[1]
    for copy in copies:
        copy.wait()


def shards_by_heads(frames, norm1_gain, w_qkv, w_out, norm2_gain, w_up, w_down, lengths, cotangent):
    _, rows, width = frames.shape
    ff = w_up.shape[1]
    count, planes = lax.axis_size("sq"), lax.axis_size("dp")
    total, part, slab = rows * count, width // count, ff // count
    local = part // HEAD_DIM
    bf16, f32 = jnp.bfloat16, jnp.float32
    blocks = ff // width
    own_rows = slab + rows * blocks + part + rows * 3
    chunks = own_rows // ZROWS
    vmem, anywhere = pl.BlockSpec(memory_space=pltpu.VMEM), pl.BlockSpec(memory_space=pl.ANY)
    smem = pl.BlockSpec(memory_space=pltpu.SMEM)

    def low_array(*shape):
        return pltpu.VMEM(shape, bf16)

    def wide_array(*shape):
        return pltpu.VMEM(shape, f32)

    def copies(*shape):
        return pltpu.SemaphoreType.DMA(shape)

    scratch = (
        [low_array(total, width)] * 5
        + [low_array(width, 3 * part), low_array(width, width), low_array(width, ff), low_array(ff, width)]
        + [low_array(width, slab), low_array(slab, width), low_array(rows, ff), low_array(rows, ff)]
        + [low_array(total, 3 * part)]
        + [low_array(local, total, part)] * 4
        + [low_array(local, total, total), wide_array(part, total)]
        + [low_array(total, part), low_array(rows, width)]
        + [wide_array(rows, width)] * 4
        + [low_array(rows, width), low_array(total, part)]
        + [low_array(total, slab)] * 3
        + [low_array(total, 3 * part)] * 2
        + [low_array(rows, 3 * width)]
        + [low_array(own_rows, width)] * 2
        + [wide_array(count, 8, part)] * 2
        + [wide_array(planes, 8, part)]
        + [copies(11), copies(4), copies(4, 10), copies(13), copies(13), copies(2)]
        + [copies(chunks)] * 2
    )
    kept = pl.pallas_call(
        functools.partial(layer_kernel, count, planes),
        out_shape=(
            KEEP((rows, width), bf16),
            KEEP((rows, width), f32),
            KEEP((8, part), f32),
            KEEP((own_rows, width), bf16),
        ),
        in_specs=[anywhere, vmem, anywhere, anywhere, vmem, anywhere, anywhere, smem, anywhere],
        out_specs=(vmem, vmem, vmem, vmem),
        scratch_shapes=scratch,
        compiler_params=pltpu.CompilerParams(
            collective_id=0, has_side_effects=True, vmem_limit_bytes=60 * 2**20),
    )(frames, norm1_gain[None], w_qkv, w_out, norm2_gain[None], w_up, w_down, lengths, cotangent)
    return pl.pallas_call(
        finish_kernel,
        out_shape=tuple(
            jax.ShapeDtypeStruct(shape, kind)
            for shape, kind in (
                ((1, rows, width), bf16), ((1, rows, width), f32), ((part,), f32),
                ((part, 3 * width), f32), ((part, width), f32), ((part,), f32),
                ((part, ff), f32), ((slab, width), f32),
            )
        ),
        in_specs=[vmem] * 4,
        out_specs=(anywhere, anywhere, vmem, anywhere, anywhere, vmem, anywhere, anywhere),
        scratch_shapes=[wide_array(own_rows, width), wide_array(8, part), copies(11)],
        compiler_params=pltpu.CompilerParams(vmem_limit_bytes=24 * 2**20),
    )(*kept)


def solution(mesh):
    by_heads = HEADS % mesh.shape["sq"] == 0 and dict(mesh.shape) == {"dp": 4, "sq": 8}
    return jax.shard_map(
        shards_by_heads if by_heads else shards_by_rows,
        mesh=mesh,
        in_specs=(
            P("dp", "sq", None),
            P(),
            P(),
            P(),
            P(),
            P(),
            P(),
            P("dp", None),
            P("dp", "sq", None),
        ),
        out_specs=(
            P("dp", "sq", None),
            P("dp", "sq", None),
            P("sq"),
            P("sq", None),
            P("sq", None),
            P("sq"),
            P("sq", None),
            P("sq", None),
        ),
        check_vma=False,
    )
```

```python
import functools

import jax
import jax.numpy as jnp
from jax import lax
from jax.experimental import pallas as pl
from jax.experimental.pallas import tpu as pltpu
from jax.sharding import PartitionSpec as P

HEADS = 16
HEAD_DIM = 64


EPSILON = 1e-05
NEG_FILL = -1000000000.0
START_MAX = -1e30


def norm_scaled(values, gain):
    return values * lax.rsqrt(jnp.mean(values * values, axis=-1, keepdims=True) + EPSILON) * gain


def segment_ids(positions, item_ends):
    return jnp.sum((positions[None, :, None] >= item_ends[:, None, :]).astype(jnp.int32), axis=2)


def running_ends(lengths):
    items = jnp.arange(lengths.shape[1], dtype=jnp.int32)
    before = items[None, None, :] <= items[None, :, None]
    return jnp.sum(jnp.where(before, lengths[:, None, :], 0), axis=2)


def visible(query_pos, query_seg, key_pos, key_seg):
    return (key_pos[None, None, :] <= query_pos[None, :, None]) & (
        key_seg[:, None, :] == query_seg[:, :, None]
    )


def block_size(count, limit):
    for candidate in range(min(count, limit), 0, -1):
        if count % candidate == 0:
            return candidate
    return count


def over_blocks(carry, arrays, start, step_fn, limit):
    count = arrays[0].shape[1]
    size = block_size(count, limit)
    number = count // size
    if number == 1:
        return step_fn(carry, arrays, start)
    stacked = tuple(
        (
            jnp.swapaxes(member.reshape((member.shape[0], number, size) + member.shape[2:]), 0, 1)
            for member in arrays
        )
    )

    def turn(state, item):
        offset, pieces = item
        return (step_fn(state, pieces, start + offset * size), None)

    offsets = jnp.arange(number, dtype=jnp.int32)
    return lax.scan(turn, carry, (offsets, stacked))[0]


def contract_rows(left, right):
    return lax.dot_general(
        left, right, (((0,), (0,)), ((), ())), preferred_element_type=jnp.float32
    )


def times_transpose(left, right):
    return lax.dot_general(
        left, right, (((1,), (1,)), ((), ())), preferred_element_type=jnp.float32
    )


def heads_flat(values, batch, rows, width):
    return values.transpose(0, 2, 1, 3).reshape(batch * rows, width)


def shards_by_rows(frames, norm1_gain, w_qkv, w_out, norm2_gain, w_up, w_down, lengths, cotangent):
    batch = frames.shape[0]
    rows = frames.shape[1]
    width = frames.shape[2]
    factor = HEAD_DIM ** (-0.5)
    first = lax.axis_index("sq") * rows
    query_pos = first + jnp.arange(rows, dtype=jnp.int32)
    item_ends = running_ends(lengths)
    query_seg = segment_ids(query_pos, item_ends)
    frames_own = frames.reshape(batch * rows, width).astype(jnp.float32)
    hidden1, norm1_pull = jax.vjp(norm_scaled, frames_own, norm1_gain)
    hidden1_low = hidden1.astype(jnp.bfloat16)
    mixed = jnp.dot(hidden1_low, w_qkv, preferred_element_type=jnp.float32).astype(jnp.bfloat16)
    query_rows = mixed[:, :width].reshape(batch, rows, width)
    key_rows = mixed[:, width : 2 * width].reshape(batch, rows, width)
    value_rows = mixed[:, 2 * width :].reshape(batch, rows, width)
    queries = query_rows.reshape(batch, rows, HEADS, HEAD_DIM)
    keys_own = key_rows.reshape(batch, rows, HEADS, HEAD_DIM)
    values_own = value_rows.reshape(batch, rows, HEADS, HEAD_DIM)

    def forward_step(carry, pieces, start):
        key_piece, value_piece = pieces
        count = key_piece.shape[1]
        key_pos = start + jnp.arange(count, dtype=jnp.int32)
        key_seg = segment_ids(key_pos, item_ends)

        def forward_work(state):
            running_max, running_sum, accum = state
            keys_block = key_piece.reshape(batch, count, HEADS, HEAD_DIM)
            values_block = value_piece.reshape(batch, count, HEADS, HEAD_DIM)
            scores = (
                jnp.einsum(
                    "rqhd,rkhd->rhqk", queries, keys_block, preferred_element_type=jnp.float32
                )
                * factor
            )
            mask = visible(query_pos, query_seg, key_pos, key_seg)[:, None]
            scores = jnp.where(mask, scores, NEG_FILL)
            new_max = jnp.maximum(running_max, jnp.max(scores, axis=-1))
            weights = jnp.where(mask, jnp.exp(scores - new_max[..., None]), 0.0)
            decay = jnp.exp(running_max - new_max)
            new_sum = decay * running_sum + jnp.sum(weights, axis=-1)
            update = jnp.einsum(
                "rhqk,rkhd->rhqd",
                weights.astype(jnp.bfloat16),
                values_block,
                preferred_element_type=jnp.float32,
            )
            return (new_max, new_sum, decay[..., None] * accum + update)

        return lax.cond(start <= query_pos[-1], forward_work, lambda state: state, carry)

    start_state = (
        jnp.full((batch, HEADS, rows), START_MAX, jnp.float32),
        jnp.zeros((batch, HEADS, rows), jnp.float32),
        jnp.zeros((batch, HEADS, rows, HEAD_DIM), jnp.float32),
    )
    final_max, final_sum, accum = over_blocks(
        start_state,
        (
            lax.all_gather(key_rows, "sq", axis=1, tiled=True),
            lax.all_gather(value_rows, "sq", axis=1, tiled=True),
        ),
        jnp.int32(0),
        forward_step,
        512,
    )
    attended = heads_flat(accum / final_sum[..., None], batch, rows, width)
    log_total = final_max + jnp.log(final_sum)
    attended_low = attended.astype(jnp.bfloat16)
    middle = frames_own + jnp.dot(attended_low, w_out, preferred_element_type=jnp.float32)
    hidden2, norm2_pull = jax.vjp(norm_scaled, middle, norm2_gain)
    hidden2_low = hidden2.astype(jnp.bfloat16)
    upward = jnp.dot(hidden2_low, w_up, preferred_element_type=jnp.float32)
    active, gelu_pull = jax.vjp(jax.nn.gelu, upward)
    active_low = active.astype(jnp.bfloat16)
    result = middle + jnp.dot(active_low, w_down, preferred_element_type=jnp.float32)
    grad_top = cotangent.reshape(batch * rows, width).astype(jnp.float32)
    grad_branch = grad_top.astype(jnp.bfloat16)
    grad_down = contract_rows(active_low, grad_branch)
    grad_active = times_transpose(grad_branch, w_down)
    grad_upward = gelu_pull(grad_active)[0].astype(jnp.bfloat16)
    grad_up = contract_rows(hidden2_low, grad_upward)
    grad_hidden2 = times_transpose(grad_upward, w_up)
    grad_middle_part, grad_gain2 = norm2_pull(grad_hidden2)
    grad_middle = grad_top + grad_middle_part
    grad_attn = grad_middle.astype(jnp.bfloat16)
    grad_outproj = contract_rows(attended_low, grad_attn)
    grad_attended = times_transpose(grad_attn, w_out).astype(jnp.bfloat16)
    grad_rows_own = grad_attended.reshape(batch, rows, width)
    grad_heads = grad_attended.reshape(batch, rows, HEADS, HEAD_DIM)
    delta_rows = jnp.sum(
        (grad_attended.astype(jnp.float32) * attended).reshape(batch, rows, HEADS, HEAD_DIM), axis=3
    )
    delta = delta_rows.transpose(0, 2, 1)

    def query_step(carry, pieces, start):
        key_piece, value_piece = pieces
        count = key_piece.shape[1]
        key_pos = start + jnp.arange(count, dtype=jnp.int32)
        key_seg = segment_ids(key_pos, item_ends)

        def query_work(grad_query):
            keys_block = key_piece.reshape(batch, count, HEADS, HEAD_DIM)
            values_block = value_piece.reshape(batch, count, HEADS, HEAD_DIM)
            scores = (
                jnp.einsum(
                    "rqhd,rkhd->rhqk", queries, keys_block, preferred_element_type=jnp.float32
                )
                * factor
            )
            mask = visible(query_pos, query_seg, key_pos, key_seg)[:, None]
            shares = jnp.where(mask, jnp.exp(scores - log_total[..., None]), 0.0)
            grad_shares = jnp.einsum(
                "rqhd,rkhd->rhqk", grad_heads, values_block, preferred_element_type=jnp.float32
            )
            grad_scores = (shares * (grad_shares - delta[..., None])).astype(jnp.bfloat16)
            return grad_query + jnp.einsum(
                "rhqk,rkhd->rhqd", grad_scores, keys_block, preferred_element_type=jnp.float32
            )

        return lax.cond(start <= query_pos[-1], query_work, lambda state: state, carry)

    zero_query = jnp.zeros((batch, HEADS, rows, HEAD_DIM), jnp.float32)
    grad_query = over_blocks(
        zero_query,
        (
            lax.all_gather(key_rows, "sq", axis=1, tiled=True),
            lax.all_gather(value_rows, "sq", axis=1, tiled=True),
        ),
        jnp.int32(0),
        query_step,
        512,
    )

    def key_step(carry, pieces, start):
        query_piece, grad_piece, total_piece, delta_piece = pieces
        count = query_piece.shape[1]
        remote_pos = start + jnp.arange(count, dtype=jnp.int32)
        remote_seg = segment_ids(remote_pos, item_ends)

        def key_work(state):
            grad_key, grad_value = state
            remote_queries = query_piece.reshape(batch, count, HEADS, HEAD_DIM)
            remote_grads = grad_piece.reshape(batch, count, HEADS, HEAD_DIM)
            scores = (
                jnp.einsum(
                    "rqhd,rkhd->rhqk", remote_queries, keys_own, preferred_element_type=jnp.float32
                )
                * factor
            )
            mask = visible(remote_pos, remote_seg, query_pos, query_seg)[:, None]
            shares = jnp.where(
                mask, jnp.exp(scores - total_piece.transpose(0, 2, 1)[..., None]), 0.0
            )
            grad_value = grad_value + jnp.einsum(
                "rhqk,rqhd->rhkd",
                shares.astype(jnp.bfloat16),
                remote_grads,
                preferred_element_type=jnp.float32,
            )
            grad_shares = jnp.einsum(
                "rqhd,rkhd->rhqk", remote_grads, values_own, preferred_element_type=jnp.float32
            )
            grad_scores = (
                shares * (grad_shares - delta_piece.transpose(0, 2, 1)[..., None])
            ).astype(jnp.bfloat16)
            grad_key = grad_key + jnp.einsum(
                "rhqk,rqhd->rhkd", grad_scores, remote_queries, preferred_element_type=jnp.float32
            )
            return (grad_key, grad_value)

        return lax.cond(start + count - 1 >= first, key_work, lambda state: state, carry)

    grad_key, grad_value = over_blocks(
        (zero_query, zero_query),
        (
            lax.all_gather(query_rows, "sq", axis=1, tiled=True),
            lax.all_gather(grad_rows_own, "sq", axis=1, tiled=True),
            lax.all_gather(
                log_total.transpose(0, 2, 1).astype(jnp.bfloat16), "sq", axis=1, tiled=True
            ).astype(jnp.float32),
            lax.all_gather(delta_rows.astype(jnp.bfloat16), "sq", axis=1, tiled=True).astype(
                jnp.float32
            ),
        ),
        jnp.int32(0),
        key_step,
        512,
    )
    grad_mixed = jnp.concatenate(
        [
            heads_flat(grad_query * factor, batch, rows, width),
            heads_flat(grad_key * factor, batch, rows, width),
            heads_flat(grad_value, batch, rows, width),
        ],
        axis=1,
    ).astype(jnp.bfloat16)
    grad_qkv = contract_rows(hidden1_low, grad_mixed)
    grad_hidden1 = times_transpose(grad_mixed, w_qkv)
    grad_frames_part, grad_gain1 = norm1_pull(grad_hidden1)
    grad_frames = (grad_middle + grad_frames_part).reshape(batch, rows, width)
    result_rows = result.astype(jnp.bfloat16).reshape(batch, rows, width)
    shares_sq = (
        lax.psum_scatter(grad_gain1, "sq", scatter_dimension=0, tiled=True),
        lax.psum_scatter(grad_qkv, "sq", scatter_dimension=0, tiled=True),
        lax.psum_scatter(grad_outproj, "sq", scatter_dimension=0, tiled=True),
        lax.psum_scatter(grad_gain2, "sq", scatter_dimension=0, tiled=True),
        lax.psum_scatter(grad_up, "sq", scatter_dimension=0, tiled=True),
        lax.psum_scatter(grad_down, "sq", scatter_dimension=0, tiled=True),
    )
    totals = (
        lax.psum(shares_sq[0].astype(jnp.bfloat16), "dp").astype(jnp.float32),
        lax.psum(shares_sq[1].astype(jnp.bfloat16), "dp").astype(jnp.float32),
        lax.psum(shares_sq[2].astype(jnp.bfloat16), "dp").astype(jnp.float32),
        lax.psum(shares_sq[3].astype(jnp.bfloat16), "dp").astype(jnp.float32),
        lax.psum(shares_sq[4].astype(jnp.bfloat16), "dp").astype(jnp.float32),
        lax.psum(shares_sq[5].astype(jnp.bfloat16), "dp").astype(jnp.float32),
    )
    return (
        result_rows,
        grad_frames,
        totals[0],
        totals[1],
        totals[2],
        totals[3],
        totals[4],
        totals[5],
    )


MESH = pl.DeviceIdType.MESH
UNIT = 32
QBLOCK = 256
KEEP = pltpu.VMEM


def dot(left, right):
    return jnp.dot(left, right, preferred_element_type=jnp.float32)


def dot_nt(left, right):
    return lax.dot_general(
        left, right, (((1,), (1,)), ((), ())), preferred_element_type=jnp.float32
    )


def dot_tn(left, right):
    return lax.dot_general(
        left, right, (((0,), (0,)), ((), ())), preferred_element_type=jnp.float32
    )


def low(values):
    return values.astype(jnp.bfloat16)


def wide(values):
    return values.astype(jnp.float32)


def span(start, size):
    return pl.ds(pl.multiple_of(start, size), size)


def chain_table(count):
    sizes = [UNIT] * (count // UNIT)
    starts = [sum(sizes[:k]) for k in range(len(sizes))]
    return list(zip(starts, sizes))


def norm_scale(values):
    return lax.rsqrt(jnp.mean(values * values, axis=-1, keepdims=True) + EPSILON)


def norm_back(values, scale, gain, grad):
    scaled = gain * grad
    inner = jnp.mean(scaled * values, axis=-1, keepdims=True)
    part = scale * scaled - values * (scale * scale * scale) * inner
    return part, jnp.sum(grad * values * scale, axis=0, keepdims=True)


def gelu_parts(values):
    root = 0.7978845608028654
    square = values * values
    inner = jnp.tanh(root * values * (1.0 + 0.044715 * square))
    half = 0.5 * (1.0 + inner)
    slope = half + 0.5 * root * values * (1.0 - inner * inner) * (1.0 + 0.134145 * square)
    return values * half, slope


def layer_kernel(
    count, planes,
    frames_in, gain1_ref, w_qkv_in, w_out_in, gain2_ref, w_up_in, w_down_in, lengths_ref, cot_in,
    result_ref, d_in_ref, gains_ref, sum_ref,
    frames_all, hidden1_all, cot_all, hidden2_all, attn_all,
    w_heads, w_out, w_up, w_down, w_up_s, w_down_s, active_rows, slope_rows,
    mixed, q_pad, k_pad, v_pad, g_pad, shares, o_turned, o_heads, o_rows,
    middle, acc_a, acc_b, grad_mid, g_rows, g_heads,
    active_s, slope_s, up_stage, mixed_grad, mixed_stage, mixed_rows,
    own, cross_in, gain_out, gain_in, gain_z,
    load_sem, ag_send, ag_recv, swap_send, swap_recv, z_send, z_outer_recv, z_cross_recv,
):
    bf16, f32 = jnp.bfloat16, jnp.float32
    rows, width = result_ref.shape
    total = rows * count
    part = width // count
    local = part // HEAD_DIM
    ff = w_up.shape[1]
    slab = ff // count
    half = rows // 2
    factor = HEAD_DIM ** (-0.5)
    me, plane = lax.axis_index("sq"), lax.axis_index("dp")

    def flip(index, bit):
        return index + bit - 2 * bit * lax.rem(lax.div(index, bit), 2)

    mate, over_x, over_y = flip(me, 1), flip(me, 2), flip(me, 4)
    corner = flip(over_x, 4)
    inner = (plane == 1) | (plane == 2)
    outer = (plane == 0) | (plane == 3)
    z_mate = planes - 1 - plane
    z_edge = jnp.where(plane == 1, 0, planes - 1)
    z_core = jnp.where(plane == 0, 1, planes - 2)

    def remote(source, target, send, recv, to, to_plane=None):
        return pltpu.make_async_remote_copy(
            src_ref=source, dst_ref=target, send_sem=send, recv_sem=recv,
            device_id=(plane if to_plane is None else to_plane, to), device_id_type=MESH,
        )

    def others(body):
        @pl.loop(1, count)
        def _(step):
            body(lax.rem(me + step, count))

    mine = span(me * rows, rows)
    loads = [
        pltpu.make_async_copy(frames_in.at[0], frames_all.at[mine], load_sem.at[0]),
        pltpu.make_async_copy(cot_in.at[0], cot_all.at[mine], load_sem.at[1]),
    ] + [
        pltpu.make_async_copy(
            w_qkv_in.at[:, span(k * width + me * part, part)],
            w_heads.at[:, pl.ds(k * part, part)],
            load_sem.at[2 + k],
        )
        for k in range(3)
    ] + [
        pltpu.make_async_copy(w_out_in, w_out, load_sem.at[5]),
        pltpu.make_async_copy(w_up_in.at[:, span(me * slab, slab)], w_up_s, load_sem.at[6]),
        pltpu.make_async_copy(w_down_in.at[span(me * slab, slab)], w_down_s, load_sem.at[7]),
    ]

    def load_up(wait=False):
        if wait:
            pltpu.make_async_copy(w_up_in, w_up, load_sem.at[9]).wait()
            return

        @pl.loop(0, ff // part)
        def _(n):
            k, s = lax.div(n, count), lax.rem(n, count)
            pltpu.make_async_copy(
                w_up_in.at[:, span(s * slab + k * part, part)],
                w_up.at[:, span(k * width + s * part, part)], load_sem.at[9]).start()

    def load_down(wait=False):
        if wait:
            pltpu.make_async_copy(w_down_in, w_down, load_sem.at[10]).wait()
            return

        @pl.loop(0, ff // part)
        def _(n):
            k, s = lax.div(n, count), lax.rem(n, count)
            pltpu.make_async_copy(
                w_down_in.at[span(s * slab + k * part, part)],
                w_down.at[span(k * width + s * part, part)], load_sem.at[10]).start()

    load_qkv = pltpu.make_async_copy(w_qkv_in, w_up.at[:, pl.ds(0, 3 * width)], load_sem.at[8])
    for load in loads[:5]:
        load.start()

    barrier = pltpu.get_barrier_semaphore()
    others(lambda s: pl.semaphore_signal(
        barrier, inc=1, device_id=(plane, s), device_id_type=MESH))

    @pl.loop(1, planes)
    def _(step):
        pl.semaphore_signal(
            barrier, inc=1, device_id=(lax.rem(plane + step, planes), me), device_id_type=MESH)

    pl.semaphore_wait(barrier, count - 1 + planes - 1)

    def slots(index):
        return [
            (me, None, mate, mate, 0),
            (me, 0, over_x, over_x, 1), (me, 1, over_x, over_x, 2),
            (me, 1, over_y, over_y, 3), (me, 0, over_y, over_y, 4),
            (over_x, 0, over_y, corner, 5), (over_y, 1, over_x, corner, 6),
            (over_x, 0, mate, flip(mate, 2), 7), (over_x, 1, mate, flip(mate, 2), 7),
            (over_y, 1, mate, flip(mate, 4), 8), (over_y, 0, mate, flip(mate, 4), 8),
            (corner, 0, mate, flip(corner, 1), 9), (corner, 1, mate, flip(corner, 1), 9),
        ][index]

    def gather(number, array, source=None):
        def piece(block, which):
            if which is None:
                return span(block * rows, rows)
            return span(block * rows + which * half, half)

        def copy(slot, sent=True, whole=False):
            block, which, target, arrives, sem = slots(slot)
            there = piece(block if sent else arrives, None if whole else which)
            here = array.at[there]
            if sent and source is not None and slot < 5:
                here = source if which is None else source.at[pl.ds(which * half, half)]
            return remote(here, array.at[there], ag_send.at[number], ag_recv.at[number, sem], target)

        def start(*numbers):
            for slot in numbers:
                copy(slot).start()

        def wait(*numbers):
            for slot in numbers:
                copy(slot, sent=False, whole=slot >= 7).wait_recv()

        def finish():
            sent = array.at[pl.ds(0, (count - 1) * rows)]
            remote(sent, sent, ag_send.at[number], ag_recv.at[number, 0], mate).wait_send()

        return start, wait, finish

    def swap(number, pairs, whole):
        def start(target):
            for source, dest in pairs(target, me):
                remote(source, dest, swap_send.at[number], swap_recv.at[number], target).start()

        def wait():
            remote(whole, whole, swap_send.at[number], swap_recv.at[number], mate).wait_recv()

        def finish():
            remote(whole, whole, swap_send.at[number], swap_recv.at[number], mate).wait_send()

        return start, wait, finish

    f_start, f_wait, f_finish = gather(0, frames_all, frames_in.at[0])
    c_start, c_wait, c_finish = gather(1, cot_all, cot_in.at[0])
    h_start, h_wait, h_finish = gather(2, hidden2_all)
    a_start, a_wait, a_finish = gather(3, attn_all)

    table = chain_table(own.shape[0])

    def z_raw(c):
        at = pl.ds(*table[c])
        return remote(own.at[at], sum_ref.at[at], z_send.at[0], z_outer_recv.at[c], me, z_core)

    def z_cross(c):
        at = pl.ds(*table[c])
        return remote(own.at[at], cross_in.at[at], z_send.at[0], z_cross_recv.at[c], me, z_mate)

    def z_back(c):
        at = pl.ds(*table[c])
        return remote(sum_ref.at[at], sum_ref.at[at], z_send.at[1], z_outer_recv.at[c], me, z_edge)

    def z_join(c):
        at = pl.ds(*table[c])
        z_raw(c).wait_recv()
        own[at, :] = low(wide(own[at, :]) + wide(sum_ref[at, :]))
        z_cross(c).start()

    def z_close(c):
        at = pl.ds(*table[c])
        z_cross(c).wait_recv()
        sum_ref[at, :] = low(wide(own[at, :]) + wide(cross_in[at, :]))
        z_back(c).start()

    z_joined, z_closed = [0], [0]

    def z_upto(units):
        todo = []
        while z_joined[0] < len(table) and sum(table[z_joined[0]]) <= units * UNIT:
            todo.append((z_join, z_joined[0]))
            end = sum(table[z_joined[0]])
            z_joined[0] += 1
            while sum(table[z_closed[0]]) + 3 * UNIT <= end:
                todo.append((z_close, z_closed[0]))
                z_closed[0] += 1
        if todo:
            @pl.when(inner)
            def _():
                for step, c in todo:
                    step(c)

    def z_outer(first, last):
        @pl.when(outer)
        def _():
            for c, (start, size) in enumerate(table):
                if first <= start < last:
                    z_raw(c).start()

    f_start(0, 1, 3, 2, 4)
    loads[5].start()
    load_up()
    load_down()
    loads[6].start()
    loads[7].start()
    pair = 2 * rows
    lane_head = lax.broadcasted_iota(jnp.int32, (pair, part), 1) // HEAD_DIM
    gain1 = gain1_ref[...]
    gain2 = gain2_ref[...]

    def chip(index):
        return span(lax.div(index, 2) * pair, pair)

    def padded(ref, at, values):
        for head in range(local):
            on = lane_head[: values.shape[0]] == head
            ref[head, at, :] = low(jnp.where(on, values, 0.0))

    def qkv_chip(index):
        qkv_rows(chip(index), pair)

    def qkv_rows(at, _):
        values = wide(frames_all[at, :])
        hidden = low(values * norm_scale(values) * gain1)
        hidden1_all[at, :] = hidden
        projected = low(dot(hidden, w_heads[...]))
        mixed[at, :] = projected
        padded(q_pad, at, wide(projected[:, :part]) * factor)
        padded(k_pad, at, wide(projected[:, part : 2 * part]))
        padded(v_pad, at, wide(projected[:, 2 * part :]))

    loads[0].wait()
    for k in range(3):
        loads[2 + k].wait()
    f_wait(0)
    qkv_chip(me)
    f_wait(1)
    f_start(5, 7)
    f_wait(3)
    f_start(6, 9)
    c_start(0, 1, 3, 2, 4)
    f_wait(2)
    f_start(8)
    f_wait(4)
    f_start(10)
    f_wait(7)
    qkv_chip(over_x)
    f_wait(9)
    qkv_chip(over_y)
    f_wait(5)
    f_start(11)
    f_wait(6)
    f_start(12)
    qkv_rows(span(corner * rows, rows), rows)
    f_wait(11)
    qkv_rows(span(flip(corner, 1) * rows, rows), rows)

    ends, running = [], None
    for item in range(lengths_ref.shape[1]):
        length = lengths_ref[0, item]
        running = length if running is None else running + length
        ends.append(running)

    keys_at = pl.ds(part, part)
    values_at = pl.ds(2 * part, part)
    query_blocks = total // QBLOCK
    per_block = QBLOCK // rows

    def o_pairs(target, source):
        yield o_heads.at[span(target * rows, rows)], o_rows.at[:, span(source * part, part)]

    o_start, o_wait, o_finish = swap(0, o_pairs, o_heads.at[pl.ds(0, total - rows)])

    for i in range(query_blocks):
        at, keys = pl.ds(i * QBLOCK, QBLOCK), pl.ds(0, (i + 1) * QBLOCK)
        query_pos = i * QBLOCK + lax.broadcasted_iota(jnp.int32, (1, QBLOCK), 1)
        begin = jnp.zeros((1, QBLOCK), jnp.int32)
        for end in ends:
            begin = jnp.maximum(begin, jnp.where(query_pos >= end, end, 0))
        key_pos = lax.broadcasted_iota(jnp.int32, ((i + 1) * QBLOCK, 1), 0)
        mask = (key_pos <= query_pos) & (key_pos >= begin)
        turned = None
        for head in range(local):
            score = jnp.where(mask, dot_nt(mixed[keys, keys_at], q_pad[head, at, :]), NEG_FILL)
            weight = jnp.exp(score - jnp.max(score, axis=0, keepdims=True))
            share = low(weight * (1.0 / jnp.sum(weight, axis=0, keepdims=True)))
            shares[head, keys, at] = share
            value = dot_tn(v_pad[head, keys, :], share)
            turned = value if turned is None else turned + value
        if i == 1:
            c_wait(1)
            c_start(5, 7)
            c_wait(3)
            c_start(6, 9)
        o_turned[:, at] = turned
        o_heads[at, :] = low(turned.T)
        for k in range(per_block):
            target = i * per_block + k

            @pl.when(target != me)
            def _():
                o_start(target)

            @pl.when(target == me)
            def _():
                o_rows[:, span(me * part, part)] = o_heads[mine, :]

    c_wait(2)
    c_start(8)
    c_wait(4)
    c_start(10)
    loads[5].wait()
    o_wait()
    middle_own = wide(frames_all[mine, :]) + dot(o_rows[...], w_out[...])
    middle[...] = middle_own
    hidden2_own = low(middle_own * norm_scale(middle_own) * gain2)
    hidden2_all[mine, :] = hidden2_own

    load_up(wait=True)
    tiles = ff // width
    pieces = []
    for k in range(tiles):
        tile = pl.ds(k * width, width)
        active, slope = gelu_parts(dot(hidden2_own, w_up[:, tile]))
        active_rows[:, tile] = low(active)
        slope_rows[:, tile] = low(slope)
        if k < tiles - 1:
            def a_pairs(target, source, k=k):
                yield (
                    active_rows.at[:, span(k * width + target * part, part)],
                    active_s.at[span(source * rows, rows), pl.ds(k * part, part)],
                )

            pieces.append(swap(7 + k, a_pairs, o_heads.at[pl.ds(0, total - rows)]))
            others(pieces[k][0])
            active_s[mine, pl.ds(k * part, part)] = active_rows[:, span(k * width + me * part, part)]
        if k == tiles - 2:
            h_start(0, 1, 3, 2, 4)
    loads[1].wait()
    load_down(wait=True)
    acc_b[...] = jnp.zeros_like(acc_b)

    def back_tile(k):
        tile = span(k * width, width)
        grad = low(dot_nt(cot_all[mine, :], w_down[tile, :]) * wide(slope_rows[:, tile]))
        acc_b[...] += dot_nt(grad, w_up[:, tile])

    def down_piece(k):
        at = pl.ds(k * part, part)
        own[at, :] = low(dot_tn(active_s[:, at], cot_all[...]))
        z_outer(k * part, (k + 1) * part)

    def out_tile(k):
        tile = pl.ds(k * width, width)
        acc_a[...] += dot(active_rows[:, tile], w_down[tile, :])

    acc_a[...] = middle_own
    back_tile(0)
    c_wait(5)
    c_start(11)
    c_wait(6)
    c_start(12)
    for k in range(tiles - 1):
        out_tile(k)
    c_wait(0, 7, 9, 11)
    pieces[0][1]()
    down_piece(0)
    back_tile(1)
    pieces[1][1]()
    down_piece(1)
    back_tile(2)
    z_upto(1)
    pieces[2][1]()
    down_piece(2)
    z_upto(2)
    back_tile(3)
    load_qkv.start()
    z_upto(4)

    middle_own = middle[...]
    back2, gain2_part = norm_back(middle_own, norm_scale(middle_own), gain2, acc_b[...])
    gain_out[...] = jnp.zeros_like(gain_out)
    for s in range(count):
        gain_out[s, 1:2, :] = gain2_part[:, s * part : (s + 1) * part]
    grad_mid_own = wide(cot_all[mine, :]) + back2
    grad_mid[...] = grad_mid_own
    attn_own = low(grad_mid_own)
    attn_all[mine, :] = attn_own
    g_rows[...] = low(dot_nt(attn_own, w_out[...]))
    out_tile(tiles - 1)
    result_ref[...] = low(acc_a[...])
    z_upto(5)

    h_wait(1)
    h_start(5, 7)
    h_wait(3)
    h_start(6, 9)

    def g_pairs(target, source):
        yield g_rows.at[:, span(target * part, part)], g_heads.at[span(source * rows, rows)]

    g_start, g_wait, g_finish = swap(1, g_pairs, g_heads.at[pl.ds(0, total - rows)])
    others(g_start)
    g_heads[mine, :] = g_rows[:, span(me * part, part)]
    loads[6].wait()
    loads[7].wait()
    for c in range(0, count, 2):
        at = span(c * rows, pair)
        slope_s[at, :] = low(dot_nt(cot_all[at, :], w_down_s[...]))
    z_upto(7)
    last_piece = pl.ds((tiles - 1) * part, part)

    def slab_chip(index):
        at = chip(index)
        active, slope = gelu_parts(dot(hidden2_all[at, :], w_up_s[...]))
        active_s[at, last_piece] = low(active[:, (tiles - 1) * part :])
        slope_s[at, :] = low(wide(slope_s[at, :]) * slope)

    h_wait(0)
    slab_chip(me)
    h_wait(2)
    h_start(8)
    h_wait(4)
    h_start(10)
    h_wait(7)
    slab_chip(over_x)
    h_wait(9)
    slab_chip(over_y)
    z_upto(9)
    h_wait(5)
    h_start(11)
    h_wait(6)
    h_start(12)
    z_upto(10)
    h_wait(11)
    slab_chip(corner)
    down_piece(tiles - 1)
    z_upto(11)

    up_at = slab
    mixed_at = up_at + rows * tiles
    out_at = mixed_at + rows * 3
    slabs = width // slab

    def distance(one, other):
        one, other = lax.div(one, 2), lax.div(other, 2)
        return lax.rem(one + other, 2) + 2 * lax.rem(lax.div(one, 2) + lax.div(other, 2), 2)

    def u_place(target, source):
        return (span(up_at + distance(target, source) * rows, rows),
                span(lax.rem(source, slabs) * slab, slab))

    u_sems = (10, 11, 11, 12)

    def u_send(target, near_by):
        here = up_stage.at[span(target * rows, rows)]
        remote(here, own.at[u_place(target, me)], swap_send.at[2], swap_recv.at[u_sems[near_by]],
               target).start()

    def u_wait(number, blocks):
        some = up_stage.at[pl.ds(0, blocks * rows)]
        remote(some, some, swap_send.at[2], swap_recv.at[number], mate).wait_recv()

    def u_finish():
        some = up_stage.at[pl.ds(0, total - rows)]
        remote(some, some, swap_send.at[2], swap_recv.at[2], mate).wait_send()

    for near_by, index in ((1, over_x), (2, over_y), (3, corner), (0, me)):
        at = chip(index)
        up_stage[at, :] = low(dot_tn(hidden2_all[:, at], slope_s[...]))
        if near_by:
            u_send(index, near_by)
            u_send(flip(index, 1), near_by)
        else:
            u_send(mate, near_by)
            own[u_place(me, me)] = up_stage[mine, :]
        if near_by in (2, 0):
            z_upto(12 if near_by else 13)
    u_wait(u_sems[0], 1)
    z_outer(up_at, up_at + rows)

    g_wait()
    for c in range(count // 2):
        at = span(c * pair, pair)
        padded(g_pad, at, wide(g_heads[at, :]))

    def late(j):
        return pl.ds(j * QBLOCK, total - j * QBLOCK)

    for j in range(query_blocks):
        keys = pl.ds(j * QBLOCK, QBLOCK)
        grad = None
        for head in range(local):
            value = dot(shares[head, keys, late(j)], g_pad[head, late(j), :])
            grad = value if grad is None else grad + value
        mixed_grad[keys, values_at] = low(grad)
    z_upto(14)
    for i in range(query_blocks):
        at, keys = pl.ds(i * QBLOCK, QBLOCK), pl.ds(0, (i + 1) * QBLOCK)
        product = wide(g_heads[at, :]).T * o_turned[:, at]
        turned = None
        for head in range(local):
            delta = jnp.sum(
                product[head * HEAD_DIM : (head + 1) * HEAD_DIM], axis=0, keepdims=True)
            grad_share = dot_nt(mixed[keys, values_at], g_pad[head, at, :])
            grad_score = low(wide(shares[head, keys, at]) * (grad_share - delta))
            shares[head, keys, at] = grad_score
            value = dot_tn(k_pad[head, keys, :], grad_score)
            turned = value if turned is None else turned + value
        mixed_grad[at, pl.ds(0, part)] = low((turned * factor).T)
        z_upto(14 + i // 2 if i < query_blocks - 1 else 16)
    for j in range(query_blocks):
        keys = pl.ds(j * QBLOCK, QBLOCK)
        grad = None
        for head in range(local):
            value = dot(shares[head, keys, late(j)], q_pad[head, late(j), :])
            grad = value if grad is None else grad + value
        mixed_grad[keys, keys_at] = low(grad)
    z_upto(17)

    def s_pairs(target, source):
        for k in range(3):
            yield (
                mixed_stage.at[span(target * rows, rows), pl.ds(k * part, part)],
                own.at[span(mixed_at + k * rows, rows), span(source * part, part)],
            )

    def m_pairs(target, source):
        for k in range(3):
            yield (
                mixed_grad.at[span(target * rows, rows), pl.ds(k * part, part)],
                mixed_rows.at[:, span(k * width + source * part, part)],
            )

    s_start, s_wait, s_finish = swap(3, s_pairs, mixed_stage.at[pl.ds(0, total - rows)])
    m_start, m_wait, m_finish = swap(4, m_pairs, mixed_grad.at[pl.ds(0, total - rows)])

    for index in (over_x, over_y, corner, me):
        at = chip(index)
        mixed_stage[at, :] = low(dot_tn(hidden1_all[:, at], mixed_grad[...]))
        if index is not me:
            s_start(index)
            s_start(flip(index, 1))
        else:
            s_start(mate)
    for k in range(3):
        own[span(mixed_at + k * rows, rows), span(me * part, part)] = (
            mixed_stage[mine, pl.ds(k * part, part)])
        mixed_rows[:, span(k * width + me * part, part)] = mixed_grad[mine, pl.ds(k * part, part)]
    a_start(0, 1, 3, 2, 4)
    z_upto(19)
    u_wait(u_sems[1], 4)
    z_outer(up_at + rows, up_at + 3 * rows)
    z_upto(26)
    u_wait(u_sems[3], 2)
    z_outer(up_at + 3 * rows, mixed_at)
    z_upto(31)
    s_wait()
    z_outer(mixed_at, out_at)

    z_upto(33)

    a_wait(1)
    a_start(5, 7)
    a_wait(3)
    a_start(6, 9)
    others(m_start)
    z_upto(35)
    a_wait(2)
    a_start(8)
    a_wait(4)
    a_start(10)
    z_upto(38)
    a_wait(5)
    a_start(11)
    a_wait(6)
    a_start(12)
    z_upto(39)
    a_wait(0, 7, 9, 11)
    own[pl.ds(out_at, part), :] = low(dot(low(o_turned[...]), attn_all[...]))
    z_outer(out_at, own.shape[0])
    z_upto(43)

    load_qkv.wait()
    m_wait()
    acc_a[...] = jnp.zeros_like(acc_a)
    for k in range(3):
        @pl.loop(k, k + 1)
        def _(k):
            at = span(k * width, width)
            acc_a[...] += dot_nt(mixed_rows[:, at], w_up[:, at])

        z_upto(44 + k // 2)

    frames_own = wide(frames_all[mine, :])
    back1, gain1_part = norm_back(frames_own, norm_scale(frames_own), gain1, acc_a[...])
    d_in_ref[...] = grad_mid[...] + back1

    for s in range(count):
        gain_out[s, 0:1, :] = gain1_part[:, s * part : (s + 1) * part]

    def n_pairs(target, source):
        yield gain_out.at[target], gain_in.at[source]

    n_start, n_wait, n_finish = swap(5, n_pairs, gain_out.at[pl.ds(0, count - 1)])

    def nz_copy(target, source):
        return remote(
            gain_z.at[source], gain_z.at[source], swap_send.at[6], swap_recv.at[6], me, target)

    others(n_start)
    gain_in[me] = gain_out[me]
    z_upto(46)
    n_wait()
    gain_sum = gain_in[0]
    for s in range(1, count):
        gain_sum = gain_sum + gain_in[s]
    gain_z[plane] = gain_sum

    @pl.loop(1, planes)
    def _(step):
        nz_copy(lax.rem(plane + step, planes), plane).start()

    z_upto(own.shape[0] // UNIT)
    gains_all = gain_z.at[pl.ds(0, planes - 1)]
    all_gains = remote(gains_all, gains_all, swap_send.at[6], swap_recv.at[6], mate)
    all_gains.wait_recv()
    gain_sum = gain_z[0]
    for p in range(1, planes):
        gain_sum = gain_sum + gain_z[p]
    gains_ref[...] = gain_sum

    @pl.when(inner)
    def _():
        for c in range(z_closed[0], len(table)):
            z_close(c)

    for finish in (
        f_finish, c_finish, h_finish, a_finish,
        o_finish, g_finish, u_finish, s_finish, m_finish, n_finish,
    ):
        finish()
    for piece in pieces:
        piece[2]()
    all_gains.wait_send()

    @pl.when(outer)
    def _():
        remote(own, own, z_send.at[0], z_outer_recv.at[0], me, z_core).wait_send()

        for c in range(len(table)):
            z_back(c).wait_recv()

    @pl.when(inner)
    def _():
        remote(own, own, z_send.at[0], z_outer_recv.at[0], me, z_mate).wait_send()
        remote(own, own, z_send.at[1], z_outer_recv.at[0], me, z_edge).wait_send()


def finish_kernel(
    result_in, d_in_in, gains_in, sum_in,
    result_ref, d_in_ref, gain1_ref, qkv_ref, out_ref, gain2_ref, up_ref, down_ref,
    staged, gains, sems,
):
    rows, width = result_in.shape
    slab, part = down_ref.shape[0], out_ref.shape[0]
    here = lax.div(lax.axis_index("sq"), 2)
    starts = list(range(0, slab, part))
    sizes = [part] * len(starts)
    targets = [down_ref.at[pl.ds(start, part)] for start in starts]
    for ref, tall in ((up_ref, rows), (qkv_ref, rows), (out_ref, part)):
        for k in range(ref.shape[1] // width):
            starts.append(starts[-1] + sizes[-1])
            sizes.append(tall)
            block = k
            if ref is up_ref:
                low_bit, high_bit = lax.rem(here, 2), lax.div(here, 2)
                block = lax.rem(low_bit + k, 2) + 2 * lax.rem(high_bit + k // 2, 2)
            targets.append(ref.at[:, span(block * width, width)])
    copies = [
        pltpu.make_async_copy(result_in, result_ref.at[0], sems.at[0]),
        pltpu.make_async_copy(d_in_in, d_in_ref.at[0], sems.at[1]),
    ]
    for copy in copies:
        copy.start()
    for k, (first, size, target) in enumerate(zip(starts, sizes, targets)):
        at = pl.ds(first, size)
        staged[at, :] = sum_in[at, :].astype(jnp.float32)
        copy = pltpu.make_async_copy(staged.at[at], target, sems.at[2 + k])
        copy.start()
        copies.append(copy)
    gain1_ref[...] = gains_in[0]
    gain2_ref[...] = gains_in[1]
    for copy in copies:
        copy.wait()


def shards_by_heads(frames, norm1_gain, w_qkv, w_out, norm2_gain, w_up, w_down, lengths, cotangent):
    _, rows, width = frames.shape
    ff = w_up.shape[1]
    count, planes = lax.axis_size("sq"), lax.axis_size("dp")
    total, part, slab = rows * count, width // count, ff // count
    local = part // HEAD_DIM
    bf16, f32 = jnp.bfloat16, jnp.float32
    blocks = ff // width
    own_rows = slab + rows * blocks + part + rows * 3
    chunks = len(chain_table(own_rows))
    vmem, anywhere = pl.BlockSpec(memory_space=pltpu.VMEM), pl.BlockSpec(memory_space=pl.ANY)
    smem = pl.BlockSpec(memory_space=pltpu.SMEM)

    def low_array(*shape):
        return pltpu.VMEM(shape, bf16)

    def wide_array(*shape):
        return pltpu.VMEM(shape, f32)

    def copies(*shape):
        return pltpu.SemaphoreType.DMA(shape)

    scratch = (
        [low_array(total, width)] * 5
        + [low_array(width, 3 * part), low_array(width, width), low_array(width, ff), low_array(ff, width)]
        + [low_array(width, slab), low_array(slab, width), low_array(rows, ff), low_array(rows, ff)]
        + [low_array(total, 3 * part)]
        + [low_array(local, total, part)] * 4
        + [low_array(local, total, total), wide_array(part, total)]
        + [low_array(total, part), low_array(rows, width)]
        + [wide_array(rows, width)] * 4
        + [low_array(rows, width), low_array(total, part)]
        + [low_array(total, slab)] * 3
        + [low_array(total, 3 * part)] * 2
        + [low_array(rows, 3 * width)]
        + [low_array(own_rows, width)] * 2
        + [wide_array(count, 8, part)] * 2
        + [wide_array(planes, 8, part)]
        + [copies(11), copies(4), copies(4, 10), copies(13), copies(13), copies(2)]
        + [copies(chunks)] * 2
    )
    kept = pl.pallas_call(
        functools.partial(layer_kernel, count, planes),
        out_shape=(
            KEEP((rows, width), bf16),
            KEEP((rows, width), f32),
            KEEP((8, part), f32),
            KEEP((own_rows, width), bf16),
        ),
        in_specs=[anywhere, vmem, anywhere, anywhere, vmem, anywhere, anywhere, smem, anywhere],
        out_specs=(vmem, vmem, vmem, vmem),
        scratch_shapes=scratch,
        compiler_params=pltpu.CompilerParams(
            collective_id=0, has_side_effects=True, vmem_limit_bytes=60 * 2**20),
    )(frames, norm1_gain[None], w_qkv, w_out, norm2_gain[None], w_up, w_down, lengths, cotangent)
    return pl.pallas_call(
        finish_kernel,
        out_shape=tuple(
            jax.ShapeDtypeStruct(shape, kind)
            for shape, kind in (
                ((1, rows, width), bf16), ((1, rows, width), f32), ((part,), f32),
                ((part, 3 * width), f32), ((part, width), f32), ((part,), f32),
                ((part, ff), f32), ((slab, width), f32),
            )
        ),
        in_specs=[vmem] * 4,
        out_specs=(anywhere, anywhere, vmem, anywhere, anywhere, vmem, anywhere, anywhere),
        scratch_shapes=[wide_array(own_rows, width), wide_array(8, part), copies(2 + slab // part + 2 * blocks)],
        compiler_params=pltpu.CompilerParams(vmem_limit_bytes=24 * 2**20),
    )(*kept)


def solution(mesh):
    by_heads = HEADS % mesh.shape["sq"] == 0 and dict(mesh.shape) == {"dp": 4, "sq": 8}
    return jax.shard_map(
        shards_by_heads if by_heads else shards_by_rows,
        mesh=mesh,
        in_specs=(
            P("dp", "sq", None),
            P(),
            P(),
            P(),
            P(),
            P(),
            P(),
            P("dp", None),
            P("dp", "sq", None),
        ),
        out_specs=(
            P("dp", "sq", None),
            P("dp", "sq", None),
            P("sq"),
            P("sq", None),
            P("sq", None),
            P("sq"),
            P("sq", None),
            P("sq", None),
        ),
        check_vma=False,
    )
```

```python
import functools

import jax
import jax.numpy as jnp
from jax import lax
from jax.experimental import pallas as pl
from jax.experimental.pallas import tpu as pltpu
from jax.sharding import PartitionSpec as P

HEADS = 16
HEAD_DIM = 64


EPSILON = 1e-05
NEG_FILL = -1000000000.0
START_MAX = -1e30


def norm_scaled(values, gain):
    return values * lax.rsqrt(jnp.mean(values * values, axis=-1, keepdims=True) + EPSILON) * gain


def segment_ids(positions, item_ends):
    return jnp.sum((positions[None, :, None] >= item_ends[:, None, :]).astype(jnp.int32), axis=2)


def running_ends(lengths):
    items = jnp.arange(lengths.shape[1], dtype=jnp.int32)
    before = items[None, None, :] <= items[None, :, None]
    return jnp.sum(jnp.where(before, lengths[:, None, :], 0), axis=2)


def visible(query_pos, query_seg, key_pos, key_seg):
    return (key_pos[None, None, :] <= query_pos[None, :, None]) & (
        key_seg[:, None, :] == query_seg[:, :, None]
    )


def block_size(count, limit):
    for candidate in range(min(count, limit), 0, -1):
        if count % candidate == 0:
            return candidate
    return count


def over_blocks(carry, arrays, start, step_fn, limit):
    count = arrays[0].shape[1]
    size = block_size(count, limit)
    number = count // size
    if number == 1:
        return step_fn(carry, arrays, start)
    stacked = tuple(
        (
            jnp.swapaxes(member.reshape((member.shape[0], number, size) + member.shape[2:]), 0, 1)
            for member in arrays
        )
    )

    def turn(state, item):
        offset, pieces = item
        return (step_fn(state, pieces, start + offset * size), None)

    offsets = jnp.arange(number, dtype=jnp.int32)
    return lax.scan(turn, carry, (offsets, stacked))[0]


def contract_rows(left, right):
    return lax.dot_general(
        left, right, (((0,), (0,)), ((), ())), preferred_element_type=jnp.float32
    )


def times_transpose(left, right):
    return lax.dot_general(
        left, right, (((1,), (1,)), ((), ())), preferred_element_type=jnp.float32
    )


def heads_flat(values, batch, rows, width):
    return values.transpose(0, 2, 1, 3).reshape(batch * rows, width)


def shards_by_rows(frames, norm1_gain, w_qkv, w_out, norm2_gain, w_up, w_down, lengths, cotangent):
    batch = frames.shape[0]
    rows = frames.shape[1]
    width = frames.shape[2]
    factor = HEAD_DIM ** (-0.5)
    first = lax.axis_index("sq") * rows
    query_pos = first + jnp.arange(rows, dtype=jnp.int32)
    item_ends = running_ends(lengths)
    query_seg = segment_ids(query_pos, item_ends)
    frames_own = frames.reshape(batch * rows, width).astype(jnp.float32)
    hidden1, norm1_pull = jax.vjp(norm_scaled, frames_own, norm1_gain)
    hidden1_low = hidden1.astype(jnp.bfloat16)
    mixed = jnp.dot(hidden1_low, w_qkv, preferred_element_type=jnp.float32).astype(jnp.bfloat16)
    query_rows = mixed[:, :width].reshape(batch, rows, width)
    key_rows = mixed[:, width : 2 * width].reshape(batch, rows, width)
    value_rows = mixed[:, 2 * width :].reshape(batch, rows, width)
    queries = query_rows.reshape(batch, rows, HEADS, HEAD_DIM)
    keys_own = key_rows.reshape(batch, rows, HEADS, HEAD_DIM)
    values_own = value_rows.reshape(batch, rows, HEADS, HEAD_DIM)

    def forward_step(carry, pieces, start):
        key_piece, value_piece = pieces
        count = key_piece.shape[1]
        key_pos = start + jnp.arange(count, dtype=jnp.int32)
        key_seg = segment_ids(key_pos, item_ends)

        def forward_work(state):
            running_max, running_sum, accum = state
            keys_block = key_piece.reshape(batch, count, HEADS, HEAD_DIM)
            values_block = value_piece.reshape(batch, count, HEADS, HEAD_DIM)
            scores = (
                jnp.einsum(
                    "rqhd,rkhd->rhqk", queries, keys_block, preferred_element_type=jnp.float32
                )
                * factor
            )
            mask = visible(query_pos, query_seg, key_pos, key_seg)[:, None]
            scores = jnp.where(mask, scores, NEG_FILL)
            new_max = jnp.maximum(running_max, jnp.max(scores, axis=-1))
            weights = jnp.where(mask, jnp.exp(scores - new_max[..., None]), 0.0)
            decay = jnp.exp(running_max - new_max)
            new_sum = decay * running_sum + jnp.sum(weights, axis=-1)
            update = jnp.einsum(
                "rhqk,rkhd->rhqd",
                weights.astype(jnp.bfloat16),
                values_block,
                preferred_element_type=jnp.float32,
            )
            return (new_max, new_sum, decay[..., None] * accum + update)

        return lax.cond(start <= query_pos[-1], forward_work, lambda state: state, carry)

    start_state = (
        jnp.full((batch, HEADS, rows), START_MAX, jnp.float32),
        jnp.zeros((batch, HEADS, rows), jnp.float32),
        jnp.zeros((batch, HEADS, rows, HEAD_DIM), jnp.float32),
    )
    final_max, final_sum, accum = over_blocks(
        start_state,
        (
            lax.all_gather(key_rows, "sq", axis=1, tiled=True),
            lax.all_gather(value_rows, "sq", axis=1, tiled=True),
        ),
        jnp.int32(0),
        forward_step,
        512,
    )
    attended = heads_flat(accum / final_sum[..., None], batch, rows, width)
    log_total = final_max + jnp.log(final_sum)
    attended_low = attended.astype(jnp.bfloat16)
    middle = frames_own + jnp.dot(attended_low, w_out, preferred_element_type=jnp.float32)
    hidden2, norm2_pull = jax.vjp(norm_scaled, middle, norm2_gain)
    hidden2_low = hidden2.astype(jnp.bfloat16)
    upward = jnp.dot(hidden2_low, w_up, preferred_element_type=jnp.float32)
    active, gelu_pull = jax.vjp(jax.nn.gelu, upward)
    active_low = active.astype(jnp.bfloat16)
    result = middle + jnp.dot(active_low, w_down, preferred_element_type=jnp.float32)
    grad_top = cotangent.reshape(batch * rows, width).astype(jnp.float32)
    grad_branch = grad_top.astype(jnp.bfloat16)
    grad_down = contract_rows(active_low, grad_branch)
    grad_active = times_transpose(grad_branch, w_down)
    grad_upward = gelu_pull(grad_active)[0].astype(jnp.bfloat16)
    grad_up = contract_rows(hidden2_low, grad_upward)
    grad_hidden2 = times_transpose(grad_upward, w_up)
    grad_middle_part, grad_gain2 = norm2_pull(grad_hidden2)
    grad_middle = grad_top + grad_middle_part
    grad_attn = grad_middle.astype(jnp.bfloat16)
    grad_outproj = contract_rows(attended_low, grad_attn)
    grad_attended = times_transpose(grad_attn, w_out).astype(jnp.bfloat16)
    grad_rows_own = grad_attended.reshape(batch, rows, width)
    grad_heads = grad_attended.reshape(batch, rows, HEADS, HEAD_DIM)
    delta_rows = jnp.sum(
        (grad_attended.astype(jnp.float32) * attended).reshape(batch, rows, HEADS, HEAD_DIM), axis=3
    )
    delta = delta_rows.transpose(0, 2, 1)

    def query_step(carry, pieces, start):
        key_piece, value_piece = pieces
        count = key_piece.shape[1]
        key_pos = start + jnp.arange(count, dtype=jnp.int32)
        key_seg = segment_ids(key_pos, item_ends)

        def query_work(grad_query):
            keys_block = key_piece.reshape(batch, count, HEADS, HEAD_DIM)
            values_block = value_piece.reshape(batch, count, HEADS, HEAD_DIM)
            scores = (
                jnp.einsum(
                    "rqhd,rkhd->rhqk", queries, keys_block, preferred_element_type=jnp.float32
                )
                * factor
            )
            mask = visible(query_pos, query_seg, key_pos, key_seg)[:, None]
            shares = jnp.where(mask, jnp.exp(scores - log_total[..., None]), 0.0)
            grad_shares = jnp.einsum(
                "rqhd,rkhd->rhqk", grad_heads, values_block, preferred_element_type=jnp.float32
            )
            grad_scores = (shares * (grad_shares - delta[..., None])).astype(jnp.bfloat16)
            return grad_query + jnp.einsum(
                "rhqk,rkhd->rhqd", grad_scores, keys_block, preferred_element_type=jnp.float32
            )

        return lax.cond(start <= query_pos[-1], query_work, lambda state: state, carry)

    zero_query = jnp.zeros((batch, HEADS, rows, HEAD_DIM), jnp.float32)
    grad_query = over_blocks(
        zero_query,
        (
            lax.all_gather(key_rows, "sq", axis=1, tiled=True),
            lax.all_gather(value_rows, "sq", axis=1, tiled=True),
        ),
        jnp.int32(0),
        query_step,
        512,
    )

    def key_step(carry, pieces, start):
        query_piece, grad_piece, total_piece, delta_piece = pieces
        count = query_piece.shape[1]
        remote_pos = start + jnp.arange(count, dtype=jnp.int32)
        remote_seg = segment_ids(remote_pos, item_ends)

        def key_work(state):
            grad_key, grad_value = state
            remote_queries = query_piece.reshape(batch, count, HEADS, HEAD_DIM)
            remote_grads = grad_piece.reshape(batch, count, HEADS, HEAD_DIM)
            scores = (
                jnp.einsum(
                    "rqhd,rkhd->rhqk", remote_queries, keys_own, preferred_element_type=jnp.float32
                )
                * factor
            )
            mask = visible(remote_pos, remote_seg, query_pos, query_seg)[:, None]
            shares = jnp.where(
                mask, jnp.exp(scores - total_piece.transpose(0, 2, 1)[..., None]), 0.0
            )
            grad_value = grad_value + jnp.einsum(
                "rhqk,rqhd->rhkd",
                shares.astype(jnp.bfloat16),
                remote_grads,
                preferred_element_type=jnp.float32,
            )
            grad_shares = jnp.einsum(
                "rqhd,rkhd->rhqk", remote_grads, values_own, preferred_element_type=jnp.float32
            )
            grad_scores = (
                shares * (grad_shares - delta_piece.transpose(0, 2, 1)[..., None])
            ).astype(jnp.bfloat16)
            grad_key = grad_key + jnp.einsum(
                "rhqk,rqhd->rhkd", grad_scores, remote_queries, preferred_element_type=jnp.float32
            )
            return (grad_key, grad_value)

        return lax.cond(start + count - 1 >= first, key_work, lambda state: state, carry)

    grad_key, grad_value = over_blocks(
        (zero_query, zero_query),
        (
            lax.all_gather(query_rows, "sq", axis=1, tiled=True),
            lax.all_gather(grad_rows_own, "sq", axis=1, tiled=True),
            lax.all_gather(
                log_total.transpose(0, 2, 1).astype(jnp.bfloat16), "sq", axis=1, tiled=True
            ).astype(jnp.float32),
            lax.all_gather(delta_rows.astype(jnp.bfloat16), "sq", axis=1, tiled=True).astype(
                jnp.float32
            ),
        ),
        jnp.int32(0),
        key_step,
        512,
    )
    grad_mixed = jnp.concatenate(
        [
            heads_flat(grad_query * factor, batch, rows, width),
            heads_flat(grad_key * factor, batch, rows, width),
            heads_flat(grad_value, batch, rows, width),
        ],
        axis=1,
    ).astype(jnp.bfloat16)
    grad_qkv = contract_rows(hidden1_low, grad_mixed)
    grad_hidden1 = times_transpose(grad_mixed, w_qkv)
    grad_frames_part, grad_gain1 = norm1_pull(grad_hidden1)
    grad_frames = (grad_middle + grad_frames_part).reshape(batch, rows, width)
    result_rows = result.astype(jnp.bfloat16).reshape(batch, rows, width)
    shares_sq = (
        lax.psum_scatter(grad_gain1, "sq", scatter_dimension=0, tiled=True),
        lax.psum_scatter(grad_qkv, "sq", scatter_dimension=0, tiled=True),
        lax.psum_scatter(grad_outproj, "sq", scatter_dimension=0, tiled=True),
        lax.psum_scatter(grad_gain2, "sq", scatter_dimension=0, tiled=True),
        lax.psum_scatter(grad_up, "sq", scatter_dimension=0, tiled=True),
        lax.psum_scatter(grad_down, "sq", scatter_dimension=0, tiled=True),
    )
    totals = (
        lax.psum(shares_sq[0].astype(jnp.bfloat16), "dp").astype(jnp.float32),
        lax.psum(shares_sq[1].astype(jnp.bfloat16), "dp").astype(jnp.float32),
        lax.psum(shares_sq[2].astype(jnp.bfloat16), "dp").astype(jnp.float32),
        lax.psum(shares_sq[3].astype(jnp.bfloat16), "dp").astype(jnp.float32),
        lax.psum(shares_sq[4].astype(jnp.bfloat16), "dp").astype(jnp.float32),
        lax.psum(shares_sq[5].astype(jnp.bfloat16), "dp").astype(jnp.float32),
    )
    return (
        result_rows,
        grad_frames,
        totals[0],
        totals[1],
        totals[2],
        totals[3],
        totals[4],
        totals[5],
    )


MESH = pl.DeviceIdType.MESH
UNIT = 32
QBLOCK = 256
KEEP = pltpu.VMEM


def dot(left, right):
    return jnp.dot(left, right, preferred_element_type=jnp.float32)


def dot_nt(left, right):
    return lax.dot_general(
        left, right, (((1,), (1,)), ((), ())), preferred_element_type=jnp.float32
    )


def dot_tn(left, right):
    return lax.dot_general(
        left, right, (((0,), (0,)), ((), ())), preferred_element_type=jnp.float32
    )


def low(values):
    return values.astype(jnp.bfloat16)


def wide(values):
    return values.astype(jnp.float32)


def span(start, size):
    return pl.ds(pl.multiple_of(start, size), size)


def chain_table(count):
    sizes = [UNIT] * (count // UNIT)
    starts = [sum(sizes[:k]) for k in range(len(sizes))]
    return list(zip(starts, sizes))


def norm_scale(values):
    return lax.rsqrt(jnp.mean(values * values, axis=-1, keepdims=True) + EPSILON)


def norm_back(values, scale, gain, grad):
    scaled = gain * grad
    inner = jnp.mean(scaled * values, axis=-1, keepdims=True)
    part = scale * scaled - values * (scale * scale * scale) * inner
    return part, jnp.sum(grad * values * scale, axis=0, keepdims=True)


def gelu_parts(values):
    root = 0.7978845608028654
    square = values * values
    inner = jnp.tanh(root * values * (1.0 + 0.044715 * square))
    half = 0.5 * (1.0 + inner)
    slope = half + 0.5 * root * values * (1.0 - inner * inner) * (1.0 + 0.134145 * square)
    return values * half, slope


def layer_kernel(
    count, planes,
    frames_in, gain1_ref, w_qkv_in, w_out_in, gain2_ref, w_up_in, w_down_in, lengths_ref, cot_in,
    result_ref, d_in_ref, gains_ref, sum_ref,
    frames_all, hidden1_all, cot_all, hidden2_all, attn_all,
    w_heads, w_out, w_up, w_down, w_up_s, w_down_s, active_rows, slope_rows,
    mixed, q_pad, k_pad, v_pad, g_pad, shares, o_turned, o_heads, o_rows,
    middle, acc_a, acc_b, grad_mid, g_rows, g_heads,
    active_s, slope_s, up_stage, mixed_grad, mixed_stage, mixed_rows,
    own, cross_in, gain_out, gain_in, gain_z,
    load_sem, ag_send, ag_recv, swap_send, swap_recv, z_send, z_outer_recv, z_cross_recv,
):
    bf16, f32 = jnp.bfloat16, jnp.float32
    rows, width = result_ref.shape
    total = rows * count
    part = width // count
    local = part // HEAD_DIM
    ff = w_up.shape[1]
    slab = ff // count
    half = rows // 2
    factor = HEAD_DIM ** (-0.5)
    me, plane = lax.axis_index("sq"), lax.axis_index("dp")

    def flip(index, bit):
        return index + bit - 2 * bit * lax.rem(lax.div(index, bit), 2)

    mate, over_x, over_y = flip(me, 1), flip(me, 2), flip(me, 4)
    corner = flip(over_x, 4)
    inner = (plane == 1) | (plane == 2)
    outer = (plane == 0) | (plane == 3)
    z_mate = planes - 1 - plane
    z_edge = jnp.where(plane == 1, 0, planes - 1)
    z_core = jnp.where(plane == 0, 1, planes - 2)

    def remote(source, target, send, recv, to, to_plane=None):
        return pltpu.make_async_remote_copy(
            src_ref=source, dst_ref=target, send_sem=send, recv_sem=recv,
            device_id=(plane if to_plane is None else to_plane, to), device_id_type=MESH,
        )

    def others(body):
        @pl.loop(1, count)
        def _(step):
            body(lax.rem(me + step, count))

    barrier = pltpu.get_barrier_semaphore()
    for step in range(1, planes):
        pl.semaphore_signal(
            barrier, inc=1, device_id=(lax.rem(plane + step, planes), me), device_id_type=MESH)
    for step in range(1, count):
        pl.semaphore_signal(
            barrier, inc=1, device_id=(plane, lax.rem(me + step, count)), device_id_type=MESH)

    mine = span(me * rows, rows)
    loads = [
        pltpu.make_async_copy(frames_in.at[0], frames_all.at[mine], load_sem.at[0]),
        pltpu.make_async_copy(cot_in.at[0], cot_all.at[mine], load_sem.at[1]),
    ] + [
        pltpu.make_async_copy(
            w_qkv_in.at[:, span(k * width + me * part, part)],
            w_heads.at[:, pl.ds(k * part, part)],
            load_sem.at[2 + k],
        )
        for k in range(3)
    ] + [
        pltpu.make_async_copy(w_out_in, w_out, load_sem.at[5]),
        pltpu.make_async_copy(w_up_in.at[:, span(me * slab, slab)], w_up_s, load_sem.at[6]),
        pltpu.make_async_copy(w_down_in.at[span(me * slab, slab)], w_down_s, load_sem.at[7]),
    ]

    def load_up(wait=False):
        if wait:
            pltpu.make_async_copy(w_up_in, w_up, load_sem.at[9]).wait()
            return

        @pl.loop(0, ff // part)
        def _(n):
            k, s = lax.div(n, count), lax.rem(n, count)
            pltpu.make_async_copy(
                w_up_in.at[:, span(s * slab + k * part, part)],
                w_up.at[:, span(k * width + s * part, part)], load_sem.at[9]).start()

    def load_down(wait=False):
        if wait:
            pltpu.make_async_copy(w_down_in, w_down, load_sem.at[10]).wait()
            return

        @pl.loop(0, ff // part)
        def _(n):
            k, s = lax.div(n, count), lax.rem(n, count)
            pltpu.make_async_copy(
                w_down_in.at[span(s * slab + k * part, part)],
                w_down.at[span(k * width + s * part, part)], load_sem.at[10]).start()

    load_qkv = pltpu.make_async_copy(w_qkv_in, w_up.at[:, pl.ds(0, 3 * width)], load_sem.at[8])
    for load in loads[:5]:
        load.start()
    loads[0].wait()
    pl.semaphore_wait(barrier, count - 1 + planes - 1)

    def slots(index):
        return [
            (me, None, mate, mate, 0),
            (me, 0, over_x, over_x, 1), (me, 1, over_x, over_x, 2),
            (me, 1, over_y, over_y, 3), (me, 0, over_y, over_y, 4),
            (over_x, 0, over_y, corner, 5), (over_y, 1, over_x, corner, 6),
            (over_x, 0, mate, flip(mate, 2), 7), (over_x, 1, mate, flip(mate, 2), 7),
            (over_y, 1, mate, flip(mate, 4), 8), (over_y, 0, mate, flip(mate, 4), 8),
            (corner, 0, mate, flip(corner, 1), 9), (corner, 1, mate, flip(corner, 1), 9),
        ][index]

    def gather(number, array, source=None):
        def piece(block, which):
            if which is None:
                return span(block * rows, rows)
            return span(block * rows + which * half, half)

        def copy(slot, sent=True, whole=False):
            block, which, target, arrives, sem = slots(slot)
            there = piece(block if sent else arrives, None if whole else which)
            here = array.at[there]
            if sent and source is not None and slot < 5:
                here = source if which is None else source.at[pl.ds(which * half, half)]
            return remote(here, array.at[there], ag_send.at[number], ag_recv.at[number, sem], target)

        def start(*numbers):
            for slot in numbers:
                copy(slot).start()

        def wait(*numbers):
            for slot in numbers:
                copy(slot, sent=False, whole=slot >= 7).wait_recv()

        def finish():
            sent = array.at[pl.ds(0, (count - 1) * rows)]
            remote(sent, sent, ag_send.at[number], ag_recv.at[number, 0], mate).wait_send()

        return start, wait, finish

    def swap(number, pairs, whole):
        def start(target):
            for source, dest in pairs(target, me):
                remote(source, dest, swap_send.at[number], swap_recv.at[number], target).start()

        def wait():
            remote(whole, whole, swap_send.at[number], swap_recv.at[number], mate).wait_recv()

        def finish():
            remote(whole, whole, swap_send.at[number], swap_recv.at[number], mate).wait_send()

        return start, wait, finish

    f_start, f_wait, f_finish = gather(0, frames_all)
    c_start, c_wait, c_finish = gather(1, cot_all, cot_in.at[0])
    h_start, h_wait, h_finish = gather(2, hidden2_all)
    a_start, a_wait, a_finish = gather(3, attn_all)

    table = chain_table(own.shape[0])

    def z_raw(c):
        at = pl.ds(*table[c])
        return remote(own.at[at], sum_ref.at[at], z_send.at[0], z_outer_recv.at[c], me, z_core)

    def z_cross(c):
        at = pl.ds(*table[c])
        return remote(own.at[at], cross_in.at[at], z_send.at[0], z_cross_recv.at[c], me, z_mate)

    def z_back(c):
        at = pl.ds(*table[c])
        return remote(sum_ref.at[at], sum_ref.at[at], z_send.at[1], z_outer_recv.at[c], me, z_edge)

    def z_join(c):
        at = pl.ds(*table[c])
        z_raw(c).wait_recv()
        own[at, :] = low(wide(own[at, :]) + wide(sum_ref[at, :]))
        z_cross(c).start()

    def z_close(c):
        at = pl.ds(*table[c])
        z_cross(c).wait_recv()
        sum_ref[at, :] = low(wide(own[at, :]) + wide(cross_in[at, :]))
        z_back(c).start()

    z_joined, z_closed = [0], [0]

    def z_upto(units):
        todo = []
        while z_joined[0] < len(table) and sum(table[z_joined[0]]) <= units * UNIT:
            todo.append((z_join, z_joined[0]))
            end = sum(table[z_joined[0]])
            z_joined[0] += 1
            while sum(table[z_closed[0]]) + 3 * UNIT <= end:
                todo.append((z_close, z_closed[0]))
                z_closed[0] += 1
        if todo:
            @pl.when(inner)
            def _():
                for step, c in todo:
                    step(c)

    def z_closes(number):
        first = z_closed[0]
        z_closed[0] = min(first + number, len(table))

        @pl.when(inner)
        def _():
            for c in range(first, z_closed[0]):
                z_close(c)

    def z_outer(first, last):
        @pl.when(outer)
        def _():
            for c, (start, size) in enumerate(table):
                if first <= start < last:
                    z_raw(c).start()

    f_start(0, 1, 3, 2, 4)
    loads[5].start()
    load_up()
    load_down()
    loads[6].start()
    loads[7].start()
    pair = 2 * rows
    lane_head = lax.broadcasted_iota(jnp.int32, (pair, part), 1) // HEAD_DIM
    gain1 = gain1_ref[...]
    gain2 = gain2_ref[...]

    def chip(index):
        return span(lax.div(index, 2) * pair, pair)

    def padded(ref, at, values):
        for head in range(local):
            on = lane_head[: values.shape[0]] == head
            ref[head, at, :] = low(jnp.where(on, values, 0.0))

    def qkv_chip(index):
        qkv_rows(chip(index), pair)

    def qkv_rows(at, _):
        values = wide(frames_all[at, :])
        hidden = low(values * norm_scale(values) * gain1)
        hidden1_all[at, :] = hidden
        projected = low(dot(hidden, w_heads[...]))
        mixed[at, :] = projected
        padded(q_pad, at, wide(projected[:, :part]) * factor)
        padded(k_pad, at, wide(projected[:, part : 2 * part]))
        padded(v_pad, at, wide(projected[:, 2 * part :]))

    for k in range(3):
        loads[2 + k].wait()
    f_wait(0)
    qkv_chip(me)
    f_wait(1)
    f_start(5, 7)
    f_wait(3)
    f_start(6, 9)
    c_start(0, 1, 3, 2, 4)
    f_wait(2)
    f_start(8)
    f_wait(4)
    f_start(10)
    f_wait(7)
    qkv_chip(over_x)
    f_wait(9)
    qkv_chip(over_y)
    f_wait(5)
    f_start(11)
    f_wait(6)
    f_start(12)
    qkv_rows(span(corner * rows, rows), rows)
    f_wait(11)
    qkv_rows(span(flip(corner, 1) * rows, rows), rows)

    ends, running = [], None
    for item in range(lengths_ref.shape[1]):
        length = lengths_ref[0, item]
        running = length if running is None else running + length
        ends.append(running)

    keys_at = pl.ds(part, part)
    values_at = pl.ds(2 * part, part)
    query_blocks = total // QBLOCK
    per_block = QBLOCK // rows

    def o_pairs(target, source):
        yield o_heads.at[span(target * rows, rows)], o_rows.at[:, span(source * part, part)]

    o_start, o_wait, o_finish = swap(0, o_pairs, o_heads.at[pl.ds(0, total - rows)])

    for i in range(query_blocks):
        at, keys = pl.ds(i * QBLOCK, QBLOCK), pl.ds(0, (i + 1) * QBLOCK)
        query_pos = i * QBLOCK + lax.broadcasted_iota(jnp.int32, (1, QBLOCK), 1)
        begin = jnp.zeros((1, QBLOCK), jnp.int32)
        for end in ends:
            begin = jnp.maximum(begin, jnp.where(query_pos >= end, end, 0))
        key_pos = lax.broadcasted_iota(jnp.int32, ((i + 1) * QBLOCK, 1), 0)
        mask = (key_pos <= query_pos) & (key_pos >= begin)
        turned = None
        for head in range(local):
            score = jnp.where(mask, dot_nt(mixed[keys, keys_at], q_pad[head, at, :]), NEG_FILL)
            weight = jnp.exp(score - jnp.max(score, axis=0, keepdims=True))
            share = low(weight * (1.0 / jnp.sum(weight, axis=0, keepdims=True)))
            shares[head, keys, at] = share
            value = dot_tn(v_pad[head, keys, :], share)
            turned = value if turned is None else turned + value
        if i == 1:
            c_wait(1)
            c_start(5, 7)
            c_wait(3)
            c_start(6, 9)
        o_turned[:, at] = turned
        o_heads[at, :] = low(turned.T)
        for k in range(per_block):
            target = i * per_block + k

            @pl.when(target != me)
            def _():
                o_start(target)

            @pl.when(target == me)
            def _():
                o_rows[:, span(me * part, part)] = o_heads[mine, :]

    c_wait(2)
    c_start(8)
    c_wait(4)
    c_start(10)
    loads[5].wait()
    o_wait()
    middle_own = wide(frames_all[mine, :]) + dot(o_rows[...], w_out[...])
    middle[...] = middle_own
    hidden2_own = low(middle_own * norm_scale(middle_own) * gain2)
    hidden2_all[mine, :] = hidden2_own

    load_up(wait=True)
    tiles = ff // width
    pieces = []
    for k in range(tiles):
        tile = pl.ds(k * width, width)
        active, slope = gelu_parts(dot(hidden2_own, w_up[:, tile]))
        active_rows[:, tile] = low(active)
        slope_rows[:, tile] = low(slope)
        if k < tiles - 1:
            def a_pairs(target, source, k=k):
                yield (
                    active_rows.at[:, span(k * width + target * part, part)],
                    active_s.at[span(source * rows, rows), pl.ds(k * part, part)],
                )

            pieces.append(swap(7 + k, a_pairs, o_heads.at[pl.ds(0, total - rows)]))
            others(pieces[k][0])
            active_s[mine, pl.ds(k * part, part)] = active_rows[:, span(k * width + me * part, part)]
        if k == tiles - 2:
            h_start(0, 1, 3, 2, 4)
    loads[1].wait()
    load_down(wait=True)
    acc_b[...] = jnp.zeros_like(acc_b)

    def back_tile(k):
        tile = span(k * width, width)
        grad = low(dot_nt(cot_all[mine, :], w_down[tile, :]) * wide(slope_rows[:, tile]))
        acc_b[...] += dot_nt(grad, w_up[:, tile])

    def down_piece(k):
        at = pl.ds(k * part, part)
        own[at, :] = low(dot_tn(active_s[:, at], cot_all[...]))
        z_outer(k * part, (k + 1) * part)

    def out_tile(k):
        tile = pl.ds(k * width, width)
        acc_a[...] += dot(active_rows[:, tile], w_down[tile, :])

    acc_a[...] = middle_own
    back_tile(0)
    c_wait(5)
    c_start(11)
    c_wait(6)
    c_start(12)
    for k in range(tiles - 1):
        out_tile(k)
    c_wait(0, 7, 9, 11)
    pieces[0][1]()
    down_piece(0)
    back_tile(1)
    pieces[1][1]()
    down_piece(1)
    back_tile(2)
    z_upto(1)
    pieces[2][1]()
    down_piece(2)
    z_upto(2)
    back_tile(3)
    load_qkv.start()
    h_wait(1)
    h_start(5, 7)
    h_wait(3)
    h_start(6, 9)
    z_upto(4)

    middle_own = middle[...]
    back2, gain2_part = norm_back(middle_own, norm_scale(middle_own), gain2, acc_b[...])
    gain_out[...] = jnp.zeros_like(gain_out)
    for s in range(count):
        gain_out[s, 1:2, :] = gain2_part[:, s * part : (s + 1) * part]
    grad_mid_own = wide(cot_all[mine, :]) + back2
    grad_mid[...] = grad_mid_own
    attn_own = low(grad_mid_own)
    attn_all[mine, :] = attn_own
    g_rows[...] = low(dot_nt(attn_own, w_out[...]))
    z_upto(5)


    def g_pairs(target, source):
        yield g_rows.at[:, span(target * part, part)], g_heads.at[span(source * rows, rows)]

    g_start, g_wait, g_finish = swap(1, g_pairs, g_heads.at[pl.ds(0, total - rows)])
    others(g_start)
    g_heads[mine, :] = g_rows[:, span(me * part, part)]
    loads[6].wait()
    loads[7].wait()
    for c in range(0, count, 2):
        at = span(c * rows, pair)
        slope_s[at, :] = low(dot_nt(cot_all[at, :], w_down_s[...]))
    z_upto(7)
    last_piece = pl.ds((tiles - 1) * part, part)

    def slab_chip(index):
        slab_rows(chip(index))

    def slab_rows(at):
        active, slope = gelu_parts(dot(hidden2_all[at, :], w_up_s[...]))
        active_s[at, last_piece] = low(active[:, (tiles - 1) * part :])
        slope_s[at, :] = low(wide(slope_s[at, :]) * slope)

    h_wait(0)
    slab_chip(me)
    h_wait(2)
    h_start(8)
    h_wait(4)
    h_start(10)
    h_wait(7)
    slab_chip(over_x)
    h_wait(9)
    slab_chip(over_y)
    z_upto(9)
    h_wait(5)
    h_start(11)
    h_wait(6)
    h_start(12)
    slab_rows(span(corner * rows, rows))
    z_upto(10)
    h_wait(11)
    slab_rows(span(flip(corner, 1) * rows, rows))
    down_piece(tiles - 1)
    z_upto(11)

    up_at = slab
    mixed_at = up_at + rows * tiles
    out_at = mixed_at + rows * 3
    slabs = width // slab

    def distance(one, other):
        one, other = lax.div(one, 2), lax.div(other, 2)
        return lax.rem(one + other, 2) + 2 * lax.rem(lax.div(one, 2) + lax.div(other, 2), 2)

    def u_place(target, source):
        return (span(up_at + distance(target, source) * rows, rows),
                span(lax.rem(source, slabs) * slab, slab))

    u_sems = (10, 11, 11, 12)

    def u_send(target, near_by):
        here = up_stage.at[span(target * rows, rows)]
        remote(here, own.at[u_place(target, me)], swap_send.at[2], swap_recv.at[u_sems[near_by]],
               target).start()

    def u_wait(number, blocks):
        some = up_stage.at[pl.ds(0, blocks * rows)]
        remote(some, some, swap_send.at[2], swap_recv.at[number], mate).wait_recv()

    def u_finish():
        some = up_stage.at[pl.ds(0, total - rows)]
        remote(some, some, swap_send.at[2], swap_recv.at[2], mate).wait_send()

    for near_by, index in ((1, over_x), (2, over_y), (3, corner), (0, me)):
        at = chip(index)
        up_stage[at, :] = low(dot_tn(hidden2_all[:, at], slope_s[...]))
        if near_by:
            u_send(index, near_by)
            u_send(flip(index, 1), near_by)
        else:
            u_send(mate, near_by)
            own[u_place(me, me)] = up_stage[mine, :]
        if near_by in (2, 0):
            z_upto(12 if near_by else 13)
    u_wait(u_sems[0], 1)
    z_outer(up_at, up_at + rows)

    g_wait()
    for c in range(count // 2):
        at = span(c * pair, pair)
        padded(g_pad, at, wide(g_heads[at, :]))

    def late(j):
        return pl.ds(j * QBLOCK, total - j * QBLOCK)

    for j in range(query_blocks):
        keys = pl.ds(j * QBLOCK, QBLOCK)
        grad = None
        for head in range(local):
            value = dot(shares[head, keys, late(j)], g_pad[head, late(j), :])
            grad = value if grad is None else grad + value
        mixed_grad[keys, values_at] = low(grad)
    z_upto(14)
    for i in range(query_blocks):
        at, keys = pl.ds(i * QBLOCK, QBLOCK), pl.ds(0, (i + 1) * QBLOCK)
        product = wide(g_heads[at, :]).T * o_turned[:, at]
        turned = None
        for head in range(local):
            delta = jnp.sum(
                product[head * HEAD_DIM : (head + 1) * HEAD_DIM], axis=0, keepdims=True)
            grad_share = dot_nt(mixed[keys, values_at], g_pad[head, at, :])
            grad_score = low(wide(shares[head, keys, at]) * (grad_share - delta))
            shares[head, keys, at] = grad_score
            value = dot_tn(k_pad[head, keys, :], grad_score)
            turned = value if turned is None else turned + value
        mixed_grad[at, pl.ds(0, part)] = low((turned * factor).T)
        z_upto(14 + i)
    for j in range(query_blocks):
        keys = pl.ds(j * QBLOCK, QBLOCK)
        grad = None
        for head in range(local):
            value = dot(shares[head, keys, late(j)], q_pad[head, late(j), :])
            grad = value if grad is None else grad + value
        mixed_grad[keys, keys_at] = low(grad)
        if j == 1:
            z_upto(18)
    z_upto(19)

    def s_pairs(target, source):
        for k in range(3):
            yield (
                mixed_stage.at[span(target * rows, rows), pl.ds(k * part, part)],
                own.at[span(mixed_at + k * rows, rows), span(source * part, part)],
            )

    def m_pairs(target, source):
        for k in range(3):
            yield (
                mixed_grad.at[span(target * rows, rows), pl.ds(k * part, part)],
                mixed_rows.at[:, span(k * width + source * part, part)],
            )

    s_start, s_wait, s_finish = swap(3, s_pairs, mixed_stage.at[pl.ds(0, total - rows)])
    m_start, m_wait, m_finish = swap(4, m_pairs, mixed_grad.at[pl.ds(0, total - rows)])

    for index in (over_x, over_y, corner, me):
        at = chip(index)
        mixed_stage[at, :] = low(dot_tn(hidden1_all[:, at], mixed_grad[...]))
        if index is not me:
            s_start(index)
            s_start(flip(index, 1))
        else:
            s_start(mate)
    for k in range(3):
        own[span(mixed_at + k * rows, rows), span(me * part, part)] = (
            mixed_stage[mine, pl.ds(k * part, part)])
        mixed_rows[:, span(k * width + me * part, part)] = mixed_grad[mine, pl.ds(k * part, part)]
    a_start(0, 1, 3, 2, 4)
    z_upto(20)
    out_tile(tiles - 1)
    result_ref[...] = low(acc_a[...])
    u_wait(u_sems[1], 4)
    z_outer(up_at + rows, up_at + 3 * rows)
    z_upto(27)
    u_wait(u_sems[3], 2)
    z_outer(up_at + 3 * rows, mixed_at)
    z_upto(31)
    s_wait()
    z_outer(mixed_at, out_at)
    z_upto(34)

    a_wait(1)
    a_start(5, 7)
    a_wait(3)
    a_start(6, 9)
    for first in (1, 4):
        @pl.loop(first, (4, count)[first // 4])
        def _(step):
            m_start(lax.rem(me + step, count))

        z_upto((35, 37)[first // 4])
    a_wait(2)
    a_start(8)
    a_wait(4)
    a_start(10)
    z_upto(39)
    a_wait(5)
    a_start(11)
    a_wait(6)
    a_start(12)
    z_upto(41)
    a_wait(0, 7, 9, 11)
    own[pl.ds(out_at, part), :] = low(dot(low(o_turned[...]), attn_all[...]))
    z_outer(out_at, own.shape[0])
    z_upto(43)

    load_qkv.wait()
    m_wait()
    acc_a[...] = jnp.zeros_like(acc_a)
    for k in range(3):
        @pl.loop(k, k + 1)
        def _(k):
            at = span(k * width, width)
            acc_a[...] += dot_nt(mixed_rows[:, at], w_up[:, at])

        z_upto(44 + k // 2)

    frames_own = wide(frames_all[mine, :])
    back1, gain1_part = norm_back(frames_own, norm_scale(frames_own), gain1, acc_a[...])
    d_in_ref[...] = grad_mid[...] + back1
    z_upto(46)

    for s in range(count):
        gain_out[s, 0:1, :] = gain1_part[:, s * part : (s + 1) * part]

    def n_pairs(target, source):
        yield gain_out.at[target], gain_in.at[source]

    n_start, n_wait, n_finish = swap(5, n_pairs, gain_out.at[pl.ds(0, count - 1)])

    def nz_copy(target, source):
        return remote(
            gain_z.at[source], gain_z.at[source], swap_send.at[6], swap_recv.at[6], me, target)

    others(n_start)
    gain_in[me] = gain_out[me]
    z_upto(own.shape[0] // UNIT)
    z_closes(1)
    n_wait()
    gain_sum = gain_in[0]
    for s in range(1, count):
        gain_sum = gain_sum + gain_in[s]
    gain_z[plane] = gain_sum

    @pl.loop(1, planes)
    def _(step):
        nz_copy(lax.rem(plane + step, planes), plane).start()

    z_closes(len(table))
    gains_all = gain_z.at[pl.ds(0, planes - 1)]
    all_gains = remote(gains_all, gains_all, swap_send.at[6], swap_recv.at[6], mate)
    all_gains.wait_recv()
    gain_sum = gain_z[0]
    for p in range(1, planes):
        gain_sum = gain_sum + gain_z[p]
    gains_ref[...] = gain_sum

    for finish in (
        f_finish, c_finish, h_finish, a_finish,
        o_finish, g_finish, u_finish, s_finish, m_finish, n_finish,
    ):
        finish()
    for piece in pieces:
        piece[2]()
    all_gains.wait_send()

    @pl.when(outer)
    def _():
        remote(own, own, z_send.at[0], z_outer_recv.at[0], me, z_core).wait_send()

        for c in range(len(table)):
            z_back(c).wait_recv()

    @pl.when(inner)
    def _():
        remote(own, own, z_send.at[0], z_outer_recv.at[0], me, z_mate).wait_send()
        remote(own, own, z_send.at[1], z_outer_recv.at[0], me, z_edge).wait_send()


def finish_kernel(
    result_in, d_in_in, gains_in, sum_in,
    result_ref, d_in_ref, gain1_ref, qkv_ref, out_ref, gain2_ref, up_ref, down_ref,
    staged, gains, sems,
):
    rows, width = result_in.shape
    slab, part = down_ref.shape[0], out_ref.shape[0]
    here = lax.div(lax.axis_index("sq"), 2)
    starts = list(range(0, slab, part))
    sizes = [part] * len(starts)
    targets = [down_ref.at[pl.ds(start, part)] for start in starts]
    for ref, tall in ((up_ref, rows), (qkv_ref, rows), (out_ref, part)):
        for k in range(ref.shape[1] // width):
            starts.append(starts[-1] + sizes[-1])
            sizes.append(tall)
            block = k
            if ref is up_ref:
                low_bit, high_bit = lax.rem(here, 2), lax.div(here, 2)
                block = lax.rem(low_bit + k, 2) + 2 * lax.rem(high_bit + k // 2, 2)
            targets.append(ref.at[:, span(block * width, width)])
    copies = [
        pltpu.make_async_copy(result_in, result_ref.at[0], sems.at[0]),
        pltpu.make_async_copy(d_in_in, d_in_ref.at[0], sems.at[1]),
    ]
    for copy in copies:
        copy.start()
    for k, (first, size, target) in enumerate(zip(starts, sizes, targets)):
        at = pl.ds(first, size)
        staged[at, :] = sum_in[at, :].astype(jnp.float32)
        copy = pltpu.make_async_copy(staged.at[at], target, sems.at[2 + k])
        copy.start()
        copies.append(copy)
    gain1_ref[...] = gains_in[0]
    gain2_ref[...] = gains_in[1]
    for copy in copies:
        copy.wait()


def shards_by_heads(frames, norm1_gain, w_qkv, w_out, norm2_gain, w_up, w_down, lengths, cotangent):
    _, rows, width = frames.shape
    ff = w_up.shape[1]
    count, planes = lax.axis_size("sq"), lax.axis_size("dp")
    total, part, slab = rows * count, width // count, ff // count
    local = part // HEAD_DIM
    bf16, f32 = jnp.bfloat16, jnp.float32
    blocks = ff // width
    own_rows = slab + rows * blocks + part + rows * 3
    chunks = len(chain_table(own_rows))
    vmem, anywhere = pl.BlockSpec(memory_space=pltpu.VMEM), pl.BlockSpec(memory_space=pl.ANY)
    smem = pl.BlockSpec(memory_space=pltpu.SMEM)

    def low_array(*shape):
        return pltpu.VMEM(shape, bf16)

    def wide_array(*shape):
        return pltpu.VMEM(shape, f32)

    def copies(*shape):
        return pltpu.SemaphoreType.DMA(shape)

    scratch = (
        [low_array(total, width)] * 5
        + [low_array(width, 3 * part), low_array(width, width), low_array(width, ff), low_array(ff, width)]
        + [low_array(width, slab), low_array(slab, width), low_array(rows, ff), low_array(rows, ff)]
        + [low_array(total, 3 * part)]
        + [low_array(local, total, part)] * 4
        + [low_array(local, total, total), wide_array(part, total)]
        + [low_array(total, part), low_array(rows, width)]
        + [wide_array(rows, width)] * 4
        + [low_array(rows, width), low_array(total, part)]
        + [low_array(total, slab)] * 3
        + [low_array(total, 3 * part)] * 2
        + [low_array(rows, 3 * width)]
        + [low_array(own_rows, width)] * 2
        + [wide_array(count, 8, part)] * 2
        + [wide_array(planes, 8, part)]
        + [copies(11), copies(4), copies(4, 10), copies(13), copies(13), copies(2)]
        + [copies(chunks)] * 2
    )
    kept = pl.pallas_call(
        functools.partial(layer_kernel, count, planes),
        out_shape=(
            KEEP((rows, width), bf16),
            KEEP((rows, width), f32),
            KEEP((8, part), f32),
            KEEP((own_rows, width), bf16),
        ),
        in_specs=[anywhere, vmem, anywhere, anywhere, vmem, anywhere, anywhere, smem, anywhere],
        out_specs=(vmem, vmem, vmem, vmem),
        scratch_shapes=scratch,
        compiler_params=pltpu.CompilerParams(
            collective_id=0, has_side_effects=True, vmem_limit_bytes=60 * 2**20),
    )(frames, norm1_gain[None], w_qkv, w_out, norm2_gain[None], w_up, w_down, lengths, cotangent)
    return pl.pallas_call(
        finish_kernel,
        out_shape=tuple(
            jax.ShapeDtypeStruct(shape, kind)
            for shape, kind in (
                ((1, rows, width), bf16), ((1, rows, width), f32), ((part,), f32),
                ((part, 3 * width), f32), ((part, width), f32), ((part,), f32),
                ((part, ff), f32), ((slab, width), f32),
            )
        ),
        in_specs=[vmem] * 4,
        out_specs=(anywhere, anywhere, vmem, anywhere, anywhere, vmem, anywhere, anywhere),
        scratch_shapes=[wide_array(own_rows, width), wide_array(8, part), copies(2 + slab // part + 2 * blocks)],
        compiler_params=pltpu.CompilerParams(vmem_limit_bytes=24 * 2**20),
    )(*kept)


def solution(mesh):
    by_heads = HEADS % mesh.shape["sq"] == 0 and dict(mesh.shape) == {"dp": 4, "sq": 8}
    return jax.shard_map(
        shards_by_heads if by_heads else shards_by_rows,
        mesh=mesh,
        in_specs=(
            P("dp", "sq", None),
            P(),
            P(),
            P(),
            P(),
            P(),
            P(),
            P("dp", None),
            P("dp", "sq", None),
        ),
        out_specs=(
            P("dp", "sq", None),
            P("dp", "sq", None),
            P("sq"),
            P("sq", None),
            P("sq", None),
            P("sq"),
            P("sq", None),
            P("sq", None),
        ),
        check_vma=False,
    )
```

```python
import functools

import jax
import jax.numpy as jnp
from jax import lax
from jax.experimental import pallas as pl
from jax.experimental.pallas import tpu as pltpu
from jax.sharding import PartitionSpec as P

HEADS = 16
HEAD_DIM = 64


EPSILON = 1e-05
NEG_FILL = -1000000000.0
START_MAX = -1e30


def norm_scaled(values, gain):
    return values * lax.rsqrt(jnp.mean(values * values, axis=-1, keepdims=True) + EPSILON) * gain


def segment_ids(positions, item_ends):
    return jnp.sum((positions[None, :, None] >= item_ends[:, None, :]).astype(jnp.int32), axis=2)


def running_ends(lengths):
    items = jnp.arange(lengths.shape[1], dtype=jnp.int32)
    before = items[None, None, :] <= items[None, :, None]
    return jnp.sum(jnp.where(before, lengths[:, None, :], 0), axis=2)


def visible(query_pos, query_seg, key_pos, key_seg):
    return (key_pos[None, None, :] <= query_pos[None, :, None]) & (
        key_seg[:, None, :] == query_seg[:, :, None]
    )


def block_size(count, limit):
    for candidate in range(min(count, limit), 0, -1):
        if count % candidate == 0:
            return candidate
    return count


def over_blocks(carry, arrays, start, step_fn, limit):
    count = arrays[0].shape[1]
    size = block_size(count, limit)
    number = count // size
    if number == 1:
        return step_fn(carry, arrays, start)
    stacked = tuple(
        (
            jnp.swapaxes(member.reshape((member.shape[0], number, size) + member.shape[2:]), 0, 1)
            for member in arrays
        )
    )

    def turn(state, item):
        offset, pieces = item
        return (step_fn(state, pieces, start + offset * size), None)

    offsets = jnp.arange(number, dtype=jnp.int32)
    return lax.scan(turn, carry, (offsets, stacked))[0]


def contract_rows(left, right):
    return lax.dot_general(
        left, right, (((0,), (0,)), ((), ())), preferred_element_type=jnp.float32
    )


def times_transpose(left, right):
    return lax.dot_general(
        left, right, (((1,), (1,)), ((), ())), preferred_element_type=jnp.float32
    )


def heads_flat(values, batch, rows, width):
    return values.transpose(0, 2, 1, 3).reshape(batch * rows, width)


def shards_by_rows(frames, norm1_gain, w_qkv, w_out, norm2_gain, w_up, w_down, lengths, cotangent):
    batch = frames.shape[0]
    rows = frames.shape[1]
    width = frames.shape[2]
    factor = HEAD_DIM ** (-0.5)
    first = lax.axis_index("sq") * rows
    query_pos = first + jnp.arange(rows, dtype=jnp.int32)
    item_ends = running_ends(lengths)
    query_seg = segment_ids(query_pos, item_ends)
    frames_own = frames.reshape(batch * rows, width).astype(jnp.float32)
    hidden1, norm1_pull = jax.vjp(norm_scaled, frames_own, norm1_gain)
    hidden1_low = hidden1.astype(jnp.bfloat16)
    mixed = jnp.dot(hidden1_low, w_qkv, preferred_element_type=jnp.float32).astype(jnp.bfloat16)
    query_rows = mixed[:, :width].reshape(batch, rows, width)
    key_rows = mixed[:, width : 2 * width].reshape(batch, rows, width)
    value_rows = mixed[:, 2 * width :].reshape(batch, rows, width)
    queries = query_rows.reshape(batch, rows, HEADS, HEAD_DIM)
    keys_own = key_rows.reshape(batch, rows, HEADS, HEAD_DIM)
    values_own = value_rows.reshape(batch, rows, HEADS, HEAD_DIM)

    def forward_step(carry, pieces, start):
        key_piece, value_piece = pieces
        count = key_piece.shape[1]
        key_pos = start + jnp.arange(count, dtype=jnp.int32)
        key_seg = segment_ids(key_pos, item_ends)

        def forward_work(state):
            running_max, running_sum, accum = state
            keys_block = key_piece.reshape(batch, count, HEADS, HEAD_DIM)
            values_block = value_piece.reshape(batch, count, HEADS, HEAD_DIM)
            scores = (
                jnp.einsum(
                    "rqhd,rkhd->rhqk", queries, keys_block, preferred_element_type=jnp.float32
                )
                * factor
            )
            mask = visible(query_pos, query_seg, key_pos, key_seg)[:, None]
            scores = jnp.where(mask, scores, NEG_FILL)
            new_max = jnp.maximum(running_max, jnp.max(scores, axis=-1))
            weights = jnp.where(mask, jnp.exp(scores - new_max[..., None]), 0.0)
            decay = jnp.exp(running_max - new_max)
            new_sum = decay * running_sum + jnp.sum(weights, axis=-1)
            update = jnp.einsum(
                "rhqk,rkhd->rhqd",
                weights.astype(jnp.bfloat16),
                values_block,
                preferred_element_type=jnp.float32,
            )
            return (new_max, new_sum, decay[..., None] * accum + update)

        return lax.cond(start <= query_pos[-1], forward_work, lambda state: state, carry)

    start_state = (
        jnp.full((batch, HEADS, rows), START_MAX, jnp.float32),
        jnp.zeros((batch, HEADS, rows), jnp.float32),
        jnp.zeros((batch, HEADS, rows, HEAD_DIM), jnp.float32),
    )
    final_max, final_sum, accum = over_blocks(
        start_state,
        (
            lax.all_gather(key_rows, "sq", axis=1, tiled=True),
            lax.all_gather(value_rows, "sq", axis=1, tiled=True),
        ),
        jnp.int32(0),
        forward_step,
        512,
    )
    attended = heads_flat(accum / final_sum[..., None], batch, rows, width)
    log_total = final_max + jnp.log(final_sum)
    attended_low = attended.astype(jnp.bfloat16)
    middle = frames_own + jnp.dot(attended_low, w_out, preferred_element_type=jnp.float32)
    hidden2, norm2_pull = jax.vjp(norm_scaled, middle, norm2_gain)
    hidden2_low = hidden2.astype(jnp.bfloat16)
    upward = jnp.dot(hidden2_low, w_up, preferred_element_type=jnp.float32)
    active, gelu_pull = jax.vjp(jax.nn.gelu, upward)
    active_low = active.astype(jnp.bfloat16)
    result = middle + jnp.dot(active_low, w_down, preferred_element_type=jnp.float32)
    grad_top = cotangent.reshape(batch * rows, width).astype(jnp.float32)
    grad_branch = grad_top.astype(jnp.bfloat16)
    grad_down = contract_rows(active_low, grad_branch)
    grad_active = times_transpose(grad_branch, w_down)
    grad_upward = gelu_pull(grad_active)[0].astype(jnp.bfloat16)
    grad_up = contract_rows(hidden2_low, grad_upward)
    grad_hidden2 = times_transpose(grad_upward, w_up)
    grad_middle_part, grad_gain2 = norm2_pull(grad_hidden2)
    grad_middle = grad_top + grad_middle_part
    grad_attn = grad_middle.astype(jnp.bfloat16)
    grad_outproj = contract_rows(attended_low, grad_attn)
    grad_attended = times_transpose(grad_attn, w_out).astype(jnp.bfloat16)
    grad_rows_own = grad_attended.reshape(batch, rows, width)
    grad_heads = grad_attended.reshape(batch, rows, HEADS, HEAD_DIM)
    delta_rows = jnp.sum(
        (grad_attended.astype(jnp.float32) * attended).reshape(batch, rows, HEADS, HEAD_DIM), axis=3
    )
    delta = delta_rows.transpose(0, 2, 1)

    def query_step(carry, pieces, start):
        key_piece, value_piece = pieces
        count = key_piece.shape[1]
        key_pos = start + jnp.arange(count, dtype=jnp.int32)
        key_seg = segment_ids(key_pos, item_ends)

        def query_work(grad_query):
            keys_block = key_piece.reshape(batch, count, HEADS, HEAD_DIM)
            values_block = value_piece.reshape(batch, count, HEADS, HEAD_DIM)
            scores = (
                jnp.einsum(
                    "rqhd,rkhd->rhqk", queries, keys_block, preferred_element_type=jnp.float32
                )
                * factor
            )
            mask = visible(query_pos, query_seg, key_pos, key_seg)[:, None]
            shares = jnp.where(mask, jnp.exp(scores - log_total[..., None]), 0.0)
            grad_shares = jnp.einsum(
                "rqhd,rkhd->rhqk", grad_heads, values_block, preferred_element_type=jnp.float32
            )
            grad_scores = (shares * (grad_shares - delta[..., None])).astype(jnp.bfloat16)
            return grad_query + jnp.einsum(
                "rhqk,rkhd->rhqd", grad_scores, keys_block, preferred_element_type=jnp.float32
            )

        return lax.cond(start <= query_pos[-1], query_work, lambda state: state, carry)

    zero_query = jnp.zeros((batch, HEADS, rows, HEAD_DIM), jnp.float32)
    grad_query = over_blocks(
        zero_query,
        (
            lax.all_gather(key_rows, "sq", axis=1, tiled=True),
            lax.all_gather(value_rows, "sq", axis=1, tiled=True),
        ),
        jnp.int32(0),
        query_step,
        512,
    )

    def key_step(carry, pieces, start):
        query_piece, grad_piece, total_piece, delta_piece = pieces
        count = query_piece.shape[1]
        remote_pos = start + jnp.arange(count, dtype=jnp.int32)
        remote_seg = segment_ids(remote_pos, item_ends)

        def key_work(state):
            grad_key, grad_value = state
            remote_queries = query_piece.reshape(batch, count, HEADS, HEAD_DIM)
            remote_grads = grad_piece.reshape(batch, count, HEADS, HEAD_DIM)
            scores = (
                jnp.einsum(
                    "rqhd,rkhd->rhqk", remote_queries, keys_own, preferred_element_type=jnp.float32
                )
                * factor
            )
            mask = visible(remote_pos, remote_seg, query_pos, query_seg)[:, None]
            shares = jnp.where(
                mask, jnp.exp(scores - total_piece.transpose(0, 2, 1)[..., None]), 0.0
            )
            grad_value = grad_value + jnp.einsum(
                "rhqk,rqhd->rhkd",
                shares.astype(jnp.bfloat16),
                remote_grads,
                preferred_element_type=jnp.float32,
            )
            grad_shares = jnp.einsum(
                "rqhd,rkhd->rhqk", remote_grads, values_own, preferred_element_type=jnp.float32
            )
            grad_scores = (
                shares * (grad_shares - delta_piece.transpose(0, 2, 1)[..., None])
            ).astype(jnp.bfloat16)
            grad_key = grad_key + jnp.einsum(
                "rhqk,rqhd->rhkd", grad_scores, remote_queries, preferred_element_type=jnp.float32
            )
            return (grad_key, grad_value)

        return lax.cond(start + count - 1 >= first, key_work, lambda state: state, carry)

    grad_key, grad_value = over_blocks(
        (zero_query, zero_query),
        (
            lax.all_gather(query_rows, "sq", axis=1, tiled=True),
            lax.all_gather(grad_rows_own, "sq", axis=1, tiled=True),
            lax.all_gather(
                log_total.transpose(0, 2, 1).astype(jnp.bfloat16), "sq", axis=1, tiled=True
            ).astype(jnp.float32),
            lax.all_gather(delta_rows.astype(jnp.bfloat16), "sq", axis=1, tiled=True).astype(
                jnp.float32
            ),
        ),
        jnp.int32(0),
        key_step,
        512,
    )
    grad_mixed = jnp.concatenate(
        [
            heads_flat(grad_query * factor, batch, rows, width),
            heads_flat(grad_key * factor, batch, rows, width),
            heads_flat(grad_value, batch, rows, width),
        ],
        axis=1,
    ).astype(jnp.bfloat16)
    grad_qkv = contract_rows(hidden1_low, grad_mixed)
    grad_hidden1 = times_transpose(grad_mixed, w_qkv)
    grad_frames_part, grad_gain1 = norm1_pull(grad_hidden1)
    grad_frames = (grad_middle + grad_frames_part).reshape(batch, rows, width)
    result_rows = result.astype(jnp.bfloat16).reshape(batch, rows, width)
    shares_sq = (
        lax.psum_scatter(grad_gain1, "sq", scatter_dimension=0, tiled=True),
        lax.psum_scatter(grad_qkv, "sq", scatter_dimension=0, tiled=True),
        lax.psum_scatter(grad_outproj, "sq", scatter_dimension=0, tiled=True),
        lax.psum_scatter(grad_gain2, "sq", scatter_dimension=0, tiled=True),
        lax.psum_scatter(grad_up, "sq", scatter_dimension=0, tiled=True),
        lax.psum_scatter(grad_down, "sq", scatter_dimension=0, tiled=True),
    )
    totals = (
        lax.psum(shares_sq[0].astype(jnp.bfloat16), "dp").astype(jnp.float32),
        lax.psum(shares_sq[1].astype(jnp.bfloat16), "dp").astype(jnp.float32),
        lax.psum(shares_sq[2].astype(jnp.bfloat16), "dp").astype(jnp.float32),
        lax.psum(shares_sq[3].astype(jnp.bfloat16), "dp").astype(jnp.float32),
        lax.psum(shares_sq[4].astype(jnp.bfloat16), "dp").astype(jnp.float32),
        lax.psum(shares_sq[5].astype(jnp.bfloat16), "dp").astype(jnp.float32),
    )
    return (
        result_rows,
        grad_frames,
        totals[0],
        totals[1],
        totals[2],
        totals[3],
        totals[4],
        totals[5],
    )


MESH = pl.DeviceIdType.MESH
UNIT = 32
RING = 12
QBLOCK = 256
KEEP = pltpu.VMEM


def dot(left, right):
    return jnp.dot(left, right, preferred_element_type=jnp.float32)


def dot_nt(left, right):
    return lax.dot_general(
        left, right, (((1,), (1,)), ((), ())), preferred_element_type=jnp.float32
    )


def dot_tn(left, right):
    return lax.dot_general(
        left, right, (((0,), (0,)), ((), ())), preferred_element_type=jnp.float32
    )


def low(values):
    return values.astype(jnp.bfloat16)


def wide(values):
    return values.astype(jnp.float32)


def span(start, size):
    return pl.ds(pl.multiple_of(start, size), size)


def chain_table(count):
    sizes = [UNIT] * (count // UNIT)
    starts = [sum(sizes[:k]) for k in range(len(sizes))]
    return list(zip(starts, sizes))


def norm_scale(values):
    return lax.rsqrt(jnp.mean(values * values, axis=-1, keepdims=True) + EPSILON)


def norm_back(values, scale, gain, grad):
    scaled = gain * grad
    inner = jnp.mean(scaled * values, axis=-1, keepdims=True)
    part = scale * scaled - values * (scale * scale * scale) * inner
    return part, jnp.sum(grad * values * scale, axis=0, keepdims=True)


def gelu_parts(values):
    root = 0.7978845608028654
    square = values * values
    inner = jnp.tanh(root * values * (1.0 + 0.044715 * square))
    half = 0.5 * (1.0 + inner)
    slope = half + 0.5 * root * values * (1.0 - inner * inner) * (1.0 + 0.134145 * square)
    return values * half, slope


def layer_kernel(
    count, planes,
    frames_in, gain1_ref, w_qkv_in, w_out_in, gain2_ref, w_up_in, w_down_in, lengths_ref, cot_in,
    result_ref, d_in_ref, gains_ref, sum_ref,
    frames_all, hidden1_all, cot_all, hidden2_all, attn_all,
    w_heads, w_out, w_up, w_down, w_up_s, w_down_s, active_rows, slope_rows, grad_rows,
    mixed, q_pad, k_pad, v_pad, g_pad, shares, o_turned, o_heads, o_rows,
    middle, acc_a, acc_b, grad_mid, g_rows, g_heads,
    active_s, slope_s, up_stage, mixed_grad, mixed_stage, mixed_rows,
    own, cross_in, gain_out, gain_in, gain_z,
    load_sem, ag_send, ag_recv, swap_send, swap_recv, z_send, z_outer_recv, z_cross_recv,
):
    bf16, f32 = jnp.bfloat16, jnp.float32
    rows, width = result_ref.shape
    total = rows * count
    part = width // count
    local = part // HEAD_DIM
    ff = w_up.shape[1]
    slab = ff // count
    half = rows // 2
    factor = HEAD_DIM ** (-0.5)
    me, plane = lax.axis_index("sq"), lax.axis_index("dp")

    def flip(index, bit):
        return index + bit - 2 * bit * lax.rem(lax.div(index, bit), 2)

    mate, over_x, over_y = flip(me, 1), flip(me, 2), flip(me, 4)
    corner = flip(over_x, 4)
    inner = (plane == 1) | (plane == 2)
    outer = (plane == 0) | (plane == 3)
    z_mate = planes - 1 - plane
    z_edge = jnp.where(plane == 1, 0, planes - 1)
    z_core = jnp.where(plane == 0, 1, planes - 2)

    def remote(source, target, send, recv, to, to_plane=None):
        return pltpu.make_async_remote_copy(
            src_ref=source, dst_ref=target, send_sem=send, recv_sem=recv,
            device_id=(plane if to_plane is None else to_plane, to), device_id_type=MESH,
        )

    def others(body):
        @pl.loop(1, count)
        def _(step):
            body(lax.rem(me + step, count))

    barrier = pltpu.get_barrier_semaphore()
    for step in range(1, planes):
        pl.semaphore_signal(
            barrier, inc=1, device_id=(lax.rem(plane + step, planes), me), device_id_type=MESH)
    for step in range(1, count):
        pl.semaphore_signal(
            barrier, inc=1, device_id=(plane, lax.rem(me + step, count)), device_id_type=MESH)

    mine = span(me * rows, rows)
    loads = [
        pltpu.make_async_copy(frames_in.at[0], frames_all.at[mine], load_sem.at[0]),
        pltpu.make_async_copy(cot_in.at[0], cot_all.at[mine], load_sem.at[1]),
    ] + [
        pltpu.make_async_copy(
            w_qkv_in.at[:, span(k * width + me * part, part)],
            w_heads.at[:, pl.ds(k * part, part)],
            load_sem.at[2 + k],
        )
        for k in range(3)
    ] + [
        pltpu.make_async_copy(w_out_in, w_out, load_sem.at[5]),
        pltpu.make_async_copy(w_up_in.at[:, span(me * slab, slab)], w_up_s, load_sem.at[6]),
        pltpu.make_async_copy(w_down_in.at[span(me * slab, slab)], w_down_s, load_sem.at[7]),
    ]

    def load_up(wait=False):
        if wait:
            pltpu.make_async_copy(w_up_in, w_up, load_sem.at[9]).wait()
            return

        @pl.loop(0, ff // part)
        def _(n):
            k, s = lax.div(n, count), lax.rem(n, count)
            pltpu.make_async_copy(
                w_up_in.at[:, span(s * slab + k * part, part)],
                w_up.at[:, span(k * width + s * part, part)], load_sem.at[9]).start()

    def load_down(wait=False):
        if wait:
            pltpu.make_async_copy(w_down_in, w_down, load_sem.at[10]).wait()
            return

        @pl.loop(0, ff // part)
        def _(n):
            k, s = lax.div(n, count), lax.rem(n, count)
            pltpu.make_async_copy(
                w_down_in.at[span(s * slab + k * part, part)],
                w_down.at[span(k * width + s * part, part)], load_sem.at[10]).start()

    load_qkv = pltpu.make_async_copy(w_qkv_in, w_up.at[:, pl.ds(0, 3 * width)], load_sem.at[8])
    for load in loads[:5]:
        load.start()
    load_down()
    loads[0].wait()
    pl.semaphore_wait(barrier, count - 1 + planes - 1)

    def slots(index):
        return [
            (me, None, mate, mate, 0),
            (me, 0, over_x, over_x, 1), (me, 1, over_x, over_x, 2),
            (me, 1, over_y, over_y, 3), (me, 0, over_y, over_y, 4),
            (over_x, 0, over_y, corner, 5), (over_y, 1, over_x, corner, 6),
            (over_x, 0, mate, flip(mate, 2), 7), (over_x, 1, mate, flip(mate, 2), 7),
            (over_y, 1, mate, flip(mate, 4), 8), (over_y, 0, mate, flip(mate, 4), 8),
            (corner, 0, mate, flip(corner, 1), 9), (corner, 1, mate, flip(corner, 1), 9),
        ][index]

    def gather(number, array, source=None):
        def piece(block, which):
            if which is None:
                return span(block * rows, rows)
            return span(block * rows + which * half, half)

        def copy(slot, sent=True, whole=False):
            block, which, target, arrives, sem = slots(slot)
            there = piece(block if sent else arrives, None if whole else which)
            here = array.at[there]
            if sent and source is not None and slot < 5:
                here = source if which is None else source.at[pl.ds(which * half, half)]
            return remote(here, array.at[there], ag_send.at[number], ag_recv.at[number, sem], target)

        def start(*numbers):
            for slot in numbers:
                copy(slot).start()

        def wait(*numbers):
            for slot in numbers:
                copy(slot, sent=False, whole=slot >= 7).wait_recv()

        def finish():
            sent = array.at[pl.ds(0, (count - 1) * rows)]
            remote(sent, sent, ag_send.at[number], ag_recv.at[number, 0], mate).wait_send()

        return start, wait, finish

    def swap(number, pairs, whole):
        def start(target):
            for source, dest in pairs(target, me):
                remote(source, dest, swap_send.at[number], swap_recv.at[number], target).start()

        def wait():
            remote(whole, whole, swap_send.at[number], swap_recv.at[number], mate).wait_recv()

        def finish():
            remote(whole, whole, swap_send.at[number], swap_recv.at[number], mate).wait_send()

        return start, wait, finish

    f_start, f_wait, f_finish = gather(0, frames_all)
    c_start, c_wait, c_finish = gather(1, cot_all, cot_in.at[0])
    h_start, h_wait, h_finish = gather(2, hidden2_all)
    a_start, a_wait, a_finish = gather(3, attn_all)

    table = chain_table(own.shape[0])

    def z_raw(c):
        at = pl.ds(*table[c])
        return remote(own.at[at], sum_ref.at[at], z_send.at[0], z_outer_recv.at[c], me, z_core)

    def z_cross(c):
        at = pl.ds(*table[c])
        return remote(own.at[at], cross_in.at[at], z_send.at[0], z_cross_recv.at[c % RING], me, z_mate)

    def z_back(c):
        at = pl.ds(*table[c])
        return remote(sum_ref.at[at], sum_ref.at[at], z_send.at[1], z_outer_recv.at[c], me, z_edge)

    def z_join(c):
        at = pl.ds(*table[c])
        z_raw(c).wait_recv()
        own[at, :] = low(wide(own[at, :]) + wide(sum_ref[at, :]))
        z_cross(c).start()

    def z_close(c):
        at = pl.ds(*table[c])
        z_cross(c).wait_recv()
        sum_ref[at, :] = low(wide(own[at, :]) + wide(cross_in[at, :]))
        z_back(c).start()

    z_joined, z_closed = [0], [0]

    def z_upto(units):
        todo = []
        while z_joined[0] < len(table) and sum(table[z_joined[0]]) <= units * UNIT:
            todo.append((z_join, z_joined[0]))
            end = sum(table[z_joined[0]])
            z_joined[0] += 1
            while sum(table[z_closed[0]]) + 3 * UNIT <= end:
                todo.append((z_close, z_closed[0]))
                z_closed[0] += 1
        if todo:
            @pl.when(inner)
            def _():
                for step, c in todo:
                    step(c)

    def z_closes(number):
        first = z_closed[0]
        z_closed[0] = min(first + number, len(table))

        @pl.when(inner)
        def _():
            for c in range(first, z_closed[0]):
                z_close(c)

    def z_outer(first, last):
        @pl.when(outer)
        def _():
            for c, (start, size) in enumerate(table):
                if first <= start < last:
                    z_raw(c).start()

    f_start(0, 1, 3, 2, 4)
    loads[5].start()
    load_up()
    loads[6].start()
    loads[7].start()
    pair = 2 * rows
    lane_head = lax.broadcasted_iota(jnp.int32, (pair, part), 1) // HEAD_DIM
    gain1 = gain1_ref[...]
    gain2 = gain2_ref[...]

    def chip(index):
        return span(lax.div(index, 2) * pair, pair)

    def padded(ref, at, values):
        for head in range(local):
            on = lane_head[: values.shape[0]] == head
            ref[head, at, :] = low(jnp.where(on, values, 0.0))

    def qkv_chip(index):
        qkv_rows(chip(index), pair)

    def qkv_rows(at, _):
        values = wide(frames_all[at, :])
        hidden = low(values * norm_scale(values) * gain1)
        hidden1_all[at, :] = hidden
        projected = low(dot(hidden, w_heads[...]))
        mixed[at, :] = projected
        padded(q_pad, at, wide(projected[:, :part]) * factor)
        padded(k_pad, at, wide(projected[:, part : 2 * part]))
        padded(v_pad, at, wide(projected[:, 2 * part :]))

    for k in range(3):
        loads[2 + k].wait()
    f_wait(0)
    qkv_chip(me)
    loads[1].wait()
    load_down(wait=True)

    def active_grad(k):
        tile = pl.ds(k * width, width)
        grad_rows[:, tile] = low(dot_nt(cot_all[mine, :], w_down[tile, :]))

    tiles = ff // width
    for k in range(tiles // 2):
        active_grad(k)
    f_wait(1)
    f_start(5, 7)
    f_wait(3)
    f_start(6, 9)
    c_start(0, 1, 3, 2, 4)
    for k in range(tiles // 2, tiles):
        active_grad(k)
    f_wait(2)
    f_start(8)
    f_wait(4)
    f_start(10)
    f_wait(7)
    qkv_chip(over_x)
    f_wait(9)
    qkv_chip(over_y)
    f_wait(5)
    f_start(11)
    f_wait(6)
    f_start(12)
    qkv_rows(span(corner * rows, rows), rows)
    f_wait(11)
    qkv_rows(span(flip(corner, 1) * rows, rows), rows)

    ends, running = [], None
    for item in range(lengths_ref.shape[1]):
        length = lengths_ref[0, item]
        running = length if running is None else running + length
        ends.append(running)

    keys_at = pl.ds(part, part)
    values_at = pl.ds(2 * part, part)
    query_blocks = total // QBLOCK
    per_block = QBLOCK // rows

    def o_pairs(target, source):
        yield o_heads.at[span(target * rows, rows)], o_rows.at[:, span(source * part, part)]

    o_start, o_wait, o_finish = swap(0, o_pairs, o_heads.at[pl.ds(0, total - rows)])

    for i in range(query_blocks):
        at, keys = pl.ds(i * QBLOCK, QBLOCK), pl.ds(0, (i + 1) * QBLOCK)
        query_pos = i * QBLOCK + lax.broadcasted_iota(jnp.int32, (1, QBLOCK), 1)
        begin = jnp.zeros((1, QBLOCK), jnp.int32)
        for end in ends:
            begin = jnp.maximum(begin, jnp.where(query_pos >= end, end, 0))
        key_pos = lax.broadcasted_iota(jnp.int32, ((i + 1) * QBLOCK, 1), 0)
        mask = (key_pos <= query_pos) & (key_pos >= begin)
        turned = None
        for head in range(local):
            score = jnp.where(mask, dot_nt(mixed[keys, keys_at], q_pad[head, at, :]), NEG_FILL)
            weight = jnp.exp(score - jnp.max(score, axis=0, keepdims=True))
            share = low(weight * (1.0 / jnp.sum(weight, axis=0, keepdims=True)))
            shares[head, keys, at] = share
            value = dot_tn(v_pad[head, keys, :], share)
            turned = value if turned is None else turned + value
        if i == 1:
            c_wait(1)
            c_start(5, 7)
            c_wait(3)
            c_start(6, 9)
        o_turned[:, at] = turned
        o_heads[at, :] = low(turned.T)
        for k in range(per_block):
            target = i * per_block + k

            @pl.when(target != me)
            def _():
                o_start(target)

            @pl.when(target == me)
            def _():
                o_rows[:, span(me * part, part)] = o_heads[mine, :]

    c_wait(2)
    c_start(8)
    c_wait(4)
    c_start(10)
    loads[5].wait()
    o_wait()
    middle_own = wide(frames_all[mine, :]) + dot(o_rows[...], w_out[...])
    middle[...] = middle_own
    hidden2_own = low(middle_own * norm_scale(middle_own) * gain2)
    hidden2_all[mine, :] = hidden2_own

    load_up(wait=True)
    pieces = []
    for k in range(tiles):
        tile = pl.ds(k * width, width)
        active, slope = gelu_parts(dot(hidden2_own, w_up[:, tile]))
        active_rows[:, tile] = low(active)
        slope_rows[:, tile] = low(slope)
        if k < tiles - 1:
            def a_pairs(target, source, k=k):
                yield (
                    active_rows.at[:, span(k * width + target * part, part)],
                    active_s.at[span(source * rows, rows), pl.ds(k * part, part)],
                )

            pieces.append(swap(7 + k, a_pairs, o_heads.at[pl.ds(0, total - rows)]))
            others(pieces[k][0])
            active_s[mine, pl.ds(k * part, part)] = active_rows[:, span(k * width + me * part, part)]
        if k == tiles - 2:
            h_start(0, 1, 3, 2, 4)
    acc_b[...] = jnp.zeros_like(acc_b)

    def back_tile(k):
        tile = span(k * width, width)
        grad = low(wide(grad_rows[:, tile]) * wide(slope_rows[:, tile]))
        acc_b[...] += dot_nt(grad, w_up[:, tile])

    def down_piece(k):
        at = pl.ds(k * part, part)
        own[at, :] = low(dot_tn(active_s[:, at], cot_all[...]))
        z_outer(k * part, (k + 1) * part)

    def out_tile(k):
        tile = pl.ds(k * width, width)
        acc_a[...] += dot(active_rows[:, tile], w_down[tile, :])

    acc_a[...] = middle_own
    back_tile(0)
    c_wait(5)
    c_start(11)
    c_wait(6)
    c_start(12)
    for k in range(tiles - 1):
        out_tile(k)
    c_wait(0, 7, 9, 11)
    pieces[0][1]()
    down_piece(0)
    back_tile(1)
    pieces[1][1]()
    down_piece(1)
    back_tile(2)
    z_upto(1)
    pieces[2][1]()
    down_piece(2)
    z_upto(2)
    back_tile(3)
    load_qkv.start()
    h_wait(1)
    h_start(5, 7)
    h_wait(3)
    h_start(6, 9)
    z_upto(4)

    middle_own = middle[...]
    back2, gain2_part = norm_back(middle_own, norm_scale(middle_own), gain2, acc_b[...])
    gain_out[...] = jnp.zeros_like(gain_out)
    for s in range(count):
        gain_out[s, 1:2, :] = gain2_part[:, s * part : (s + 1) * part]
    grad_mid_own = wide(cot_all[mine, :]) + back2
    grad_mid[...] = grad_mid_own
    attn_own = low(grad_mid_own)
    attn_all[mine, :] = attn_own
    g_rows[...] = low(dot_nt(attn_own, w_out[...]))
    z_upto(5)


    def g_pairs(target, source):
        yield g_rows.at[:, span(target * part, part)], g_heads.at[span(source * rows, rows)]

    g_start, g_wait, g_finish = swap(1, g_pairs, g_heads.at[pl.ds(0, total - rows)])
    others(g_start)
    g_heads[mine, :] = g_rows[:, span(me * part, part)]
    loads[6].wait()
    loads[7].wait()
    for c in range(0, count, 2):
        at = span(c * rows, pair)
        slope_s[at, :] = low(dot_nt(cot_all[at, :], w_down_s[...]))
    z_upto(6)
    last_piece = pl.ds((tiles - 1) * part, part)

    def slab_chip(index):
        slab_rows(chip(index))

    def slab_rows(at):
        active, slope = gelu_parts(dot(hidden2_all[at, :], w_up_s[...]))
        active_s[at, last_piece] = low(active[:, (tiles - 1) * part :])
        slope_s[at, :] = low(wide(slope_s[at, :]) * slope)

    h_wait(0)
    slab_chip(me)
    h_wait(2)
    h_start(8)
    h_wait(4)
    h_start(10)
    h_wait(7)
    slab_chip(over_x)
    h_wait(9)
    slab_chip(over_y)
    z_upto(7)
    h_wait(5)
    h_start(11)
    h_wait(6)
    h_start(12)
    slab_rows(span(corner * rows, rows))
    z_upto(9)
    h_wait(11)
    slab_rows(span(flip(corner, 1) * rows, rows))
    down_piece(tiles - 1)
    z_upto(10)

    up_at = slab
    mixed_at = up_at + rows * tiles
    out_at = mixed_at + rows * 3
    slabs = width // slab

    def distance(one, other):
        one, other = lax.div(one, 2), lax.div(other, 2)
        return lax.rem(one + other, 2) + 2 * lax.rem(lax.div(one, 2) + lax.div(other, 2), 2)

    def u_place(target, source):
        return (span(up_at + distance(target, source) * rows, rows),
                span(lax.rem(source, slabs) * slab, slab))

    u_sems = (10, 11, 11, 12)

    def u_send(target, near_by):
        here = up_stage.at[span(target * rows, rows)]
        remote(here, own.at[u_place(target, me)], swap_send.at[2], swap_recv.at[u_sems[near_by]],
               target).start()

    def u_wait(number, blocks):
        some = up_stage.at[pl.ds(0, blocks * rows)]
        remote(some, some, swap_send.at[2], swap_recv.at[number], mate).wait_recv()

    def u_finish():
        some = up_stage.at[pl.ds(0, total - rows)]
        remote(some, some, swap_send.at[2], swap_recv.at[2], mate).wait_send()

    for near_by, index in ((1, over_x), (2, over_y), (3, corner), (0, me)):
        at = chip(index)
        up_stage[at, :] = low(dot_tn(hidden2_all[:, at], slope_s[...]))
        if near_by:
            u_send(index, near_by)
            u_send(flip(index, 1), near_by)
        else:
            u_send(mate, near_by)
            own[u_place(me, me)] = up_stage[mine, :]
        if near_by in (2, 0):
            z_upto(11 if near_by else 13)
    u_wait(u_sems[0], 1)
    z_outer(up_at, up_at + rows)

    g_wait()
    for c in range(count // 2):
        at = span(c * pair, pair)
        padded(g_pad, at, wide(g_heads[at, :]))

    def late(j):
        return pl.ds(j * QBLOCK, total - j * QBLOCK)

    for j in range(query_blocks):
        keys = pl.ds(j * QBLOCK, QBLOCK)
        grad = None
        for head in range(local):
            value = dot(shares[head, keys, late(j)], g_pad[head, late(j), :])
            grad = value if grad is None else grad + value
        mixed_grad[keys, values_at] = low(grad)
    z_upto(14)
    for i in range(query_blocks):
        at, keys = pl.ds(i * QBLOCK, QBLOCK), pl.ds(0, (i + 1) * QBLOCK)
        product = wide(g_heads[at, :]).T * o_turned[:, at]
        turned = None
        for head in range(local):
            delta = jnp.sum(
                product[head * HEAD_DIM : (head + 1) * HEAD_DIM], axis=0, keepdims=True)
            grad_share = dot_nt(mixed[keys, values_at], g_pad[head, at, :])
            grad_score = low(wide(shares[head, keys, at]) * (grad_share - delta))
            shares[head, keys, at] = grad_score
            value = dot_tn(k_pad[head, keys, :], grad_score)
            turned = value if turned is None else turned + value
        mixed_grad[at, pl.ds(0, part)] = low((turned * factor).T)
        z_upto(14 + i)
    for j in range(query_blocks):
        keys = pl.ds(j * QBLOCK, QBLOCK)
        grad = None
        for head in range(local):
            value = dot(shares[head, keys, late(j)], q_pad[head, late(j), :])
            grad = value if grad is None else grad + value
        mixed_grad[keys, keys_at] = low(grad)
        if j == 1:
            z_upto(18)
    z_upto(19)

    def s_pairs(target, source):
        for k in range(3):
            yield (
                mixed_stage.at[span(target * rows, rows), pl.ds(k * part, part)],
                own.at[span(mixed_at + k * rows, rows), span(source * part, part)],
            )

    def m_pairs(target, source):
        for k in range(3):
            yield (
                mixed_grad.at[span(target * rows, rows), pl.ds(k * part, part)],
                mixed_rows.at[:, span(k * width + source * part, part)],
            )

    s_start, s_wait, s_finish = swap(3, s_pairs, mixed_stage.at[pl.ds(0, total - rows)])
    m_start, m_wait, m_finish = swap(4, m_pairs, mixed_grad.at[pl.ds(0, total - rows)])

    for index in (over_x, over_y, corner, me):
        at = chip(index)
        mixed_stage[at, :] = low(dot_tn(hidden1_all[:, at], mixed_grad[...]))
        if index is not me:
            s_start(index)
            s_start(flip(index, 1))
        else:
            s_start(mate)
    for k in range(3):
        own[span(mixed_at + k * rows, rows), span(me * part, part)] = (
            mixed_stage[mine, pl.ds(k * part, part)])
        mixed_rows[:, span(k * width + me * part, part)] = mixed_grad[mine, pl.ds(k * part, part)]
    a_start(0, 1, 3, 2, 4)
    z_upto(20)
    out_tile(tiles - 1)
    result_ref[...] = low(acc_a[...])
    u_wait(u_sems[1], 4)
    z_outer(up_at + rows, up_at + 3 * rows)
    z_upto(27)
    u_wait(u_sems[3], 2)
    z_outer(up_at + 3 * rows, mixed_at)
    z_upto(31)
    s_wait()
    z_outer(mixed_at, out_at)
    z_upto(34)

    a_wait(1)
    a_start(5, 7)
    a_wait(3)
    a_start(6, 9)
    for first in (1, 4):
        @pl.loop(first, (4, count)[first // 4])
        def _(step):
            m_start(lax.rem(me + step, count))

        z_upto((35, 37)[first // 4])
    a_wait(2)
    a_start(8)
    a_wait(4)
    a_start(10)
    z_upto(39)
    a_wait(5)
    a_start(11)
    a_wait(6)
    a_start(12)
    z_upto(41)
    a_wait(0, 7, 9, 11)
    own[pl.ds(out_at, part), :] = low(dot(low(o_turned[...]), attn_all[...]))
    z_outer(out_at, own.shape[0])
    z_upto(43)

    load_qkv.wait()
    m_wait()
    acc_a[...] = jnp.zeros_like(acc_a)
    for k in range(3):
        @pl.loop(k, k + 1)
        def _(k):
            at = span(k * width, width)
            acc_a[...] += dot_nt(mixed_rows[:, at], w_up[:, at])

        z_upto(44 + k // 2)

    frames_own = wide(frames_all[mine, :])
    back1, gain1_part = norm_back(frames_own, norm_scale(frames_own), gain1, acc_a[...])
    d_in_ref[...] = grad_mid[...] + back1
    z_upto(46)

    for s in range(count):
        gain_out[s, 0:1, :] = gain1_part[:, s * part : (s + 1) * part]

    def n_pairs(target, source):
        yield gain_out.at[target], gain_in.at[source]

    n_start, n_wait, n_finish = swap(5, n_pairs, gain_out.at[pl.ds(0, count - 1)])

    def nz_copy(target, source):
        return remote(
            gain_z.at[source], gain_z.at[source], swap_send.at[6], swap_recv.at[6], me, target)

    others(n_start)
    gain_in[me] = gain_out[me]
    z_upto(own.shape[0] // UNIT)
    z_closes(1)
    n_wait()
    gain_sum = gain_in[0]
    for s in range(1, count):
        gain_sum = gain_sum + gain_in[s]
    gain_z[plane] = gain_sum

    @pl.loop(1, planes)
    def _(step):
        nz_copy(lax.rem(plane + step, planes), plane).start()

    z_closes(len(table))
    gains_all = gain_z.at[pl.ds(0, planes - 1)]
    all_gains = remote(gains_all, gains_all, swap_send.at[6], swap_recv.at[6], mate)
    all_gains.wait_recv()
    gain_sum = gain_z[0]
    for p in range(1, planes):
        gain_sum = gain_sum + gain_z[p]
    gains_ref[...] = gain_sum

    for finish in (
        f_finish, c_finish, h_finish, a_finish,
        o_finish, g_finish, u_finish, s_finish, m_finish, n_finish,
    ):
        finish()
    for piece in pieces:
        piece[2]()
    all_gains.wait_send()

    @pl.when(outer)
    def _():
        remote(own, own, z_send.at[0], z_outer_recv.at[0], me, z_core).wait_send()

        for c in range(len(table)):
            z_back(c).wait_recv()

    @pl.when(inner)
    def _():
        remote(own, own, z_send.at[0], z_outer_recv.at[0], me, z_mate).wait_send()
        remote(own, own, z_send.at[1], z_outer_recv.at[0], me, z_edge).wait_send()


def finish_kernel(
    result_in, d_in_in, gains_in, sum_in,
    result_ref, d_in_ref, gain1_ref, qkv_ref, out_ref, gain2_ref, up_ref, down_ref,
    staged, gains, sems,
):
    rows, width = result_in.shape
    slab, part = down_ref.shape[0], out_ref.shape[0]
    here = lax.div(lax.axis_index("sq"), 2)
    starts = list(range(0, slab, part))
    sizes = [part] * len(starts)
    targets = [down_ref.at[pl.ds(start, part)] for start in starts]
    for ref, tall in ((up_ref, rows), (qkv_ref, rows), (out_ref, part)):
        for k in range(ref.shape[1] // width):
            starts.append(starts[-1] + sizes[-1])
            sizes.append(tall)
            block = k
            if ref is up_ref:
                low_bit, high_bit = lax.rem(here, 2), lax.div(here, 2)
                block = lax.rem(low_bit + k, 2) + 2 * lax.rem(high_bit + k // 2, 2)
            targets.append(ref.at[:, span(block * width, width)])
    copies = [
        pltpu.make_async_copy(result_in, result_ref.at[0], sems.at[0]),
        pltpu.make_async_copy(d_in_in, d_in_ref.at[0], sems.at[1]),
    ]
    for copy in copies:
        copy.start()
    for k, (first, size, target) in enumerate(zip(starts, sizes, targets)):
        at = pl.ds(first, size)
        staged[at, :] = sum_in[at, :].astype(jnp.float32)
        copy = pltpu.make_async_copy(staged.at[at], target, sems.at[2 + k])
        copy.start()
        copies.append(copy)
    gain1_ref[...] = gains_in[0]
    gain2_ref[...] = gains_in[1]
    for copy in copies:
        copy.wait()


def shards_by_heads(frames, norm1_gain, w_qkv, w_out, norm2_gain, w_up, w_down, lengths, cotangent):
    _, rows, width = frames.shape
    ff = w_up.shape[1]
    count, planes = lax.axis_size("sq"), lax.axis_size("dp")
    total, part, slab = rows * count, width // count, ff // count
    local = part // HEAD_DIM
    bf16, f32 = jnp.bfloat16, jnp.float32
    blocks = ff // width
    own_rows = slab + rows * blocks + part + rows * 3
    chunks = len(chain_table(own_rows))
    vmem, anywhere = pl.BlockSpec(memory_space=pltpu.VMEM), pl.BlockSpec(memory_space=pl.ANY)
    smem = pl.BlockSpec(memory_space=pltpu.SMEM)

    def low_array(*shape):
        return pltpu.VMEM(shape, bf16)

    def wide_array(*shape):
        return pltpu.VMEM(shape, f32)

    def copies(*shape):
        return pltpu.SemaphoreType.DMA(shape)

    scratch = (
        [low_array(total, width)] * 5
        + [low_array(width, 3 * part), low_array(width, width), low_array(width, ff), low_array(ff, width)]
        + [low_array(width, slab), low_array(slab, width)]
        + [low_array(rows, ff)] * 3
        + [low_array(total, 3 * part)]
        + [low_array(local, total, part)] * 4
        + [low_array(local, total, total), wide_array(part, total)]
        + [low_array(total, part), low_array(rows, width)]
        + [wide_array(rows, width)] * 4
        + [low_array(rows, width), low_array(total, part)]
        + [low_array(total, slab)] * 3
        + [low_array(total, 3 * part)] * 2
        + [low_array(rows, 3 * width)]
        + [low_array(own_rows, width)] * 2
        + [wide_array(count, 8, part)] * 2
        + [wide_array(planes, 8, part)]
        + [copies(11), copies(4), copies(4, 10), copies(13), copies(13), copies(2)]
        + [copies(chunks), copies(RING)]
    )
    kept = pl.pallas_call(
        functools.partial(layer_kernel, count, planes),
        out_shape=(
            KEEP((rows, width), bf16),
            KEEP((rows, width), f32),
            KEEP((8, part), f32),
            KEEP((own_rows, width), bf16),
        ),
        in_specs=[anywhere, vmem, anywhere, anywhere, vmem, anywhere, anywhere, smem, anywhere],
        out_specs=(vmem, vmem, vmem, vmem),
        scratch_shapes=scratch,
        compiler_params=pltpu.CompilerParams(
            collective_id=0, has_side_effects=True, vmem_limit_bytes=60 * 2**20),
    )(frames, norm1_gain[None], w_qkv, w_out, norm2_gain[None], w_up, w_down, lengths, cotangent)
    return pl.pallas_call(
        finish_kernel,
        out_shape=tuple(
            jax.ShapeDtypeStruct(shape, kind)
            for shape, kind in (
                ((1, rows, width), bf16), ((1, rows, width), f32), ((part,), f32),
                ((part, 3 * width), f32), ((part, width), f32), ((part,), f32),
                ((part, ff), f32), ((slab, width), f32),
            )
        ),
        in_specs=[vmem] * 4,
        out_specs=(anywhere, anywhere, vmem, anywhere, anywhere, vmem, anywhere, anywhere),
        scratch_shapes=[wide_array(own_rows, width), wide_array(8, part), copies(2 + slab // part + 2 * blocks)],
        compiler_params=pltpu.CompilerParams(vmem_limit_bytes=24 * 2**20),
    )(*kept)


def solution(mesh):
    by_heads = HEADS % mesh.shape["sq"] == 0 and dict(mesh.shape) == {"dp": 4, "sq": 8}
    return jax.shard_map(
        shards_by_heads if by_heads else shards_by_rows,
        mesh=mesh,
        in_specs=(
            P("dp", "sq", None),
            P(),
            P(),
            P(),
            P(),
            P(),
            P(),
            P("dp", None),
            P("dp", "sq", None),
        ),
        out_specs=(
            P("dp", "sq", None),
            P("dp", "sq", None),
            P("sq"),
            P("sq", None),
            P("sq", None),
            P("sq"),
            P("sq", None),
            P("sq", None),
        ),
        check_vma=False,
    )
```

```python
import functools

import jax
import jax.numpy as jnp
from jax import lax
from jax.experimental import pallas as pl
from jax.experimental.pallas import tpu as pltpu
from jax.sharding import PartitionSpec as P

HEADS = 16
HEAD_DIM = 64


EPSILON = 1e-05
NEG_FILL = -1000000000.0
START_MAX = -1e30


def norm_scaled(values, gain):
    return values * lax.rsqrt(jnp.mean(values * values, axis=-1, keepdims=True) + EPSILON) * gain


def segment_ids(positions, item_ends):
    return jnp.sum((positions[None, :, None] >= item_ends[:, None, :]).astype(jnp.int32), axis=2)


def running_ends(lengths):
    items = jnp.arange(lengths.shape[1], dtype=jnp.int32)
    before = items[None, None, :] <= items[None, :, None]
    return jnp.sum(jnp.where(before, lengths[:, None, :], 0), axis=2)


def visible(query_pos, query_seg, key_pos, key_seg):
    return (key_pos[None, None, :] <= query_pos[None, :, None]) & (
        key_seg[:, None, :] == query_seg[:, :, None]
    )


def block_size(count, limit):
    for candidate in range(min(count, limit), 0, -1):
        if count % candidate == 0:
            return candidate
    return count


def over_blocks(carry, arrays, start, step_fn, limit):
    count = arrays[0].shape[1]
    size = block_size(count, limit)
    number = count // size
    if number == 1:
        return step_fn(carry, arrays, start)
    stacked = tuple(
        (
            jnp.swapaxes(member.reshape((member.shape[0], number, size) + member.shape[2:]), 0, 1)
            for member in arrays
        )
    )

    def turn(state, item):
        offset, pieces = item
        return (step_fn(state, pieces, start + offset * size), None)

    offsets = jnp.arange(number, dtype=jnp.int32)
    return lax.scan(turn, carry, (offsets, stacked))[0]


def contract_rows(left, right):
    return lax.dot_general(
        left, right, (((0,), (0,)), ((), ())), preferred_element_type=jnp.float32
    )


def times_transpose(left, right):
    return lax.dot_general(
        left, right, (((1,), (1,)), ((), ())), preferred_element_type=jnp.float32
    )


def heads_flat(values, batch, rows, width):
    return values.transpose(0, 2, 1, 3).reshape(batch * rows, width)


def shards_by_rows(frames, norm1_gain, w_qkv, w_out, norm2_gain, w_up, w_down, lengths, cotangent):
    batch = frames.shape[0]
    rows = frames.shape[1]
    width = frames.shape[2]
    factor = HEAD_DIM ** (-0.5)
    first = lax.axis_index("sq") * rows
    query_pos = first + jnp.arange(rows, dtype=jnp.int32)
    item_ends = running_ends(lengths)
    query_seg = segment_ids(query_pos, item_ends)
    frames_own = frames.reshape(batch * rows, width).astype(jnp.float32)
    hidden1, norm1_pull = jax.vjp(norm_scaled, frames_own, norm1_gain)
    hidden1_low = hidden1.astype(jnp.bfloat16)
    mixed = jnp.dot(hidden1_low, w_qkv, preferred_element_type=jnp.float32).astype(jnp.bfloat16)
    query_rows = mixed[:, :width].reshape(batch, rows, width)
    key_rows = mixed[:, width : 2 * width].reshape(batch, rows, width)
    value_rows = mixed[:, 2 * width :].reshape(batch, rows, width)
    queries = query_rows.reshape(batch, rows, HEADS, HEAD_DIM)
    keys_own = key_rows.reshape(batch, rows, HEADS, HEAD_DIM)
    values_own = value_rows.reshape(batch, rows, HEADS, HEAD_DIM)

    def forward_step(carry, pieces, start):
        key_piece, value_piece = pieces
        count = key_piece.shape[1]
        key_pos = start + jnp.arange(count, dtype=jnp.int32)
        key_seg = segment_ids(key_pos, item_ends)

        def forward_work(state):
            running_max, running_sum, accum = state
            keys_block = key_piece.reshape(batch, count, HEADS, HEAD_DIM)
            values_block = value_piece.reshape(batch, count, HEADS, HEAD_DIM)
            scores = (
                jnp.einsum(
                    "rqhd,rkhd->rhqk", queries, keys_block, preferred_element_type=jnp.float32
                )
                * factor
            )
            mask = visible(query_pos, query_seg, key_pos, key_seg)[:, None]
            scores = jnp.where(mask, scores, NEG_FILL)
            new_max = jnp.maximum(running_max, jnp.max(scores, axis=-1))
            weights = jnp.where(mask, jnp.exp(scores - new_max[..., None]), 0.0)
            decay = jnp.exp(running_max - new_max)
            new_sum = decay * running_sum + jnp.sum(weights, axis=-1)
            update = jnp.einsum(
                "rhqk,rkhd->rhqd",
                weights.astype(jnp.bfloat16),
                values_block,
                preferred_element_type=jnp.float32,
            )
            return (new_max, new_sum, decay[..., None] * accum + update)

        return lax.cond(start <= query_pos[-1], forward_work, lambda state: state, carry)

    start_state = (
        jnp.full((batch, HEADS, rows), START_MAX, jnp.float32),
        jnp.zeros((batch, HEADS, rows), jnp.float32),
        jnp.zeros((batch, HEADS, rows, HEAD_DIM), jnp.float32),
    )
    final_max, final_sum, accum = over_blocks(
        start_state,
        (
            lax.all_gather(key_rows, "sq", axis=1, tiled=True),
            lax.all_gather(value_rows, "sq", axis=1, tiled=True),
        ),
        jnp.int32(0),
        forward_step,
        512,
    )
    attended = heads_flat(accum / final_sum[..., None], batch, rows, width)
    log_total = final_max + jnp.log(final_sum)
    attended_low = attended.astype(jnp.bfloat16)
    middle = frames_own + jnp.dot(attended_low, w_out, preferred_element_type=jnp.float32)
    hidden2, norm2_pull = jax.vjp(norm_scaled, middle, norm2_gain)
    hidden2_low = hidden2.astype(jnp.bfloat16)
    upward = jnp.dot(hidden2_low, w_up, preferred_element_type=jnp.float32)
    active, gelu_pull = jax.vjp(jax.nn.gelu, upward)
    active_low = active.astype(jnp.bfloat16)
    result = middle + jnp.dot(active_low, w_down, preferred_element_type=jnp.float32)
    grad_top = cotangent.reshape(batch * rows, width).astype(jnp.float32)
    grad_branch = grad_top.astype(jnp.bfloat16)
    grad_down = contract_rows(active_low, grad_branch)
    grad_active = times_transpose(grad_branch, w_down)
    grad_upward = gelu_pull(grad_active)[0].astype(jnp.bfloat16)
    grad_up = contract_rows(hidden2_low, grad_upward)
    grad_hidden2 = times_transpose(grad_upward, w_up)
    grad_middle_part, grad_gain2 = norm2_pull(grad_hidden2)
    grad_middle = grad_top + grad_middle_part
    grad_attn = grad_middle.astype(jnp.bfloat16)
    grad_outproj = contract_rows(attended_low, grad_attn)
    grad_attended = times_transpose(grad_attn, w_out).astype(jnp.bfloat16)
    grad_rows_own = grad_attended.reshape(batch, rows, width)
    grad_heads = grad_attended.reshape(batch, rows, HEADS, HEAD_DIM)
    delta_rows = jnp.sum(
        (grad_attended.astype(jnp.float32) * attended).reshape(batch, rows, HEADS, HEAD_DIM), axis=3
    )
    delta = delta_rows.transpose(0, 2, 1)

    def query_step(carry, pieces, start):
        key_piece, value_piece = pieces
        count = key_piece.shape[1]
        key_pos = start + jnp.arange(count, dtype=jnp.int32)
        key_seg = segment_ids(key_pos, item_ends)

        def query_work(grad_query):
            keys_block = key_piece.reshape(batch, count, HEADS, HEAD_DIM)
            values_block = value_piece.reshape(batch, count, HEADS, HEAD_DIM)
            scores = (
                jnp.einsum(
                    "rqhd,rkhd->rhqk", queries, keys_block, preferred_element_type=jnp.float32
                )
                * factor
            )
            mask = visible(query_pos, query_seg, key_pos, key_seg)[:, None]
            shares = jnp.where(mask, jnp.exp(scores - log_total[..., None]), 0.0)
            grad_shares = jnp.einsum(
                "rqhd,rkhd->rhqk", grad_heads, values_block, preferred_element_type=jnp.float32
            )
            grad_scores = (shares * (grad_shares - delta[..., None])).astype(jnp.bfloat16)
            return grad_query + jnp.einsum(
                "rhqk,rkhd->rhqd", grad_scores, keys_block, preferred_element_type=jnp.float32
            )

        return lax.cond(start <= query_pos[-1], query_work, lambda state: state, carry)

    zero_query = jnp.zeros((batch, HEADS, rows, HEAD_DIM), jnp.float32)
    grad_query = over_blocks(
        zero_query,
        (
            lax.all_gather(key_rows, "sq", axis=1, tiled=True),
            lax.all_gather(value_rows, "sq", axis=1, tiled=True),
        ),
        jnp.int32(0),
        query_step,
        512,
    )

    def key_step(carry, pieces, start):
        query_piece, grad_piece, total_piece, delta_piece = pieces
        count = query_piece.shape[1]
        remote_pos = start + jnp.arange(count, dtype=jnp.int32)
        remote_seg = segment_ids(remote_pos, item_ends)

        def key_work(state):
            grad_key, grad_value = state
            remote_queries = query_piece.reshape(batch, count, HEADS, HEAD_DIM)
            remote_grads = grad_piece.reshape(batch, count, HEADS, HEAD_DIM)
            scores = (
                jnp.einsum(
                    "rqhd,rkhd->rhqk", remote_queries, keys_own, preferred_element_type=jnp.float32
                )
                * factor
            )
            mask = visible(remote_pos, remote_seg, query_pos, query_seg)[:, None]
            shares = jnp.where(
                mask, jnp.exp(scores - total_piece.transpose(0, 2, 1)[..., None]), 0.0
            )
            grad_value = grad_value + jnp.einsum(
                "rhqk,rqhd->rhkd",
                shares.astype(jnp.bfloat16),
                remote_grads,
                preferred_element_type=jnp.float32,
            )
            grad_shares = jnp.einsum(
                "rqhd,rkhd->rhqk", remote_grads, values_own, preferred_element_type=jnp.float32
            )
            grad_scores = (
                shares * (grad_shares - delta_piece.transpose(0, 2, 1)[..., None])
            ).astype(jnp.bfloat16)
            grad_key = grad_key + jnp.einsum(
                "rhqk,rqhd->rhkd", grad_scores, remote_queries, preferred_element_type=jnp.float32
            )
            return (grad_key, grad_value)

        return lax.cond(start + count - 1 >= first, key_work, lambda state: state, carry)

    grad_key, grad_value = over_blocks(
        (zero_query, zero_query),
        (
            lax.all_gather(query_rows, "sq", axis=1, tiled=True),
            lax.all_gather(grad_rows_own, "sq", axis=1, tiled=True),
            lax.all_gather(
                log_total.transpose(0, 2, 1).astype(jnp.bfloat16), "sq", axis=1, tiled=True
            ).astype(jnp.float32),
            lax.all_gather(delta_rows.astype(jnp.bfloat16), "sq", axis=1, tiled=True).astype(
                jnp.float32
            ),
        ),
        jnp.int32(0),
        key_step,
        512,
    )
    grad_mixed = jnp.concatenate(
        [
            heads_flat(grad_query * factor, batch, rows, width),
            heads_flat(grad_key * factor, batch, rows, width),
            heads_flat(grad_value, batch, rows, width),
        ],
        axis=1,
    ).astype(jnp.bfloat16)
    grad_qkv = contract_rows(hidden1_low, grad_mixed)
    grad_hidden1 = times_transpose(grad_mixed, w_qkv)
    grad_frames_part, grad_gain1 = norm1_pull(grad_hidden1)
    grad_frames = (grad_middle + grad_frames_part).reshape(batch, rows, width)
    result_rows = result.astype(jnp.bfloat16).reshape(batch, rows, width)
    shares_sq = (
        lax.psum_scatter(grad_gain1, "sq", scatter_dimension=0, tiled=True),
        lax.psum_scatter(grad_qkv, "sq", scatter_dimension=0, tiled=True),
        lax.psum_scatter(grad_outproj, "sq", scatter_dimension=0, tiled=True),
        lax.psum_scatter(grad_gain2, "sq", scatter_dimension=0, tiled=True),
        lax.psum_scatter(grad_up, "sq", scatter_dimension=0, tiled=True),
        lax.psum_scatter(grad_down, "sq", scatter_dimension=0, tiled=True),
    )
    totals = (
        lax.psum(shares_sq[0].astype(jnp.bfloat16), "dp").astype(jnp.float32),
        lax.psum(shares_sq[1].astype(jnp.bfloat16), "dp").astype(jnp.float32),
        lax.psum(shares_sq[2].astype(jnp.bfloat16), "dp").astype(jnp.float32),
        lax.psum(shares_sq[3].astype(jnp.bfloat16), "dp").astype(jnp.float32),
        lax.psum(shares_sq[4].astype(jnp.bfloat16), "dp").astype(jnp.float32),
        lax.psum(shares_sq[5].astype(jnp.bfloat16), "dp").astype(jnp.float32),
    )
    return (
        result_rows,
        grad_frames,
        totals[0],
        totals[1],
        totals[2],
        totals[3],
        totals[4],
        totals[5],
    )


MESH = pl.DeviceIdType.MESH
UNIT = 32
RING = 12
QBLOCK = 256
KEEP = pltpu.VMEM


def dot(left, right):
    return jnp.dot(left, right, preferred_element_type=jnp.float32)


def dot_nt(left, right):
    return lax.dot_general(
        left, right, (((1,), (1,)), ((), ())), preferred_element_type=jnp.float32
    )


def dot_tn(left, right):
    return lax.dot_general(
        left, right, (((0,), (0,)), ((), ())), preferred_element_type=jnp.float32
    )


def low(values):
    return values.astype(jnp.bfloat16)


def wide(values):
    return values.astype(jnp.float32)


def span(start, size):
    return pl.ds(pl.multiple_of(start, size), size)


def chain_table(count):
    sizes = [UNIT] * (count // UNIT)
    starts = [sum(sizes[:k]) for k in range(len(sizes))]
    return list(zip(starts, sizes))


def norm_scale(values):
    return lax.rsqrt(jnp.mean(values * values, axis=-1, keepdims=True) + EPSILON)


def norm_back(values, scale, gain, grad):
    scaled = gain * grad
    inner = jnp.mean(scaled * values, axis=-1, keepdims=True)
    part = scale * scaled - values * (scale * scale * scale) * inner
    return part, jnp.sum(grad * values * scale, axis=0, keepdims=True)


def gelu_parts(values):
    root = 0.7978845608028654
    square = values * values
    inner = jnp.tanh(root * values * (1.0 + 0.044715 * square))
    half = 0.5 * (1.0 + inner)
    slope = half + 0.5 * root * values * (1.0 - inner * inner) * (1.0 + 0.134145 * square)
    return values * half, slope


def layer_kernel(
    count, planes,
    frames_in, gain1_ref, w_qkv_in, w_out_in, gain2_ref, w_up_in, w_down_in, lengths_ref, cot_in,
    result_ref, d_in_ref, gains_ref, sum_ref,
    frames_all, hidden1_all, cot_all, hidden2_all, attn_all,
    w_heads, w_out, w_up, w_down, w_up_s, w_down_s, active_rows, slope_rows, grad_rows,
    mixed, q_pad, k_pad, v_pad, g_pad, shares, o_turned, o_heads, o_rows,
    middle, acc_a, acc_b, grad_mid, g_rows, g_heads,
    active_s, slope_s, up_stage, mixed_grad, mixed_stage, mixed_rows,
    own, cross_in, gain_out, gain_in, gain_z,
    load_sem, ag_send, ag_recv, swap_send, swap_recv, z_send, z_outer_recv, z_cross_recv,
):
    bf16, f32 = jnp.bfloat16, jnp.float32
    rows, width = result_ref.shape
    total = rows * count
    part = width // count
    local = part // HEAD_DIM
    ff = w_up.shape[1]
    slab = ff // count
    half = rows // 2
    factor = HEAD_DIM ** (-0.5)
    me, plane = lax.axis_index("sq"), lax.axis_index("dp")

    def flip(index, bit):
        return index + bit - 2 * bit * lax.rem(lax.div(index, bit), 2)

    mate, over_x, over_y = flip(me, 1), flip(me, 2), flip(me, 4)
    corner = flip(over_x, 4)
    inner = (plane == 1) | (plane == 2)
    outer = (plane == 0) | (plane == 3)
    z_mate = planes - 1 - plane
    z_edge = jnp.where(plane == 1, 0, planes - 1)
    z_core = jnp.where(plane == 0, 1, planes - 2)

    def remote(source, target, send, recv, to, to_plane=None):
        return pltpu.make_async_remote_copy(
            src_ref=source, dst_ref=target, send_sem=send, recv_sem=recv,
            device_id=(plane if to_plane is None else to_plane, to), device_id_type=MESH,
        )

    def others(body):
        @pl.loop(1, count)
        def _(step):
            body(lax.rem(me + step, count))

    barrier = pltpu.get_barrier_semaphore()
    for step in range(1, planes):
        pl.semaphore_signal(
            barrier, inc=1, device_id=(lax.rem(plane + step, planes), me), device_id_type=MESH)
    for step in range(1, count):
        pl.semaphore_signal(
            barrier, inc=1, device_id=(plane, lax.rem(me + step, count)), device_id_type=MESH)

    mine = span(me * rows, rows)
    loads = [
        pltpu.make_async_copy(frames_in.at[0], frames_all.at[mine], load_sem.at[0]),
        pltpu.make_async_copy(cot_in.at[0], cot_all.at[mine], load_sem.at[1]),
    ] + [
        pltpu.make_async_copy(
            w_qkv_in.at[:, span(k * width + me * part, part)],
            w_heads.at[:, pl.ds(k * part, part)],
            load_sem.at[2 + k],
        )
        for k in range(3)
    ] + [
        pltpu.make_async_copy(w_out_in, w_out, load_sem.at[5]),
        pltpu.make_async_copy(w_up_in.at[:, span(me * slab, slab)], w_up_s, load_sem.at[6]),
        pltpu.make_async_copy(w_down_in.at[span(me * slab, slab)], w_down_s, load_sem.at[7]),
    ]

    def load_up(wait=False):
        if wait:
            pltpu.make_async_copy(w_up_in, w_up, load_sem.at[9]).wait()
            return

        @pl.loop(0, ff // part)
        def _(n):
            k, s = lax.div(n, count), lax.rem(n, count)
            pltpu.make_async_copy(
                w_up_in.at[:, span(s * slab + k * part, part)],
                w_up.at[:, span(k * width + s * part, part)], load_sem.at[9]).start()

    def load_down(wait=False):
        if wait:
            pltpu.make_async_copy(w_down_in, w_down, load_sem.at[10]).wait()
            return

        @pl.loop(0, ff // part)
        def _(n):
            k, s = lax.div(n, count), lax.rem(n, count)
            pltpu.make_async_copy(
                w_down_in.at[span(s * slab + k * part, part)],
                w_down.at[span(k * width + s * part, part)], load_sem.at[10]).start()

    load_qkv = pltpu.make_async_copy(w_qkv_in, w_up.at[:, pl.ds(0, 3 * width)], load_sem.at[8])
    for load in loads[:5]:
        load.start()
    load_down()
    loads[0].wait()
    pl.semaphore_wait(barrier, count - 1 + planes - 1)

    def slots(index):
        return [
            (me, None, mate, mate, 0),
            (me, 0, over_x, over_x, 1), (me, 1, over_x, over_x, 2),
            (me, 1, over_y, over_y, 3), (me, 0, over_y, over_y, 4),
            (over_x, 0, over_y, corner, 5), (over_y, 1, over_x, corner, 6),
            (over_x, 0, mate, flip(mate, 2), 7), (over_x, 1, mate, flip(mate, 2), 7),
            (over_y, 1, mate, flip(mate, 4), 8), (over_y, 0, mate, flip(mate, 4), 8),
            (corner, 0, mate, flip(corner, 1), 9), (corner, 1, mate, flip(corner, 1), 9),
        ][index]

    def gather(number, array, source=None):
        def piece(block, which):
            if which is None:
                return span(block * rows, rows)
            return span(block * rows + which * half, half)

        def copy(slot, sent=True, whole=False):
            block, which, target, arrives, sem = slots(slot)
            there = piece(block if sent else arrives, None if whole else which)
            here = array.at[there]
            if sent and source is not None and slot < 5:
                here = source if which is None else source.at[pl.ds(which * half, half)]
            return remote(here, array.at[there], ag_send.at[number], ag_recv.at[number, sem], target)

        def start(*numbers):
            for slot in numbers:
                copy(slot).start()

        def wait(*numbers):
            for slot in numbers:
                copy(slot, sent=False, whole=slot >= 7).wait_recv()

        def finish():
            sent = array.at[pl.ds(0, (count - 1) * rows)]
            remote(sent, sent, ag_send.at[number], ag_recv.at[number, 0], mate).wait_send()

        return start, wait, finish

    def swap(number, pairs, whole):
        def start(target):
            for source, dest in pairs(target, me):
                remote(source, dest, swap_send.at[number], swap_recv.at[number], target).start()

        def wait():
            remote(whole, whole, swap_send.at[number], swap_recv.at[number], mate).wait_recv()

        def finish():
            remote(whole, whole, swap_send.at[number], swap_recv.at[number], mate).wait_send()

        return start, wait, finish

    f_start, f_wait, f_finish = gather(0, frames_all)
    c_start, c_wait, c_finish = gather(1, cot_all, cot_in.at[0])
    h_start, h_wait, h_finish = gather(2, hidden2_all)
    a_start, a_wait, a_finish = gather(3, attn_all)

    table = chain_table(own.shape[0])

    def z_raw(c):
        at = pl.ds(*table[c])
        return remote(own.at[at], sum_ref.at[at], z_send.at[0], z_outer_recv.at[c % (2 * RING)], me, z_core)

    def z_cross(c):
        at = pl.ds(*table[c])
        return remote(own.at[at], cross_in.at[at], z_send.at[0], z_cross_recv.at[c % RING], me, z_mate)

    def z_back(c):
        at = pl.ds(*table[c])
        return remote(sum_ref.at[at], sum_ref.at[at], z_send.at[1], z_outer_recv.at[c % (2 * RING)], me, z_edge)

    def z_join(c):
        at = pl.ds(*table[c])
        z_raw(c).wait_recv()
        own[at, :] = low(wide(own[at, :]) + wide(sum_ref[at, :]))
        z_cross(c).start()

    def z_close(c):
        at = pl.ds(*table[c])
        z_cross(c).wait_recv()
        sum_ref[at, :] = low(wide(own[at, :]) + wide(cross_in[at, :]))
        z_back(c).start()

    z_joined, z_closed = [0], [0]

    def z_upto(units):
        todo = []
        while z_joined[0] < len(table) and sum(table[z_joined[0]]) <= units * UNIT:
            todo.append((z_join, z_joined[0]))
            end = sum(table[z_joined[0]])
            z_joined[0] += 1
            while sum(table[z_closed[0]]) + 3 * UNIT <= end:
                todo.append((z_close, z_closed[0]))
                z_closed[0] += 1
        if todo:
            @pl.when(inner)
            def _():
                for step, c in todo:
                    step(c)

    def z_closes(number):
        first = z_closed[0]
        z_closed[0] = min(first + number, len(table))

        @pl.when(inner)
        def _():
            for c in range(first, z_closed[0]):
                z_close(c)

    def z_outer(first, last):
        @pl.when(outer)
        def _():
            for c, (start, size) in enumerate(table):
                if first <= start < last:
                    if c >= 2 * RING:
                        z_back(c - 2 * RING).wait_recv()
                    z_raw(c).start()

    f_start(0, 1, 3, 2, 4)
    loads[5].start()
    load_up()
    loads[6].start()
    loads[7].start()
    pair = 2 * rows
    lane_head = lax.broadcasted_iota(jnp.int32, (pair, part), 1) // HEAD_DIM
    gain1 = gain1_ref[...]
    gain2 = gain2_ref[...]

    def chip(index):
        return span(lax.div(index, 2) * pair, pair)

    def padded(ref, at, values):
        for head in range(local):
            on = lane_head[: values.shape[0]] == head
            ref[head, at, :] = low(jnp.where(on, values, 0.0))

    def qkv_chip(index):
        qkv_rows(chip(index), pair)

    def qkv_rows(at, _):
        values = wide(frames_all[at, :])
        hidden = low(values * norm_scale(values) * gain1)
        hidden1_all[at, :] = hidden
        projected = low(dot(hidden, w_heads[...]))
        mixed[at, :] = projected
        padded(q_pad, at, wide(projected[:, :part]) * factor)
        padded(k_pad, at, wide(projected[:, part : 2 * part]))
        padded(v_pad, at, wide(projected[:, 2 * part :]))

    for k in range(3):
        loads[2 + k].wait()
    f_wait(0)
    qkv_chip(me)
    loads[1].wait()
    load_down(wait=True)

    def active_grad(k):
        tile = pl.ds(k * width, width)
        grad_rows[:, tile] = low(dot_nt(cot_all[mine, :], w_down[tile, :]))

    tiles = ff // width
    for k in range(tiles // 2):
        active_grad(k)
    f_wait(1)
    f_start(5, 7)
    f_wait(3)
    f_start(6, 9)
    c_start(0, 1, 3, 2, 4)
    for k in range(tiles // 2, tiles):
        active_grad(k)
    f_wait(2)
    f_start(8)
    f_wait(4)
    f_start(10)
    f_wait(7)
    qkv_chip(over_x)
    f_wait(9)
    qkv_chip(over_y)
    f_wait(5)
    f_start(11)
    f_wait(6)
    f_start(12)
    qkv_rows(span(corner * rows, rows), rows)
    f_wait(11)
    qkv_rows(span(flip(corner, 1) * rows, rows), rows)

    ends, running = [], None
    for item in range(lengths_ref.shape[1]):
        length = lengths_ref[0, item]
        running = length if running is None else running + length
        ends.append(running)

    keys_at = pl.ds(part, part)
    values_at = pl.ds(2 * part, part)
    query_blocks = total // QBLOCK
    per_block = QBLOCK // rows

    def o_pairs(target, source):
        yield o_heads.at[span(target * rows, rows)], o_rows.at[:, span(source * part, part)]

    o_start, o_wait, o_finish = swap(0, o_pairs, o_heads.at[pl.ds(0, total - rows)])

    for i in range(query_blocks):
        at, keys = pl.ds(i * QBLOCK, QBLOCK), pl.ds(0, (i + 1) * QBLOCK)
        query_pos = i * QBLOCK + lax.broadcasted_iota(jnp.int32, (1, QBLOCK), 1)
        begin = jnp.zeros((1, QBLOCK), jnp.int32)
        for end in ends:
            begin = jnp.maximum(begin, jnp.where(query_pos >= end, end, 0))
        key_pos = lax.broadcasted_iota(jnp.int32, ((i + 1) * QBLOCK, 1), 0)
        mask = (key_pos <= query_pos) & (key_pos >= begin)
        turned = None
        for head in range(local):
            score = jnp.where(mask, dot_nt(mixed[keys, keys_at], q_pad[head, at, :]), NEG_FILL)
            weight = jnp.exp(score - jnp.max(score, axis=0, keepdims=True))
            share = low(weight * (1.0 / jnp.sum(weight, axis=0, keepdims=True)))
            shares[head, keys, at] = share
            value = dot_tn(v_pad[head, keys, :], share)
            turned = value if turned is None else turned + value
        if i == 1:
            c_wait(1)
            c_start(5, 7)
            c_wait(3)
            c_start(6, 9)
        o_turned[:, at] = turned
        o_heads[at, :] = low(turned.T)
        for k in range(per_block):
            target = i * per_block + k

            @pl.when(target != me)
            def _():
                o_start(target)

            @pl.when(target == me)
            def _():
                o_rows[:, span(me * part, part)] = o_heads[mine, :]

    c_wait(2)
    c_start(8)
    c_wait(4)
    c_start(10)
    loads[5].wait()
    o_wait()
    middle_own = wide(frames_all[mine, :]) + dot(o_rows[...], w_out[...])
    middle[...] = middle_own
    hidden2_own = low(middle_own * norm_scale(middle_own) * gain2)
    hidden2_all[mine, :] = hidden2_own

    load_up(wait=True)
    pieces = []
    for k in range(tiles):
        tile = pl.ds(k * width, width)
        active, slope = gelu_parts(dot(hidden2_own, w_up[:, tile]))
        active_rows[:, tile] = low(active)
        slope_rows[:, tile] = low(slope)
        if k < tiles - 1:
            def a_pairs(target, source, k=k):
                yield (
                    active_rows.at[:, span(k * width + target * part, part)],
                    active_s.at[span(source * rows, rows), pl.ds(k * part, part)],
                )

            pieces.append(swap(7 + k, a_pairs, o_heads.at[pl.ds(0, total - rows)]))
            others(pieces[k][0])
            active_s[mine, pl.ds(k * part, part)] = active_rows[:, span(k * width + me * part, part)]
        if k == tiles - 2:
            h_start(0, 1, 3, 2, 4)
    acc_b[...] = jnp.zeros_like(acc_b)

    def back_tile(k):
        tile = span(k * width, width)
        grad = low(wide(grad_rows[:, tile]) * wide(slope_rows[:, tile]))
        acc_b[...] += dot_nt(grad, w_up[:, tile])

    def down_piece(k):
        at = pl.ds(k * part, part)
        own[at, :] = low(dot_tn(active_s[:, at], cot_all[...]))
        z_outer(k * part, (k + 1) * part)

    def out_tile(k):
        tile = pl.ds(k * width, width)
        acc_a[...] += dot(active_rows[:, tile], w_down[tile, :])

    acc_a[...] = middle_own
    back_tile(0)
    c_wait(5)
    c_start(11)
    c_wait(6)
    c_start(12)
    for k in range(tiles - 1):
        out_tile(k)
    c_wait(0, 7, 9, 11)
    pieces[0][1]()
    down_piece(0)
    back_tile(1)
    pieces[1][1]()
    down_piece(1)
    back_tile(2)
    z_upto(1)
    pieces[2][1]()
    down_piece(2)
    z_upto(2)
    back_tile(3)
    load_qkv.start()
    h_wait(1)
    h_start(5, 7)
    h_wait(3)
    h_start(6, 9)
    z_upto(4)

    middle_own = middle[...]
    back2, gain2_part = norm_back(middle_own, norm_scale(middle_own), gain2, acc_b[...])
    gain_out[...] = jnp.zeros_like(gain_out)
    for s in range(count):
        gain_out[s, 1:2, :] = gain2_part[:, s * part : (s + 1) * part]
    grad_mid_own = wide(cot_all[mine, :]) + back2
    grad_mid[...] = grad_mid_own
    attn_own = low(grad_mid_own)
    attn_all[mine, :] = attn_own
    g_rows[...] = low(dot_nt(attn_own, w_out[...]))
    z_upto(5)


    def g_pairs(target, source):
        yield g_rows.at[:, span(target * part, part)], g_heads.at[span(source * rows, rows)]

    g_start, g_wait, g_finish = swap(1, g_pairs, g_heads.at[pl.ds(0, total - rows)])
    others(g_start)
    g_heads[mine, :] = g_rows[:, span(me * part, part)]
    loads[6].wait()
    loads[7].wait()
    for c in range(0, count, 2):
        at = span(c * rows, pair)
        slope_s[at, :] = low(dot_nt(cot_all[at, :], w_down_s[...]))
    z_upto(6)
    last_piece = pl.ds((tiles - 1) * part, part)

    def slab_chip(index):
        slab_rows(chip(index))

    def slab_rows(at):
        active, slope = gelu_parts(dot(hidden2_all[at, :], w_up_s[...]))
        active_s[at, last_piece] = low(active[:, (tiles - 1) * part :])
        slope_s[at, :] = low(wide(slope_s[at, :]) * slope)

    h_wait(0)
    slab_chip(me)
    h_wait(2)
    h_start(8)
    h_wait(4)
    h_start(10)
    h_wait(7)
    slab_chip(over_x)
    h_wait(9)
    slab_chip(over_y)
    z_upto(7)
    h_wait(5)
    h_start(11)
    h_wait(6)
    h_start(12)
    slab_rows(span(corner * rows, rows))
    z_upto(9)
    h_wait(11)
    slab_rows(span(flip(corner, 1) * rows, rows))
    down_piece(tiles - 1)
    z_upto(10)

    up_at = slab
    mixed_at = up_at + rows * tiles
    out_at = mixed_at + rows * 3
    slabs = width // slab

    def distance(one, other):
        one, other = lax.div(one, 2), lax.div(other, 2)
        return lax.rem(one + other, 2) + 2 * lax.rem(lax.div(one, 2) + lax.div(other, 2), 2)

    def u_place(target, source):
        return (span(up_at + distance(target, source) * rows, rows),
                span(lax.rem(source, slabs) * slab, slab))

    u_sems = (10, 11, 11, 12)

    def u_send(target, near_by):
        here = up_stage.at[span(target * rows, rows)]
        remote(here, own.at[u_place(target, me)], swap_send.at[2], swap_recv.at[u_sems[near_by]],
               target).start()

    def u_wait(number, blocks):
        some = up_stage.at[pl.ds(0, blocks * rows)]
        remote(some, some, swap_send.at[2], swap_recv.at[number], mate).wait_recv()

    def u_finish():
        some = up_stage.at[pl.ds(0, total - rows)]
        remote(some, some, swap_send.at[2], swap_recv.at[2], mate).wait_send()

    for near_by, index in ((1, over_x), (2, over_y), (3, corner), (0, me)):
        at = chip(index)
        up_stage[at, :] = low(dot_tn(hidden2_all[:, at], slope_s[...]))
        if near_by:
            u_send(index, near_by)
            u_send(flip(index, 1), near_by)
        else:
            u_send(mate, near_by)
            own[u_place(me, me)] = up_stage[mine, :]
        if near_by in (2, 0):
            z_upto(11 if near_by else 13)
    u_wait(u_sems[0], 1)
    z_outer(up_at, up_at + rows)

    g_wait()
    for c in range(count // 2):
        at = span(c * pair, pair)
        padded(g_pad, at, wide(g_heads[at, :]))

    def late(j):
        return pl.ds(j * QBLOCK, total - j * QBLOCK)

    for j in range(query_blocks):
        keys = pl.ds(j * QBLOCK, QBLOCK)
        grad = None
        for head in range(local):
            value = dot(shares[head, keys, late(j)], g_pad[head, late(j), :])
            grad = value if grad is None else grad + value
        mixed_grad[keys, values_at] = low(grad)
    z_upto(14)
    for i in range(query_blocks):
        at, keys = pl.ds(i * QBLOCK, QBLOCK), pl.ds(0, (i + 1) * QBLOCK)
        product = wide(g_heads[at, :]).T * o_turned[:, at]
        turned = None
        for head in range(local):
            delta = jnp.sum(
                product[head * HEAD_DIM : (head + 1) * HEAD_DIM], axis=0, keepdims=True)
            grad_share = dot_nt(mixed[keys, values_at], g_pad[head, at, :])
            grad_score = low(wide(shares[head, keys, at]) * (grad_share - delta))
            shares[head, keys, at] = grad_score
            value = dot_tn(k_pad[head, keys, :], grad_score)
            turned = value if turned is None else turned + value
        mixed_grad[at, pl.ds(0, part)] = low((turned * factor).T)
        z_upto(14 + i)
    for j in range(query_blocks):
        keys = pl.ds(j * QBLOCK, QBLOCK)
        grad = None
        for head in range(local):
            value = dot(shares[head, keys, late(j)], q_pad[head, late(j), :])
            grad = value if grad is None else grad + value
        mixed_grad[keys, keys_at] = low(grad)
        if j == 1:
            z_upto(18)
    z_upto(19)

    def s_pairs(target, source):
        for k in range(3):
            yield (
                mixed_stage.at[span(target * rows, rows), pl.ds(k * part, part)],
                own.at[span(mixed_at + k * rows, rows), span(source * part, part)],
            )

    def m_pairs(target, source):
        for k in range(3):
            yield (
                mixed_grad.at[span(target * rows, rows), pl.ds(k * part, part)],
                mixed_rows.at[:, span(k * width + source * part, part)],
            )

    s_start, s_wait, s_finish = swap(3, s_pairs, mixed_stage.at[pl.ds(0, total - rows)])
    m_start, m_wait, m_finish = swap(4, m_pairs, mixed_grad.at[pl.ds(0, total - rows)])

    for index in (over_x, over_y, corner, me):
        at = chip(index)
        mixed_stage[at, :] = low(dot_tn(hidden1_all[:, at], mixed_grad[...]))
        if index is not me:
            s_start(index)
            s_start(flip(index, 1))
        else:
            s_start(mate)
    for k in range(3):
        own[span(mixed_at + k * rows, rows), span(me * part, part)] = (
            mixed_stage[mine, pl.ds(k * part, part)])
        mixed_rows[:, span(k * width + me * part, part)] = mixed_grad[mine, pl.ds(k * part, part)]
    a_start(0, 1, 3, 2, 4)
    z_upto(20)
    out_tile(tiles - 1)
    result_ref[...] = low(acc_a[...])
    u_wait(u_sems[1], 4)
    z_outer(up_at + rows, up_at + 3 * rows)
    z_upto(27)
    u_wait(u_sems[3], 2)
    z_outer(up_at + 3 * rows, mixed_at)
    z_upto(31)
    s_wait()
    z_outer(mixed_at, out_at)
    z_upto(34)

    a_wait(1)
    a_start(5, 7)
    a_wait(3)
    a_start(6, 9)
    for first in (1, 4):
        @pl.loop(first, (4, count)[first // 4])
        def _(step):
            m_start(lax.rem(me + step, count))

        z_upto((35, 37)[first // 4])
    a_wait(2)
    a_start(8)
    a_wait(4)
    a_start(10)
    z_upto(39)
    a_wait(5)
    a_start(11)
    a_wait(6)
    a_start(12)
    z_upto(41)
    a_wait(0, 7, 9, 11)
    own[pl.ds(out_at, part), :] = low(dot(low(o_turned[...]), attn_all[...]))
    z_outer(out_at, own.shape[0])
    z_upto(43)

    load_qkv.wait()
    m_wait()
    acc_a[...] = jnp.zeros_like(acc_a)
    for k in range(3):
        @pl.loop(k, k + 1)
        def _(k):
            at = span(k * width, width)
            acc_a[...] += dot_nt(mixed_rows[:, at], w_up[:, at])

        z_upto(44 + k // 2)

    frames_own = wide(frames_all[mine, :])
    back1, gain1_part = norm_back(frames_own, norm_scale(frames_own), gain1, acc_a[...])
    d_in_ref[...] = grad_mid[...] + back1
    z_upto(46)

    for s in range(count):
        gain_out[s, 0:1, :] = gain1_part[:, s * part : (s + 1) * part]

    def n_pairs(target, source):
        yield gain_out.at[target], gain_in.at[source]

    n_start, n_wait, n_finish = swap(5, n_pairs, gain_out.at[pl.ds(0, count - 1)])

    def nz_copy(target, source):
        return remote(
            gain_z.at[source], gain_z.at[source], swap_send.at[6], swap_recv.at[6], me, target)

    others(n_start)
    gain_in[me] = gain_out[me]
    z_upto(own.shape[0] // UNIT)
    z_closes(1)
    n_wait()
    gain_sum = gain_in[0]
    for s in range(1, count):
        gain_sum = gain_sum + gain_in[s]
    gain_z[plane] = gain_sum

    @pl.loop(1, planes)
    def _(step):
        nz_copy(lax.rem(plane + step, planes), plane).start()

    z_closes(len(table))
    gains_all = gain_z.at[pl.ds(0, planes - 1)]
    all_gains = remote(gains_all, gains_all, swap_send.at[6], swap_recv.at[6], mate)
    all_gains.wait_recv()
    gain_sum = gain_z[0]
    for p in range(1, planes):
        gain_sum = gain_sum + gain_z[p]
    gains_ref[...] = gain_sum

    for finish in (
        f_finish, c_finish, h_finish, a_finish,
        o_finish, g_finish, u_finish, s_finish, m_finish, n_finish,
    ):
        finish()
    for piece in pieces:
        piece[2]()
    all_gains.wait_send()

    @pl.when(outer)
    def _():
        remote(own, own, z_send.at[0], z_outer_recv.at[0], me, z_core).wait_send()

        for c in range(len(table) - 2 * RING, len(table)):
            z_back(c).wait_recv()

    @pl.when(inner)
    def _():
        remote(own, own, z_send.at[0], z_outer_recv.at[0], me, z_mate).wait_send()
        remote(own, own, z_send.at[1], z_outer_recv.at[0], me, z_edge).wait_send()


def finish_kernel(
    result_in, d_in_in, gains_in, sum_in,
    result_ref, d_in_ref, gain1_ref, qkv_ref, out_ref, gain2_ref, up_ref, down_ref,
    staged, gains, sems,
):
    rows, width = result_in.shape
    slab, part = down_ref.shape[0], out_ref.shape[0]
    here = lax.div(lax.axis_index("sq"), 2)
    starts = list(range(0, slab, part))
    sizes = [part] * len(starts)
    targets = [down_ref.at[pl.ds(start, part)] for start in starts]
    for ref, tall in ((up_ref, rows), (qkv_ref, rows), (out_ref, part)):
        for k in range(ref.shape[1] // width):
            starts.append(starts[-1] + sizes[-1])
            sizes.append(tall)
            block = k
            if ref is up_ref:
                low_bit, high_bit = lax.rem(here, 2), lax.div(here, 2)
                block = lax.rem(low_bit + k, 2) + 2 * lax.rem(high_bit + k // 2, 2)
            targets.append(ref.at[:, span(block * width, width)])
    copies = [
        pltpu.make_async_copy(result_in, result_ref.at[0], sems.at[0]),
        pltpu.make_async_copy(d_in_in, d_in_ref.at[0], sems.at[1]),
    ]
    for copy in copies:
        copy.start()
    for k, (first, size, target) in enumerate(zip(starts, sizes, targets)):
        at = pl.ds(first, size)
        staged[at, :] = sum_in[at, :].astype(jnp.float32)
        copy = pltpu.make_async_copy(staged.at[at], target, sems.at[2 + k])
        copy.start()
        copies.append(copy)
    gain1_ref[...] = gains_in[0]
    gain2_ref[...] = gains_in[1]
    for copy in copies:
        copy.wait()


def shards_by_heads(frames, norm1_gain, w_qkv, w_out, norm2_gain, w_up, w_down, lengths, cotangent):
    _, rows, width = frames.shape
    ff = w_up.shape[1]
    count, planes = lax.axis_size("sq"), lax.axis_size("dp")
    total, part, slab = rows * count, width // count, ff // count
    local = part // HEAD_DIM
    bf16, f32 = jnp.bfloat16, jnp.float32
    blocks = ff // width
    own_rows = slab + rows * blocks + part + rows * 3
    vmem, anywhere = pl.BlockSpec(memory_space=pltpu.VMEM), pl.BlockSpec(memory_space=pl.ANY)
    smem = pl.BlockSpec(memory_space=pltpu.SMEM)

    def low_array(*shape):
        return pltpu.VMEM(shape, bf16)

    def wide_array(*shape):
        return pltpu.VMEM(shape, f32)

    def copies(*shape):
        return pltpu.SemaphoreType.DMA(shape)

    scratch = (
        [low_array(total, width)] * 5
        + [low_array(width, 3 * part), low_array(width, width), low_array(width, ff), low_array(ff, width)]
        + [low_array(width, slab), low_array(slab, width)]
        + [low_array(rows, ff)] * 3
        + [low_array(total, 3 * part)]
        + [low_array(local, total, part)] * 4
        + [low_array(local, total, total), wide_array(part, total)]
        + [low_array(total, part), low_array(rows, width)]
        + [wide_array(rows, width)] * 4
        + [low_array(rows, width), low_array(total, part)]
        + [low_array(total, slab)] * 3
        + [low_array(total, 3 * part)] * 2
        + [low_array(rows, 3 * width)]
        + [low_array(own_rows, width)] * 2
        + [wide_array(count, 8, part)] * 2
        + [wide_array(planes, 8, part)]
        + [copies(11), copies(4), copies(4, 10), copies(13), copies(13), copies(2)]
        + [copies(2 * RING), copies(RING)]
    )
    kept = pl.pallas_call(
        functools.partial(layer_kernel, count, planes),
        out_shape=(
            KEEP((rows, width), bf16),
            KEEP((rows, width), f32),
            KEEP((8, part), f32),
            KEEP((own_rows, width), bf16),
        ),
        in_specs=[anywhere, vmem, anywhere, anywhere, vmem, anywhere, anywhere, smem, anywhere],
        out_specs=(vmem, vmem, vmem, vmem),
        scratch_shapes=scratch,
        compiler_params=pltpu.CompilerParams(
            collective_id=0, has_side_effects=True, vmem_limit_bytes=60 * 2**20),
    )(frames, norm1_gain[None], w_qkv, w_out, norm2_gain[None], w_up, w_down, lengths, cotangent)
    return pl.pallas_call(
        finish_kernel,
        out_shape=tuple(
            jax.ShapeDtypeStruct(shape, kind)
            for shape, kind in (
                ((1, rows, width), bf16), ((1, rows, width), f32), ((part,), f32),
                ((part, 3 * width), f32), ((part, width), f32), ((part,), f32),
                ((part, ff), f32), ((slab, width), f32),
            )
        ),
        in_specs=[vmem] * 4,
        out_specs=(anywhere, anywhere, vmem, anywhere, anywhere, vmem, anywhere, anywhere),
        scratch_shapes=[wide_array(own_rows, width), wide_array(8, part), copies(2 + slab // part + 2 * blocks)],
        compiler_params=pltpu.CompilerParams(vmem_limit_bytes=24 * 2**20),
    )(*kept)


def solution(mesh):
    by_heads = HEADS % mesh.shape["sq"] == 0 and dict(mesh.shape) == {"dp": 4, "sq": 8}
    return jax.shard_map(
        shards_by_heads if by_heads else shards_by_rows,
        mesh=mesh,
        in_specs=(
            P("dp", "sq", None),
            P(),
            P(),
            P(),
            P(),
            P(),
            P(),
            P("dp", None),
            P("dp", "sq", None),
        ),
        out_specs=(
            P("dp", "sq", None),
            P("dp", "sq", None),
            P("sq"),
            P("sq", None),
            P("sq", None),
            P("sq"),
            P("sq", None),
            P("sq", None),
        ),
        check_vma=False,
    )
```
